32 devices in a mesh: rep: 4 (over z), member: 8 (over y, x, core).
Axes of the slice: x: 2, y: 2, z: 4, core: 2. Of those that a mesh axis runs over, the one named last changes fastest.
Arguments:
- acts: bfloat16 [512, 2, 100, 128], P(('rep', 'member')), may hold values from -6 to 6
- cotangent: bfloat16 [512, 2, 100, 128], P(('rep', 'member')), may hold values from -6 to 6
- routes: int32 [512, 2], P(('rep', 'member')), may hold values from 0 to 7, all different within a row; in each aligned block of 16 rows (0 to 15, 16 to 31, ...) at most 8 rows name the same one
- w_first: bfloat16 [8, 1152, 128], P('member'), may hold values from -0.1875 to 0.1875
- w_second: bfloat16 [8, 1152, 128], P('member'), may hold values from -0.1875 to 0.1875
- b_first: float32 [8, 128], P('member'), may hold values from -3 to 3
- b_second: float32 [8, 128], P('member'), may hold values from -3 to 3
Outputs:
- out_acts: bfloat16 [512, 2, 100, 128], P(('rep', 'member'))
- grad_acts: bfloat16 [512, 2, 100, 128], P(('rep', 'member'))
- grad_w_first: float32 [8, 1152, 128], P('member')
- grad_w_second: float32 [8, 1152, 128], P('member')
- grad_b_first: float32 [8, 128], P('member')
- grad_b_second: float32 [8, 128], P('member')
The draws below stay inside these ranges and needn't reach their ends.
Inputs may be any that keep to these rules, and one draw needn't show every extreme that they name: `routes`: the two members of a state differ. Among the 16 states of one device no member is named more than 8 times, and in some device one member is named exactly 8 times. Every member is named by some state.
All inputs are finite; a program needn't handle non-finite values.
Results may differ from the reference program's by a relative error of at most 0.007.
Values may be sent and summed in bfloat16 or wider, within the bound.
A program may use at most 64 MiB of HBM per device.

```python
import math
import jax
import jax.numpy as jnp
import numpy as np
from jax import lax

CH = 128
BOARD = 10
S_DEV = 16
CELLS = 100
MEMBERS = 8
CAP = 8
STATES = 512


def block_levels(stream_key, dims, pieces, least, high):
    def one(axis_at, shards_of):
        heights = jax.random.uniform(jax.random.fold_in(jax.random.fold_in(stream_key, 6), axis_at), (shards_of,), jnp.float32, least / len(pieces), high / len(pieces))
        return jnp.repeat(jnp.exp(heights), dims[axis_at] // shards_of).reshape((-1,) + (1,) * (len(dims) - axis_at - 1))

    level = one(*pieces[0])
    for cut in pieces[1:]:
        level = level * one(*cut)
    return level


def assign_block(stream_key, own, number, rows, amount, top, bound, skew):
    ranking = jax.random.permutation(stream_key, amount)
    crowded, usual = shares(amount, rows * top, bound, skew, True), shares(amount, rows * top, bound, skew, False)
    places = jnp.arange(amount)

    def named(tallies, rotation):
        used = int((tallies > 0).sum())
        fixed = max(1, used // 4)
        moved = fixed + (places - fixed + rotation * (used - fixed)) % max(1, amount - fixed)
        return jnp.zeros((amount,), jnp.int32).at[ranking[jnp.where(places < fixed, places, moved)]].set(jnp.asarray(tallies, jnp.int32))

    tallies = jnp.where(number % 4 == 0, named(crowded, number // 4), named(usual, number - number // 4 - 1))
    mixed = jax.random.permutation(jax.random.fold_in(own, 3), amount)
    giver, sink = mixed[0:amount // 2 * 2:2], mixed[1:amount // 2 * 2:2]
    margin = jnp.minimum(tallies[giver] - 1, bound - tallies[sink]) // 2
    margin = jnp.where((giver == ranking[0]) | (sink == ranking[0]) | (tallies[sink] == 0), 0, jnp.maximum(margin, 0))
    moved = jax.random.randint(jax.random.fold_in(own, 4), (amount // 2,), 0, 1 << 20) % (margin + 1)
    tallies = tallies.at[giver].add(-moved).at[sink].add(moved)
    members = jnp.searchsorted(jnp.cumsum(tallies), jnp.arange(rows * top), side="right").astype(jnp.int32)
    grid = members.reshape(top, rows).T
    grid = grid[jax.random.permutation(jax.random.fold_in(own, 1), rows)]
    rotation = jax.random.randint(jax.random.fold_in(own, 2), (rows, 1), 0, top)
    return jnp.take_along_axis(grid, (jnp.arange(top)[None, :] + rotation) % top, axis=1)


def shares(number_of, total, limit, lean, full):
    portions = [(1 << 20) // math.isqrt(rank ** lean) + 1 for rank in range(1, number_of + 1)]
    largest = limit if full else min(limit, max(-(-total // number_of), total * portions[0] // sum(portions)))
    least = 1 if total - largest >= number_of - 1 else 0
    counts, spare = [largest] + [least] * (number_of - 1), total - largest - least * (number_of - 1)
    while spare > 0:
        candidates = [i for i in range(1, number_of) if counts[i] < largest] or [i for i in range(1, number_of) if counts[i] < limit]
        whole, budget = sum([portions[i] for i in candidates]), spare
        for i in candidates:
            addition = min(limit - counts[i], max(1, budget * portions[i] // whole), spare)
            counts[i] = counts[i] + addition
            spare = spare - addition
    return np.array(counts)


def centred(rng, extent, spread, limit, cuts=(), kind=jnp.bfloat16):
    factor_of = block_levels(rng, extent, cuts, -0.22, 0.18) if cuts else 1.0
    values = jax.random.normal(rng, extent, jnp.float32) * spread * factor_of
    return jnp.minimum(jnp.maximum(values, -limit), limit).astype(kind)


def setup_inputs(seed: int = 0) -> dict:
    seeds = jax.random.split(jax.random.key(seed), 8)
    acts = centred(seeds[0], (STATES, 2, CELLS, CH), 1.0, 6.0, ((0, 32),))
    cotangent = centred(seeds[1], (STATES, 2, CELLS, CH), 1.0, 6.0, ((0, 32),))
    routes_keys = jax.random.split(jax.random.fold_in(seeds[2], 1), STATES // S_DEV)
    routes_turns = jax.random.permutation(jax.random.fold_in(seeds[2], 3), STATES // S_DEV)
    routes = jax.vmap(lambda own, number: assign_block(jax.random.fold_in(seeds[2], 2), own, number, S_DEV, MEMBERS, 2, CAP, 2))(routes_keys, routes_turns).reshape((STATES, 2))
    w_first = centred(seeds[3], (MEMBERS, 9 * CH, CH), (9 * CH) ** -0.5, 0.1875, ((0, 8),))
    w_second = centred(seeds[4], (MEMBERS, 9 * CH, CH), (9 * CH) ** -0.5, 0.1875, ((0, 8),))
    b_first = centred(seeds[5], (MEMBERS, CH), 0.5, 3.0, ((0, 8),), jnp.float32)
    b_second = centred(seeds[6], (MEMBERS, CH), 0.5, 3.0, ((0, 8),), jnp.float32)
    return dict(acts=acts, cotangent=cotangent, routes=routes, w_first=w_first, w_second=w_second, b_first=b_first, b_second=b_second)


def patches(values):
    leading = values.shape[:-2]
    channels = values.shape[-1]
    board_view = values.reshape(leading + (BOARD, BOARD, channels))
    padded = jnp.pad(board_view, [(0, 0)] * len(leading) + [(1, 1), (1, 1), (0, 0)])
    shifted = [padded[..., row_off:row_off + BOARD, col_off:col_off + BOARD, :] for row_off in range(3) for col_off in range(3)]
    return jnp.concatenate(shifted, axis=-1).reshape(leading + (BOARD * BOARD, 9 * channels))


def flipped(weight):
    channels = weight.shape[-1]
    stacked = weight.reshape(weight.shape[:-2] + (9, channels, channels))
    reversed_taps = jnp.flip(stacked, axis=-3)
    return jnp.swapaxes(reversed_taps, -1, -2).reshape(weight.shape)


def silu_slope(pre_act):
    sigmoid_vals = jax.nn.sigmoid(pre_act)
    return sigmoid_vals * (1.0 + pre_act * (1.0 - sigmoid_vals))


def reference(acts, cotangent, routes, w_first, w_second, b_first, b_second):
    inputs = acts.reshape(-1, CELLS, CH)
    upstream = cotangent.reshape(-1, CELLS, CH)
    member_ids = routes.reshape(-1).astype(jnp.int32)
    block_rows = 16
    num_blocks = inputs.shape[0] // block_rows
    highest = lax.Precision.HIGHEST

    def one_block(running, block_num):
        start = (block_num * block_rows).astype(jnp.int32)
        states_blk = lax.dynamic_slice_in_dim(inputs, start, block_rows, 0)
        upstream_blk = lax.dynamic_slice_in_dim(upstream, start, block_rows, 0)
        ids_blk = lax.dynamic_slice_in_dim(member_ids, start, block_rows, 0)
        weight_one = w_first[ids_blk].astype(jnp.float32)
        weight_two = w_second[ids_blk].astype(jnp.float32)
        in_patch = patches(states_blk).astype(jnp.float32)
        pre_act = jnp.einsum("rpk,rkc->rpc", in_patch, weight_one, precision=highest) + b_first[ids_blk][:, None, :]
        hidden = jax.nn.silu(pre_act).astype(jnp.bfloat16)
        hid_patch = patches(hidden).astype(jnp.float32)
        result = (states_blk.astype(jnp.float32) + jnp.einsum("rpk,rkc->rpc", hid_patch, weight_two, precision=highest) + b_second[ids_blk][:, None, :]).astype(jnp.bfloat16)
        grad_up = upstream_blk.astype(jnp.float32)
        grad_two = jnp.einsum("rpk,rpc->rkc", hid_patch, grad_up, precision=highest)
        bias_two = jnp.sum(grad_up, axis=1)
        up_patch = patches(upstream_blk).astype(jnp.float32)
        hidden_grad = jnp.einsum("rpk,rkc->rpc", up_patch, flipped(weight_two), precision=highest)
        pre_grad = (hidden_grad * silu_slope(pre_act)).astype(jnp.bfloat16)
        pre_grad_f = pre_grad.astype(jnp.float32)
        grad_one = jnp.einsum("rpk,rpc->rkc", in_patch, pre_grad_f, precision=highest)
        bias_one = jnp.sum(pre_grad_f, axis=1)
        delta_patch = patches(pre_grad).astype(jnp.float32)
        input_grad = (grad_up + jnp.einsum("rpk,rkc->rpc", delta_patch, flipped(weight_one), precision=highest)).astype(jnp.bfloat16)
        total_one, total_two, total_b_one, total_b_two = running
        running = (total_one.at[ids_blk].add(grad_one), total_two.at[ids_blk].add(grad_two),
                   total_b_one.at[ids_blk].add(bias_one), total_b_two.at[ids_blk].add(bias_two))
        return running, (result, input_grad)

    initial = (jnp.zeros((MEMBERS, 9 * CH, CH), jnp.float32), jnp.zeros((MEMBERS, 9 * CH, CH), jnp.float32),
               jnp.zeros((MEMBERS, CH), jnp.float32), jnp.zeros((MEMBERS, CH), jnp.float32))
    running, (results, input_grads) = lax.scan(one_block, initial, jnp.arange(num_blocks, dtype=jnp.int32))
    return (results.reshape(acts.shape), input_grads.reshape(acts.shape),
            running[0], running[1], running[2], running[3])
```

```python
import functools

import jax
import jax.numpy as jnp
from jax import lax
from jax.experimental import pallas as pl
from jax.experimental.pallas import tpu as pltpu
from jax.sharding import PartitionSpec as P

BOARD = 10


def flipped(weight):
    channels = weight.shape[-1]
    stacked = weight.reshape(weight.shape[:-2] + (9, channels, channels))
    reversed_taps = jnp.flip(stacked, axis=-3)
    return jnp.swapaxes(reversed_taps, -1, -2).reshape(weight.shape)


def silu_slope(pre_act):
    sigmoid_vals = jax.nn.sigmoid(pre_act)
    return sigmoid_vals * (1.0 + pre_act * (1.0 - sigmoid_vals))


def board_conv(values, weight):
    count = values.shape[0]
    channels = values.shape[-1]
    side = BOARD
    boards = values.reshape(count, side, side, channels)
    kernel = weight.reshape(3, 3, channels, channels)
    result = lax.conv_general_dilated(
        boards,
        kernel,
        (1, 1),
        ((1, 1), (1, 1)),
        dimension_numbers=("NHWC", "HWIO", "NHWC"),
        preferred_element_type=jnp.float32,
    )
    return result.reshape(count, side * side, channels)


def weight_conv(values, grads):
    count = values.shape[0]
    channels = values.shape[-1]
    side = BOARD
    boards = values.reshape(count, side, side, channels)
    grad_boards = grads.reshape(count, side, side, channels)
    result = lax.conv_general_dilated(
        boards,
        grad_boards,
        (1, 1),
        ((1, 1), (1, 1)),
        dimension_numbers=("CHWN", "IHWO", "NHWC"),
        preferred_element_type=jnp.float32,
    )
    return jnp.transpose(result, (1, 2, 0, 3)).reshape(9 * channels, channels)


def shards(acts, cotangent, routes, w_first, w_second, b_first, b_second):
    per_owner = w_first.shape[0]
    owners = lax.axis_size("member")
    members_all = owners * per_owner
    capacity = max(2, 4 * routes.shape[0] // members_all)
    channels = acts.shape[-1]
    cell_count = acts.shape[-2]
    member_ids = routes.reshape(-1)
    onehot = (member_ids[:, None] == jnp.arange(members_all, dtype=jnp.int32)[None, :]).astype(
        jnp.int32
    )
    order = jnp.arange(member_ids.shape[0], dtype=jnp.int32)
    earlier = jnp.sum((order[:, None] > order[None, :])[:, :, None] * onehot[None], axis=1)
    slot_index = jnp.sum(earlier * onehot, axis=1)
    target = member_ids * capacity + slot_index
    dispatch = (
        jnp.arange(members_all * capacity, dtype=jnp.int32)[:, None] == target[None, :]
    ).astype(jnp.bfloat16)

    def scatter_rows(values):
        flattened = values.reshape(-1, cell_count * channels)
        placed = jnp.dot(dispatch, flattened, preferred_element_type=jnp.float32).astype(
            jnp.bfloat16
        )
        return placed.reshape(members_all, capacity, cell_count, channels)

    def gather_rows(values):
        flattened = values.reshape(members_all * capacity, cell_count * channels)
        picked = jnp.dot(dispatch.T, flattened, preferred_element_type=jnp.float32).astype(
            jnp.bfloat16
        )
        return picked.reshape(acts.shape)

    def to_local(received):
        grouped = received.reshape(owners, per_owner, capacity, cell_count, channels)
        return jnp.swapaxes(grouped, 0, 1).reshape(
            per_owner, owners * capacity, cell_count, channels
        )

    def from_local(values):
        grouped = values.reshape(per_owner, owners, capacity, cell_count, channels)
        return jnp.swapaxes(grouped, 0, 1).reshape(members_all, capacity, cell_count, channels)

    send_acts = scatter_rows(acts)
    send_grads = scatter_rows(cotangent)
    recv_acts, recv_grads = (
        lax.all_to_all(send_acts, "member", split_axis=0, concat_axis=0, tiled=True),
        lax.all_to_all(send_grads, "member", split_axis=0, concat_axis=0, tiled=True),
    )
    inputs = to_local(recv_acts)
    upstream = to_local(recv_grads)
    owned = 0
    pre_one = board_conv(inputs[owned], w_first[owned]) + b_first[owned][None, None, :]
    hidden_one = jax.nn.silu(pre_one).astype(jnp.bfloat16)
    result_one = (
        inputs[owned].astype(jnp.float32)
        + board_conv(hidden_one, w_second[owned])
        + b_second[owned][None, None, :]
    ).astype(jnp.bfloat16)
    pre_list = [pre_one]
    hidden_list = [hidden_one]
    result_list = [result_one]
    result = jnp.stack(result_list)
    owned = 0
    upstream_one = upstream[owned]
    grad_two_list = [weight_conv(hidden_list[owned], upstream_one)]
    bias_two_list = [jnp.sum(upstream_one.astype(jnp.float32), axis=(0, 1))]
    hidden_grad = board_conv(upstream_one, flipped(w_second[owned]))
    pre_grad = (hidden_grad * silu_slope(pre_list[owned])).astype(jnp.bfloat16)
    grad_one_list = [weight_conv(inputs[owned], pre_grad)]
    bias_one_list = [jnp.sum(pre_grad.astype(jnp.float32), axis=(0, 1))]
    input_list = [
        (upstream_one.astype(jnp.float32) + board_conv(pre_grad, flipped(w_first[owned]))).astype(
            jnp.bfloat16
        )
    ]
    input_grad = jnp.stack(input_list)
    grad_one = jnp.stack(grad_one_list)
    grad_two = jnp.stack(grad_two_list)
    bias_one = jnp.stack(bias_one_list)
    bias_two = jnp.stack(bias_two_list)
    back_out, back_in = (
        lax.all_to_all(from_local(result), "member", split_axis=0, concat_axis=0, tiled=True),
        lax.all_to_all(from_local(input_grad), "member", split_axis=0, concat_axis=0, tiled=True),
    )
    totals = lax.psum((grad_one, grad_two, bias_one, bias_two), "rep")
    return (gather_rows(back_out), gather_rows(back_in), totals[0], totals[1], totals[2], totals[3])


SLOTS = 8
SIDE = BOARD + 2
CELLS = BOARD * BOARD
ROWS = CELLS * SLOTS
LINE = BOARD * SLOTS
PLACES = SIDE * SIDE * SLOTS
TAIL = 64
MESH_ID = pl.DeviceIdType.MESH

ORDER = (
    ["A0", "A1", "B0", "C0", "A2", "A4", "A3", "A5", "A6", "A7"]
    + ["B2", "B4", "C2", "B6", "B7", "B3", "B5", "B1"]
    + ["C1", "C4", "C3", "C5", "C6", "C7"]
)
AT = {name: index for index, name in enumerate(ORDER)}


def inner(line):
    return ((line + 1) * SIDE + 1) * SLOTS


def wide(lhs, rhs):
    return lax.dot_general(lhs, rhs, (((1,), (1,)), ((), ())), preferred_element_type=jnp.float32)


def league_kernel(
    table, acts_in, cot_in, w1_in, w2_in, b_in,
    out_ref, back_ref, grad_one, grad_two, bias_one, bias_two,
    acts, cot, w1, w2, bs, xb, gb, hb, pb, slope, mix, res_out, res_back,
    even, odd, paired, chips, diag, cross, total, split, parts, whole,
    load_sems, w_send, w_recv, g_send, g_recv, z_send, z_recv,
):
    f32, bf16 = jnp.float32, jnp.bfloat16
    channels = w1.shape[-1]
    taps = 9 * channels
    half_w = taps // 2
    rows_g = taps + TAIL
    half_g = rows_g // 2
    copies = whole.shape[1]
    quarter = rows_g // copies
    me = lax.axis_index("member")
    rep = lax.axis_index("rep")
    near = {"core": me ^ 1, "x": me ^ 2, "y": me ^ 4}

    loads = [
        pltpu.make_async_copy(src, dst, load_sems.at[at])
        for at, (src, dst) in enumerate(
            ((acts_in, acts), (cot_in, cot), (w1_in.at[0], w1.at[0]), (w2_in.at[0], w2.at[0]), (b_in, bs.at[0]))
        )
    ]
    for load in loads:
        load.start()

    barrier = pltpu.get_barrier_semaphore()
    for peer in near.values():
        pl.semaphore_signal(barrier, inc=1, device_id={"member": peer}, device_id_type=MESH_ID)
    for far in range(1, copies):
        pl.semaphore_signal(barrier, inc=1, device_id={"rep": rep ^ far}, device_id_type=MESH_ID)

    for ref in (xb, gb, hb, pb):
        ref[...] = jnp.zeros_like(ref)
    for load in loads:
        load.wait()
    pl.semaphore_wait(barrier, 2 + copies)

    def remote(src, dst, sends, recvs, at, peer):
        return pltpu.make_async_remote_copy(
            src_ref=src, dst_ref=dst, send_sem=sends.at[at], recv_sem=recvs.at[at],
            device_id=peer, device_id_type=MESH_ID,
        )

    def member(name):
        return {"member": near[name]}

    low, high = pl.ds(0, half_w), pl.ds(half_w, taps - half_w)

    def give(kind, at):
        buffer = (w1, w2, bs)[kind]
        moves = [
            (0, 1, None, "core"), (0, 2, None, "x"), (0, 4, None, "y"),
            (2, 3, None, "core"), (4, 5, None, "core"),
            (2, 6, low, "y"), (4, 6, high, "x"), (6, 7, None, "core"),
        ]
        src, dst, rows, peer = moves[at]
        if kind == 2 or rows is None:
            pair = (buffer.at[src], buffer.at[dst])
        else:
            pair = (buffer.at[src, rows, :], buffer.at[dst, rows, :])
        return remote(pair[0], pair[1], w_send, w_recv, kind * 8 + at, member(peer))

    def biases(ats):
        return [at for at in ats if at != 6]

    def send_weights(kind, ats):
        for at in ats:
            give(kind, at).start()
        if kind == 0:
            for at in biases(ats):
                give(2, at).start()

    def have_weights(kind, ats):
        for at in ats:
            give(kind, at).wait_recv()
        if kind == 0:
            for at in biases(ats):
                give(2, at).wait_recv()

    first, second = pl.ds(0, half_g), pl.ds(half_g, half_g)

    def grad_copy(j, at):
        if at < 4:
            return remote(odd.at[j, at], paired.at[j, at], g_send, g_recv, j * 8 + at, member("core"))
        if at == 4:
            return remote(chips.at[j, 3, first, :], diag.at[j, 0], g_send, g_recv, j * 8 + 4, member("x"))
        if at == 5:
            return remote(chips.at[j, 3, second, :], diag.at[j, 1], g_send, g_recv, j * 8 + 5, member("y"))
        return remote(
            chips.at[j, at - 5], cross.at[j, at - 6], g_send, g_recv, j * 8 + at, member("x" if at == 6 else "y")
        )

    def rep_copy(j, stage, far):
        at = (j * 2 + stage) * copies + far
        peer = {"rep": rep ^ far}
        if stage == 0:
            return remote(
                split.at[j, pl.ds((rep ^ far) * quarter, quarter), :], parts.at[j, far - 1], z_send, z_recv, at, peer
            )
        return remote(whole.at[j, rep], whole.at[j, rep], z_send, z_recv, at, peer)

    def arrived_rep(j, far):
        return remote(
            whole.at[j, rep], whole.at[j, rep ^ far], z_send, z_recv, (j * 2 + 1) * copies + far, {"rep": rep ^ far}
        )

    def pair_up(j, p):
        grad_copy(j, p).wait_recv()
        return even[j, p] + paired[j, p].astype(f32)

    def send_diag(j):
        chips[j, 3] = pair_up(j, 3).astype(bf16)
        grad_copy(j, 4).start()
        grad_copy(j, 5).start()

    def send_cross(j, p):
        value = pair_up(j, p)
        if p == 1:
            grad_copy(j, 5).wait_recv()
            chips[j, 1, :half_g] = value[:half_g].astype(bf16)
            chips[j, 1, half_g:] = (value[half_g:] + diag[j, 1].astype(f32)).astype(bf16)
            grad_copy(j, 6).start()
        else:
            grad_copy(j, 4).wait_recv()
            chips[j, 2, :half_g] = (value[:half_g] + diag[j, 0].astype(f32)).astype(bf16)
            chips[j, 2, half_g:] = value[half_g:].astype(bf16)
            grad_copy(j, 7).start()

    def send_split(j):
        value = pair_up(j, 0)
        grad_copy(j, 6).wait_recv()
        grad_copy(j, 7).wait_recv()
        value = value + cross[j, 0].astype(f32) + cross[j, 1].astype(f32)
        total[j] = value
        split[j] = value.astype(bf16)
        for far in range(1, copies):
            rep_copy(j, 0, far).start()

    def send_whole(j):
        mine = total[j, pl.ds(rep * quarter, quarter), :]
        for far in range(1, copies):
            rep_copy(j, 0, far).wait_recv()
            mine = mine + parts[j, far - 1].astype(f32)
        whole[j, rep] = mine.astype(bf16)
        for far in range(1, copies):
            rep_copy(j, 1, far).start()

    def finish(j):
        grad, bias = ((grad_one, bias_one), (grad_two, bias_two))[j]
        for far in range(1, copies):
            arrived_rep(j, far).wait_recv()
        stacked = jnp.concatenate([whole[j, at] for at in range(copies)], axis=0).astype(f32)
        for tap in range(9):
            rows = slice(tap * channels, (tap + 1) * channels)
            grad[0, rows, :] = stacked[rows].T
        bias[...] = whole[j, copies - 1, quarter - TAIL : quarter - TAIL + 8].astype(f32)[:1]

    def patch(board, q):
        columns = []
        for tap in range(9):
            down, right = tap // 3, tap % 3
            lines = []
            for line in range(BOARD):
                start = ((line + down) * SIDE + right) * SLOTS
                lines.append(board[q, start : start + LINE, :])
            columns.append(jnp.concatenate(lines, axis=0))
        return jnp.concatenate(columns, axis=1)

    def put(board, q, value):
        for line in range(BOARD):
            board[q, inner(line) : inner(line) + LINE, :] = value[line * LINE : (line + 1) * LINE].astype(bf16)

    def centre(board, q):
        return jnp.concatenate(
            [board[q, inner(line) : inner(line) + LINE, :] for line in range(BOARD)], axis=0
        ).astype(f32)

    def flipped_wide(weight, q):
        return jnp.concatenate(
            [weight[q, (8 - tap) * channels : (9 - tap) * channels, :] for tap in range(9)], axis=1
        )

    def gather(src, board, q):
        for slot in range(SLOTS):
            row = table[q * SLOTS + slot]
            value = src[jnp.maximum(row, 0)].astype(f32)
            mix[pl.ds(slot, CELLS, stride=SLOTS), :] = jnp.where(row >= 0, value, 0.0)
        put(board, q, mix[...])

    def spread(ref, q, value):
        mix[...] = value
        for slot in range(SLOTS):
            ref[q * SLOTS + slot] = mix[pl.ds(slot, CELLS, stride=SLOTS), :].astype(bf16)

    def keep_grad(j, q, grad, patches):
        turned = jnp.dot(grad.T.astype(bf16), patches, preferred_element_type=f32)
        bias = jnp.broadcast_to(jnp.sum(grad, axis=0, keepdims=True), (TAIL, channels))
        pair = q // 2

        def write(ref, kind):
            for tap in range(9):
                ref[j, pair, tap * channels : (tap + 1) * channels, :] = turned[
                    :, tap * channels : (tap + 1) * channels
                ].astype(kind)
            ref[j, pair, taps:, :] = bias.astype(kind)

        @pl.when(q % 2 == 0)
        def _():
            write(even, f32)

        @pl.when(q % 2 == 1)
        def _():
            write(odd, bf16)

    def phase_a(q):
        gather(acts, xb, q)
        gather(cot, gb, q)
        pre = jnp.dot(patch(xb, q), w1[q], preferred_element_type=f32) + bs[q, 0:1]
        gate = 0.5 * jnp.tanh(0.5 * pre) + 0.5
        slope[q] = gate * (1.0 + pre * (1.0 - gate))
        put(hb, q, pre * gate)
        keep_grad(1, q, centre(gb, q), patch(hb, q))

    def phase_b(q):
        pre_grad = wide(patch(gb, q), flipped_wide(w2, q)) * slope[q]
        put(pb, q, pre_grad)
        keep_grad(0, q, pre_grad.astype(bf16).astype(f32), patch(xb, q))

    def phase_c(q):
        spread(
            res_out, q,
            jnp.dot(patch(hb, q), w2[q], preferred_element_type=f32) + bs[q, 1:2] + centre(xb, q),
        )
        spread(res_back, q, wide(patch(pb, q), flipped_wide(w1, q)) + centre(gb, q))

    before = {name: [] for name in ORDER}

    def on(name, action, *args):
        before[name].append(functools.partial(action, *args))

    send_weights(0, (1, 2, 0))
    on("A1", have_weights, 0, (0,))
    on("A2", have_weights, 0, (1, 2))
    on("A2", send_weights, 0, (5, 6, 3, 4))
    on("A2", send_weights, 1, (1, 2, 0))
    on("A3", have_weights, 0, (3,))
    on("A5", have_weights, 0, (4,))
    on("A6", have_weights, 0, (5, 6))
    on("A6", send_weights, 0, (7,))
    on("A7", have_weights, 0, (7,))
    on("B2", have_weights, 1, (1, 2))
    on("B2", send_weights, 1, (5, 6, 3, 4))
    on("B6", have_weights, 1, (5, 6))
    on("B6", send_weights, 1, (7,))
    on("B7", have_weights, 1, (7,))
    on("B3", have_weights, 1, (3,))
    on("B5", have_weights, 1, (4,))
    on("B1", have_weights, 1, (0,))

    for j, phase in ((1, "A"), (0, "B")):
        for p in range(4):
            done = AT[phase + str(2 * p + 1)]
            on(ORDER[done + 1], lambda j=j, p=p: grad_copy(j, p).start())

    on("B4", send_diag, 1)
    on("B6", send_cross, 1, 1)
    on("B6", send_cross, 1, 2)
    on("B5", send_diag, 0)
    on("C1", send_split, 1)
    on("C1", send_cross, 0, 1)
    on("C4", send_cross, 0, 2)
    on("C5", send_whole, 1)
    on("C7", send_split, 0)

    phases = {"A": phase_a, "B": phase_b, "C": phase_c}

    def step(at, carry):
        q = jnp.int32(0)
        kind = jnp.int32(0)
        for index, name in enumerate(ORDER):
            q = jnp.where(at == index, int(name[1]), q)
            kind = jnp.where(at == index, "ABC".index(name[0]), kind)
            if before[name]:

                @pl.when(at == index)
                def _(name=name):
                    for action in before[name]:
                        action()

        for index, name in enumerate("ABC"):

            @pl.when(kind == index)
            def _(name=name):
                phases[name](q)

        return carry

    lax.fori_loop(0, len(ORDER), step, 0)

    send_whole(0)
    for row in range(out_ref.shape[0]):
        at = table[8 * SLOTS + row]
        out_ref[row] = res_out[at]
        back_ref[row] = res_back[at]
    finish(1)
    finish(0)

    for kind in range(3):
        for at in range(8):
            if kind < 2 or at != 6:
                give(kind, at).wait_send()
    for j in range(2):
        for at in range(8):
            grad_copy(j, at).wait_send()
        for stage in range(2):
            for far in range(1, copies):
                rep_copy(j, stage, far).wait_send()


def at_home(acts, cotangent, routes, w_first, w_second, b_first, b_second):
    owners = lax.axis_size("member")
    copies = lax.axis_size("rep")
    channels = acts.shape[-1]
    taps = 9 * channels
    rows_g = taps + TAIL
    f32, bf16 = jnp.float32, jnp.bfloat16
    me = lax.axis_index("member")
    ids = routes.reshape(-1)
    count = ids.shape[0]
    order = jnp.arange(count, dtype=jnp.int32)
    place = jnp.sum(((order[:, None] > order[None, :]) & (ids[:, None] == ids[None, :])).astype(jnp.int32), axis=1)
    position = (ids ^ me) * SLOTS + place
    hit = position[None, :] == jnp.arange(owners * SLOTS, dtype=jnp.int32)[:, None]
    rows = jnp.sum(jnp.where(hit, order[None, :] + 1, 0), axis=1) - 1
    table = jnp.concatenate([rows, position])
    biases = jnp.concatenate([b_first, b_second, jnp.zeros((6, channels), f32)], axis=0)

    x = acts.reshape((count,) + acts.shape[2:])
    g = cotangent.reshape((count,) + acts.shape[2:])
    anywhere = pl.BlockSpec(memory_space=pl.ANY)
    vmem = pl.BlockSpec(memory_space=pltpu.VMEM)
    shape = jax.ShapeDtypeStruct
    board = pltpu.VMEM((owners, PLACES, channels), bf16)
    weight = pltpu.VMEM((owners, taps, channels), bf16)
    results = pltpu.VMEM((owners * SLOTS, CELLS, channels), bf16)
    sems = pltpu.SemaphoreType.DMA
    made = pl.pallas_call(
        league_kernel,
        out_shape=(
            shape(x.shape, bf16),
            shape(x.shape, bf16),
            shape((1, taps, channels), f32),
            shape((1, taps, channels), f32),
            shape((1, channels), f32),
            shape((1, channels), f32),
        ),
        in_specs=[pl.BlockSpec(memory_space=pltpu.SMEM)] + [anywhere] * 5,
        out_specs=(vmem,) * 6,
        scratch_shapes=[
            pltpu.VMEM(x.shape, bf16),
            pltpu.VMEM(x.shape, bf16),
            weight,
            weight,
            pltpu.VMEM((owners, 8, channels), f32),
            board,
            board,
            board,
            board,
            pltpu.VMEM((owners, ROWS, channels), f32),
            pltpu.VMEM((ROWS, channels), f32),
            results,
            results,
            pltpu.VMEM((2, 4, rows_g, channels), f32),
            pltpu.VMEM((2, 4, rows_g, channels), bf16),
            pltpu.VMEM((2, 4, rows_g, channels), bf16),
            pltpu.VMEM((2, 4, rows_g, channels), bf16),
            pltpu.VMEM((2, 2, rows_g // 2, channels), bf16),
            pltpu.VMEM((2, 2, rows_g, channels), bf16),
            pltpu.VMEM((2, rows_g, channels), f32),
            pltpu.VMEM((2, rows_g, channels), bf16),
            pltpu.VMEM((2, copies - 1, rows_g // copies, channels), bf16),
            pltpu.VMEM((2, copies, rows_g // copies, channels), bf16),
            sems((5,)),
            sems((24,)),
            sems((24,)),
            sems((16,)),
            sems((16,)),
            sems((4 * copies,)),
            sems((4 * copies,)),
        ],
        compiler_params=pltpu.CompilerParams(
            collective_id=0, has_side_effects=True, vmem_limit_bytes=60 * 1024 * 1024
        ),
        cost_estimate=pl.CostEstimate(
            flops=12 * owners * ROWS * taps * channels, bytes_accessed=9000000, transcendentals=owners * ROWS * channels
        ),
        name="league",
    )(table, x, g, w_first, w_second, biases)
    return (made[0].reshape(acts.shape), made[1].reshape(acts.shape)) + tuple(made[2:])


def solution(mesh):
    placed = (
        P(("rep", "member"), None, None, None),
        P(("rep", "member"), None, None, None),
        P(("rep", "member"), None),
        P("member", None, None),
        P("member", None, None),
        P("member", None),
        P("member", None),
    )
    return jax.shard_map(
        at_home if mesh.shape["member"] == 8 and mesh.shape["rep"] == 4 else shards,
        mesh=mesh,
        in_specs=placed,
        out_specs=(
            P(("rep", "member"), None, None, None),
            P(("rep", "member"), None, None, None),
            P("member", None, None),
            P("member", None, None),
            P("member", None),
            P("member", None),
        ),
        check_vma=False,
    )
```

```python
import functools

import jax
import jax.numpy as jnp
from jax import lax
from jax.experimental import pallas as pl
from jax.experimental.pallas import tpu as pltpu
from jax.sharding import PartitionSpec as P

BOARD = 10


def flipped(weight):
    channels = weight.shape[-1]
    stacked = weight.reshape(weight.shape[:-2] + (9, channels, channels))
    reversed_taps = jnp.flip(stacked, axis=-3)
    return jnp.swapaxes(reversed_taps, -1, -2).reshape(weight.shape)


def silu_slope(pre_act):
    sigmoid_vals = jax.nn.sigmoid(pre_act)
    return sigmoid_vals * (1.0 + pre_act * (1.0 - sigmoid_vals))


def board_conv(values, weight):
    count = values.shape[0]
    channels = values.shape[-1]
    side = BOARD
    boards = values.reshape(count, side, side, channels)
    kernel = weight.reshape(3, 3, channels, channels)
    result = lax.conv_general_dilated(
        boards,
        kernel,
        (1, 1),
        ((1, 1), (1, 1)),
        dimension_numbers=("NHWC", "HWIO", "NHWC"),
        preferred_element_type=jnp.float32,
    )
    return result.reshape(count, side * side, channels)


def weight_conv(values, grads):
    count = values.shape[0]
    channels = values.shape[-1]
    side = BOARD
    boards = values.reshape(count, side, side, channels)
    grad_boards = grads.reshape(count, side, side, channels)
    result = lax.conv_general_dilated(
        boards,
        grad_boards,
        (1, 1),
        ((1, 1), (1, 1)),
        dimension_numbers=("CHWN", "IHWO", "NHWC"),
        preferred_element_type=jnp.float32,
    )
    return jnp.transpose(result, (1, 2, 0, 3)).reshape(9 * channels, channels)


def shards(acts, cotangent, routes, w_first, w_second, b_first, b_second):
    per_owner = w_first.shape[0]
    owners = lax.axis_size("member")
    members_all = owners * per_owner
    capacity = max(2, 4 * routes.shape[0] // members_all)
    channels = acts.shape[-1]
    cell_count = acts.shape[-2]
    member_ids = routes.reshape(-1)
    onehot = (member_ids[:, None] == jnp.arange(members_all, dtype=jnp.int32)[None, :]).astype(
        jnp.int32
    )
    order = jnp.arange(member_ids.shape[0], dtype=jnp.int32)
    earlier = jnp.sum((order[:, None] > order[None, :])[:, :, None] * onehot[None], axis=1)
    slot_index = jnp.sum(earlier * onehot, axis=1)
    target = member_ids * capacity + slot_index
    dispatch = (
        jnp.arange(members_all * capacity, dtype=jnp.int32)[:, None] == target[None, :]
    ).astype(jnp.bfloat16)

    def scatter_rows(values):
        flattened = values.reshape(-1, cell_count * channels)
        placed = jnp.dot(dispatch, flattened, preferred_element_type=jnp.float32).astype(
            jnp.bfloat16
        )
        return placed.reshape(members_all, capacity, cell_count, channels)

    def gather_rows(values):
        flattened = values.reshape(members_all * capacity, cell_count * channels)
        picked = jnp.dot(dispatch.T, flattened, preferred_element_type=jnp.float32).astype(
            jnp.bfloat16
        )
        return picked.reshape(acts.shape)

    def to_local(received):
        grouped = received.reshape(owners, per_owner, capacity, cell_count, channels)
        return jnp.swapaxes(grouped, 0, 1).reshape(
            per_owner, owners * capacity, cell_count, channels
        )

    def from_local(values):
        grouped = values.reshape(per_owner, owners, capacity, cell_count, channels)
        return jnp.swapaxes(grouped, 0, 1).reshape(members_all, capacity, cell_count, channels)

    send_acts = scatter_rows(acts)
    send_grads = scatter_rows(cotangent)
    recv_acts, recv_grads = (
        lax.all_to_all(send_acts, "member", split_axis=0, concat_axis=0, tiled=True),
        lax.all_to_all(send_grads, "member", split_axis=0, concat_axis=0, tiled=True),
    )
    inputs = to_local(recv_acts)
    upstream = to_local(recv_grads)
    owned = 0
    pre_one = board_conv(inputs[owned], w_first[owned]) + b_first[owned][None, None, :]
    hidden_one = jax.nn.silu(pre_one).astype(jnp.bfloat16)
    result_one = (
        inputs[owned].astype(jnp.float32)
        + board_conv(hidden_one, w_second[owned])
        + b_second[owned][None, None, :]
    ).astype(jnp.bfloat16)
    pre_list = [pre_one]
    hidden_list = [hidden_one]
    result_list = [result_one]
    result = jnp.stack(result_list)
    owned = 0
    upstream_one = upstream[owned]
    grad_two_list = [weight_conv(hidden_list[owned], upstream_one)]
    bias_two_list = [jnp.sum(upstream_one.astype(jnp.float32), axis=(0, 1))]
    hidden_grad = board_conv(upstream_one, flipped(w_second[owned]))
    pre_grad = (hidden_grad * silu_slope(pre_list[owned])).astype(jnp.bfloat16)
    grad_one_list = [weight_conv(inputs[owned], pre_grad)]
    bias_one_list = [jnp.sum(pre_grad.astype(jnp.float32), axis=(0, 1))]
    input_list = [
        (upstream_one.astype(jnp.float32) + board_conv(pre_grad, flipped(w_first[owned]))).astype(
            jnp.bfloat16
        )
    ]
    input_grad = jnp.stack(input_list)
    grad_one = jnp.stack(grad_one_list)
    grad_two = jnp.stack(grad_two_list)
    bias_one = jnp.stack(bias_one_list)
    bias_two = jnp.stack(bias_two_list)
    back_out, back_in = (
        lax.all_to_all(from_local(result), "member", split_axis=0, concat_axis=0, tiled=True),
        lax.all_to_all(from_local(input_grad), "member", split_axis=0, concat_axis=0, tiled=True),
    )
    totals = lax.psum((grad_one, grad_two, bias_one, bias_two), "rep")
    return (gather_rows(back_out), gather_rows(back_in), totals[0], totals[1], totals[2], totals[3])


SLOTS = 8
SIDE = BOARD + 2
CELLS = BOARD * BOARD
ROWS = CELLS * SLOTS
LINE = BOARD * SLOTS
PLACES = SIDE * SIDE * SLOTS
TAIL = 64
MESH_ID = pl.DeviceIdType.MESH

ORDER = (
    ["A0", "A1", "B0", "C0", "A2", "A4", "A3", "A5", "A6", "A7"]
    + ["B2", "B4", "C2", "B6", "B7", "B3", "B5", "B1"]
    + ["C1", "C4", "C3", "C5", "C6", "C7"]
)
AT = {name: index for index, name in enumerate(ORDER)}


def inner(line):
    return ((line + 1) * SIDE + 1) * SLOTS


def wide(lhs, rhs):
    return lax.dot_general(lhs, rhs, (((1,), (1,)), ((), ())), preferred_element_type=jnp.float32)


def league_kernel(
    table, acts_in, cot_in, w1_in, w2_in, b1_in, b2_in,
    out_ref, back_ref, whole,
    acts_pair, cot_pair, pair, acts, cot, w1, w2, bs, xb, gb, hb, pb, slope, mix, res_out, res_back,
    even, odd, paired, chips, diag, cross, total, split, parts,
    load_sems, w_send, w_recv, g_send, g_recv, z_send, z_recv,
):
    f32, bf16 = jnp.float32, jnp.bfloat16
    channels = w1.shape[-1]
    taps = 9 * channels
    half_w = taps // 2
    rows_g = taps + TAIL
    half_g = rows_g // 2
    copies = whole.shape[1]
    quarter = rows_g // copies
    me = lax.axis_index("member")
    rep = lax.axis_index("rep")
    near = {"core": me ^ 1, "x": me ^ 2, "y": me ^ 4}

    loads = [
        pltpu.make_async_copy(src, dst, load_sems.at[at])
        for at, (src, dst) in enumerate(
            (
                (w1_in.at[0], w1.at[0]), (w2_in.at[0], w2.at[0]),
                (b1_in, bs.at[0, pl.ds(0, 1), :]), (b2_in, bs.at[0, pl.ds(1, 1), :]),
                (acts_in, acts_pair), (cot_in, cot_pair),
            )
        )
    ]
    for load in loads:
        load.start()

    barrier = pltpu.get_barrier_semaphore()
    for peer in near.values():
        pl.semaphore_signal(barrier, inc=1, device_id={"member": peer}, device_id_type=MESH_ID)
    for far in range(1, copies):
        pl.semaphore_signal(barrier, inc=1, device_id={"rep": rep ^ far}, device_id_type=MESH_ID)

    for ref in (xb, gb, hb, pb):
        ref[...] = jnp.zeros_like(ref)
    for load in loads:
        load.wait()

    def apart(state, carry):
        for at, (src, dst) in enumerate(((acts_pair, acts), (cot_pair, cot))):
            pair[at] = src[state].astype(f32)
            for side in range(2):
                dst[state * 2 + side] = pair[at, pl.ds(side, CELLS, stride=2), :].astype(bf16)
        return carry

    lax.fori_loop(0, acts_pair.shape[0], apart, 0)
    pl.semaphore_wait(barrier, 2 + copies)

    def remote(src, dst, sends, recvs, at, peer):
        return pltpu.make_async_remote_copy(
            src_ref=src, dst_ref=dst, send_sem=sends.at[at], recv_sem=recvs.at[at],
            device_id=peer, device_id_type=MESH_ID,
        )

    def member(name):
        return {"member": near[name]}

    low, high = pl.ds(0, half_w), pl.ds(half_w, taps - half_w)

    def give(kind, at):
        buffer = (w1, w2, bs)[kind]
        moves = [
            (0, 1, None, "core"), (0, 2, None, "x"), (0, 4, None, "y"),
            (2, 3, None, "core"), (4, 5, None, "core"),
            (2, 6, low, "y"), (4, 6, high, "x"), (6, 7, None, "core"),
        ]
        src, dst, rows, peer = moves[at]
        if kind == 2 or rows is None:
            pair = (buffer.at[src], buffer.at[dst])
        else:
            pair = (buffer.at[src, rows, :], buffer.at[dst, rows, :])
        return remote(pair[0], pair[1], w_send, w_recv, kind * 8 + at, member(peer))

    def biases(ats):
        return [at for at in ats if at != 6]

    def send_weights(kind, ats):
        for at in ats:
            give(kind, at).start()
        if kind == 0:
            for at in biases(ats):
                give(2, at).start()

    def have_weights(kind, ats):
        for at in ats:
            give(kind, at).wait_recv()
        if kind == 0:
            for at in biases(ats):
                give(2, at).wait_recv()

    first, second = pl.ds(0, half_g), pl.ds(half_g, half_g)

    def grad_copy(j, at):
        if at < 4:
            return remote(odd.at[j, at], paired.at[j, at], g_send, g_recv, j * 8 + at, member("core"))
        if at == 4:
            return remote(chips.at[j, 3, first, :], diag.at[j, 0], g_send, g_recv, j * 8 + 4, member("x"))
        if at == 5:
            return remote(chips.at[j, 3, second, :], diag.at[j, 1], g_send, g_recv, j * 8 + 5, member("y"))
        return remote(
            chips.at[j, at - 5], cross.at[j, at - 6], g_send, g_recv, j * 8 + at, member("x" if at == 6 else "y")
        )

    def rep_copy(j, stage, far):
        at = (j * 2 + stage) * copies + far
        peer = {"rep": rep ^ far}
        if stage == 0:
            return remote(
                split.at[j, pl.ds((rep ^ far) * quarter, quarter), :], parts.at[j, far - 1], z_send, z_recv, at, peer
            )
        return remote(whole.at[j, rep], whole.at[j, rep], z_send, z_recv, at, peer)

    def arrived_rep(j, far):
        return remote(
            whole.at[j, rep], whole.at[j, rep ^ far], z_send, z_recv, (j * 2 + 1) * copies + far, {"rep": rep ^ far}
        )

    def pair_up(j, p):
        grad_copy(j, p).wait_recv()
        return even[j, p] + paired[j, p].astype(f32)

    def send_diag(j):
        chips[j, 3] = pair_up(j, 3).astype(bf16)
        grad_copy(j, 4).start()
        grad_copy(j, 5).start()

    def send_cross(j, p):
        value = pair_up(j, p)
        if p == 1:
            grad_copy(j, 5).wait_recv()
            chips[j, 1, :half_g] = value[:half_g].astype(bf16)
            chips[j, 1, half_g:] = (value[half_g:] + diag[j, 1].astype(f32)).astype(bf16)
            grad_copy(j, 6).start()
        else:
            grad_copy(j, 4).wait_recv()
            chips[j, 2, :half_g] = (value[:half_g] + diag[j, 0].astype(f32)).astype(bf16)
            chips[j, 2, half_g:] = value[half_g:].astype(bf16)
            grad_copy(j, 7).start()

    def send_split(j):
        value = pair_up(j, 0)
        grad_copy(j, 6).wait_recv()
        grad_copy(j, 7).wait_recv()
        value = value + cross[j, 0].astype(f32) + cross[j, 1].astype(f32)
        total[j] = value
        split[j] = value.astype(bf16)
        for far in range(1, copies):
            rep_copy(j, 0, far).start()

    def send_whole(j):
        mine = total[j, pl.ds(rep * quarter, quarter), :]
        for far in range(1, copies):
            rep_copy(j, 0, far).wait_recv()
            mine = mine + parts[j, far - 1].astype(f32)
        whole[j, rep] = mine.astype(bf16)
        for far in range(1, copies):
            rep_copy(j, 1, far).start()

    def finish(j):
        for far in range(1, copies):
            arrived_rep(j, far).wait_recv()

    def patch(board, q):
        columns = []
        for tap in range(9):
            down, right = tap // 3, tap % 3
            lines = []
            for line in range(BOARD):
                start = ((line + down) * SIDE + right) * SLOTS
                lines.append(board[q, start : start + LINE, :])
            columns.append(jnp.concatenate(lines, axis=0))
        return jnp.concatenate(columns, axis=1)

    def put(board, q, value):
        for line in range(BOARD):
            board[q, inner(line) : inner(line) + LINE, :] = value[line * LINE : (line + 1) * LINE].astype(bf16)

    def centre(board, q):
        return jnp.concatenate(
            [board[q, inner(line) : inner(line) + LINE, :] for line in range(BOARD)], axis=0
        ).astype(f32)

    def flipped_wide(weight, q):
        return jnp.concatenate(
            [weight[q, (8 - tap) * channels : (9 - tap) * channels, :] for tap in range(9)], axis=1
        )

    def gather(src, board, q):
        for slot in range(SLOTS):
            row = table[q * SLOTS + slot]
            value = src[jnp.maximum(row, 0)].astype(f32)
            mix[pl.ds(slot, CELLS, stride=SLOTS), :] = jnp.where(row >= 0, value, 0.0)
        put(board, q, mix[...])

    def spread(ref, q, value):
        mix[...] = value
        for slot in range(SLOTS):
            ref[q * SLOTS + slot] = mix[pl.ds(slot, CELLS, stride=SLOTS), :].astype(bf16)

    def keep_grad(j, q, grad, patches):
        turned = jnp.dot(grad.T.astype(bf16), patches, preferred_element_type=f32)
        bias = jnp.broadcast_to(jnp.sum(grad, axis=0, keepdims=True), (TAIL, channels))
        pair = q // 2

        def write(ref, kind):
            for tap in range(9):
                ref[j, pair, tap * channels : (tap + 1) * channels, :] = turned[
                    :, tap * channels : (tap + 1) * channels
                ].astype(kind)
            ref[j, pair, taps:, :] = bias.astype(kind)

        @pl.when(q % 2 == 0)
        def _():
            write(even, f32)

        @pl.when(q % 2 == 1)
        def _():
            write(odd, bf16)

    def phase_a(q):
        gather(acts, xb, q)
        gather(cot, gb, q)
        pre = jnp.dot(patch(xb, q), w1[q], preferred_element_type=f32) + bs[q, 0:1]
        gate = 0.5 * jnp.tanh(0.5 * pre) + 0.5
        slope[q] = gate * (1.0 + pre * (1.0 - gate))
        put(hb, q, pre * gate)
        keep_grad(1, q, centre(gb, q), patch(hb, q))

    def phase_b(q):
        pre_grad = wide(patch(gb, q), flipped_wide(w2, q)) * slope[q]
        put(pb, q, pre_grad)
        keep_grad(0, q, pre_grad.astype(bf16).astype(f32), patch(xb, q))

    def phase_c(q):
        spread(
            res_out, q,
            jnp.dot(patch(hb, q), w2[q], preferred_element_type=f32) + bs[q, 1:2] + centre(xb, q),
        )
        spread(res_back, q, wide(patch(pb, q), flipped_wide(w1, q)) + centre(gb, q))

    before = {name: [] for name in ORDER}

    def on(name, action, *args):
        before[name].append(functools.partial(action, *args))

    send_weights(0, (1, 2, 0))
    on("A1", have_weights, 0, (0,))
    on("A2", have_weights, 0, (1, 2))
    on("A2", send_weights, 0, (5, 6, 3, 4))
    on("A2", send_weights, 1, (1, 2, 0))
    on("A3", have_weights, 0, (3,))
    on("A5", have_weights, 0, (4,))
    on("A6", have_weights, 0, (5, 6))
    on("A6", send_weights, 0, (7,))
    on("A7", have_weights, 0, (7,))
    on("B2", have_weights, 1, (1, 2))
    on("B2", send_weights, 1, (5, 6, 3, 4))
    on("B6", have_weights, 1, (5, 6))
    on("B6", send_weights, 1, (7,))
    on("B7", have_weights, 1, (7,))
    on("B3", have_weights, 1, (3,))
    on("B5", have_weights, 1, (4,))
    on("B1", have_weights, 1, (0,))

    for j, phase in ((1, "A"), (0, "B")):
        for p in range(4):
            done = AT[phase + str(2 * p + 1)]
            on(ORDER[done + 1], lambda j=j, p=p: grad_copy(j, p).start())

    on("B4", send_diag, 1)
    on("B6", send_cross, 1, 1)
    on("B6", send_cross, 1, 2)
    on("B5", send_diag, 0)
    on("C1", send_split, 1)
    on("C1", send_cross, 0, 1)
    on("C4", send_cross, 0, 2)
    on("C5", send_whole, 1)
    on("C7", send_split, 0)

    phases = {"A": phase_a, "B": phase_b, "C": phase_c}

    def step(at, carry):
        q = jnp.int32(0)
        kind = jnp.int32(0)
        for index, name in enumerate(ORDER):
            q = jnp.where(at == index, int(name[1]), q)
            kind = jnp.where(at == index, "ABC".index(name[0]), kind)
            if before[name]:

                @pl.when(at == index)
                def _(name=name):
                    for action in before[name]:
                        action()

        for index, name in enumerate("ABC"):

            @pl.when(kind == index)
            def _(name=name):
                phases[name](q)

        return carry

    lax.fori_loop(0, len(ORDER), step, 0)

    send_whole(0)

    def together(state, carry):
        for at, (src, dst) in enumerate(((res_out, out_ref), (res_back, back_ref))):
            for side in range(2):
                row = table[8 * SLOTS + state * 2 + side]
                pair[at, pl.ds(side, CELLS, stride=2), :] = src[row].astype(f32)
            dst[state] = pair[at].astype(bf16)
        return carry

    lax.fori_loop(0, out_ref.shape[0], together, 0)
    finish(1)
    finish(0)

    for kind in range(3):
        for at in range(8):
            if kind < 2 or at != 6:
                give(kind, at).wait_send()
    for j in range(2):
        for at in range(8):
            grad_copy(j, at).wait_send()
        for stage in range(2):
            for far in range(1, copies):
                rep_copy(j, stage, far).wait_send()


def last_kernel(out_in, back_in, whole, out_ref, back_ref, grad_one, grad_two, bias_one, bias_two, sems):
    channels = whole.shape[-1]
    moves = [
        pltpu.make_async_copy(src, dst, sems.at[at])
        for at, (src, dst) in enumerate(((out_in, out_ref), (back_in, back_ref)))
    ]
    for move in moves:
        move.start()
    copies, quarter = whole.shape[1:3]
    for j, (grad, bias) in enumerate(((grad_one, bias_one), (grad_two, bias_two))):
        stacked = jnp.concatenate([whole[j, at] for at in range(copies)], axis=0).astype(jnp.float32)
        for tap in range(9):
            rows = slice(tap * channels, (tap + 1) * channels)
            grad[0, rows, :] = stacked[rows].T
        bias[...] = whole[j, copies - 1, quarter - TAIL : quarter - TAIL + 8].astype(jnp.float32)[:1]
    for move in moves:
        move.wait()


def at_home(acts, cotangent, routes, w_first, w_second, b_first, b_second):
    owners = lax.axis_size("member")
    copies = lax.axis_size("rep")
    channels = acts.shape[-1]
    taps = 9 * channels
    rows_g = taps + TAIL
    f32, bf16 = jnp.float32, jnp.bfloat16
    me = lax.axis_index("member")
    ids = routes.reshape(-1)
    count = ids.shape[0]
    order = jnp.arange(count, dtype=jnp.int32)
    place = jnp.sum(((order[:, None] > order[None, :]) & (ids[:, None] == ids[None, :])).astype(jnp.int32), axis=1)
    position = (ids ^ me) * SLOTS + place
    hit = position[None, :] == jnp.arange(owners * SLOTS, dtype=jnp.int32)[:, None]
    rows = jnp.sum(jnp.where(hit, order[None, :] + 1, 0), axis=1) - 1
    table = jnp.concatenate([rows, position])
    def paired(values):
        return jnp.swapaxes(values, 1, 2).reshape(values.shape[0], 2 * values.shape[2], channels)

    x, g = paired(acts), paired(cotangent)
    anywhere = pl.BlockSpec(memory_space=pl.ANY)
    vmem = pl.BlockSpec(memory_space=pltpu.VMEM)
    shape = jax.ShapeDtypeStruct
    board = pltpu.VMEM((owners, PLACES, channels), bf16)
    weight = pltpu.VMEM((owners, taps, channels), bf16)
    results = pltpu.VMEM((owners * SLOTS, CELLS, channels), bf16)
    sems = pltpu.SemaphoreType.DMA
    made = pl.pallas_call(
        league_kernel,
        out_shape=(
            shape(x.shape, bf16),
            shape(x.shape, bf16),
            shape((2, copies, rows_g // copies, channels), bf16),
        ),
        in_specs=[pl.BlockSpec(memory_space=pltpu.SMEM)] + [anywhere] * 6,
        out_specs=(vmem,) * 3,
        scratch_shapes=[
            pltpu.VMEM(x.shape, bf16),
            pltpu.VMEM(x.shape, bf16),
            pltpu.VMEM((2, 2 * CELLS, channels), f32),
            pltpu.VMEM((count, CELLS, channels), bf16),
            pltpu.VMEM((count, CELLS, channels), bf16),
            weight,
            weight,
            pltpu.VMEM((owners, 8, channels), f32),
            board,
            board,
            board,
            board,
            pltpu.VMEM((owners, ROWS, channels), f32),
            pltpu.VMEM((ROWS, channels), f32),
            results,
            results,
            pltpu.VMEM((2, 4, rows_g, channels), f32),
            pltpu.VMEM((2, 4, rows_g, channels), bf16),
            pltpu.VMEM((2, 4, rows_g, channels), bf16),
            pltpu.VMEM((2, 4, rows_g, channels), bf16),
            pltpu.VMEM((2, 2, rows_g // 2, channels), bf16),
            pltpu.VMEM((2, 2, rows_g, channels), bf16),
            pltpu.VMEM((2, rows_g, channels), f32),
            pltpu.VMEM((2, rows_g, channels), bf16),
            pltpu.VMEM((2, copies - 1, rows_g // copies, channels), bf16),
            sems((6,)),
            sems((24,)),
            sems((24,)),
            sems((16,)),
            sems((16,)),
            sems((4 * copies,)),
            sems((4 * copies,)),
        ],
        compiler_params=pltpu.CompilerParams(
            collective_id=0, has_side_effects=True, vmem_limit_bytes=60 * 1024 * 1024
        ),
        cost_estimate=pl.CostEstimate(
            flops=12 * owners * ROWS * taps * channels, bytes_accessed=9000000, transcendentals=owners * ROWS * channels
        ),
        name="league",
    )(table, x, g, w_first, w_second, b_first, b_second)
    done = pl.pallas_call(
        last_kernel,
        out_shape=(
            shape(x.shape, bf16),
            shape(x.shape, bf16),
            shape((1, taps, channels), f32),
            shape((1, taps, channels), f32),
            shape((1, channels), f32),
            shape((1, channels), f32),
        ),
        in_specs=[anywhere] * 2 + [vmem],
        out_specs=(anywhere,) * 2 + (vmem,) * 4,
        scratch_shapes=[sems((2,))],
        compiler_params=pltpu.CompilerParams(vmem_limit_bytes=8 * 1024 * 1024),
        cost_estimate=pl.CostEstimate(flops=0, bytes_accessed=5000000, transcendentals=0),
        name="last",
    )(*made)

    def unpaired(values):
        return jnp.swapaxes(values.reshape(acts.shape[0], acts.shape[2], 2, channels), 1, 2)

    return (unpaired(done[0]), unpaired(done[1])) + tuple(done[2:])


def solution(mesh):
    placed = (
        P(("rep", "member"), None, None, None),
        P(("rep", "member"), None, None, None),
        P(("rep", "member"), None),
        P("member", None, None),
        P("member", None, None),
        P("member", None),
        P("member", None),
    )
    return jax.shard_map(
        at_home if mesh.shape["member"] == 8 and mesh.shape["rep"] == 4 else shards,
        mesh=mesh,
        in_specs=placed,
        out_specs=(
            P(("rep", "member"), None, None, None),
            P(("rep", "member"), None, None, None),
            P("member", None, None),
            P("member", None, None),
            P("member", None),
            P("member", None),
        ),
        check_vma=False,
    )
```

```python
import functools

import jax
import jax.numpy as jnp
from jax import lax
from jax.experimental import pallas as pl
from jax.experimental.pallas import tpu as pltpu
from jax.sharding import PartitionSpec as P

BOARD = 10


def flipped(weight):
    channels = weight.shape[-1]
    stacked = weight.reshape(weight.shape[:-2] + (9, channels, channels))
    reversed_taps = jnp.flip(stacked, axis=-3)
    return jnp.swapaxes(reversed_taps, -1, -2).reshape(weight.shape)


def silu_slope(pre_act):
    sigmoid_vals = jax.nn.sigmoid(pre_act)
    return sigmoid_vals * (1.0 + pre_act * (1.0 - sigmoid_vals))


def board_conv(values, weight):
    count = values.shape[0]
    channels = values.shape[-1]
    side = BOARD
    boards = values.reshape(count, side, side, channels)
    kernel = weight.reshape(3, 3, channels, channels)
    result = lax.conv_general_dilated(
        boards,
        kernel,
        (1, 1),
        ((1, 1), (1, 1)),
        dimension_numbers=("NHWC", "HWIO", "NHWC"),
        preferred_element_type=jnp.float32,
    )
    return result.reshape(count, side * side, channels)


def weight_conv(values, grads):
    count = values.shape[0]
    channels = values.shape[-1]
    side = BOARD
    boards = values.reshape(count, side, side, channels)
    grad_boards = grads.reshape(count, side, side, channels)
    result = lax.conv_general_dilated(
        boards,
        grad_boards,
        (1, 1),
        ((1, 1), (1, 1)),
        dimension_numbers=("CHWN", "IHWO", "NHWC"),
        preferred_element_type=jnp.float32,
    )
    return jnp.transpose(result, (1, 2, 0, 3)).reshape(9 * channels, channels)


def shards(acts, cotangent, routes, w_first, w_second, b_first, b_second):
    per_owner = w_first.shape[0]
    owners = lax.axis_size("member")
    members_all = owners * per_owner
    capacity = max(2, 4 * routes.shape[0] // members_all)
    channels = acts.shape[-1]
    cell_count = acts.shape[-2]
    member_ids = routes.reshape(-1)
    onehot = (member_ids[:, None] == jnp.arange(members_all, dtype=jnp.int32)[None, :]).astype(
        jnp.int32
    )
    order = jnp.arange(member_ids.shape[0], dtype=jnp.int32)
    earlier = jnp.sum((order[:, None] > order[None, :])[:, :, None] * onehot[None], axis=1)
    slot_index = jnp.sum(earlier * onehot, axis=1)
    target = member_ids * capacity + slot_index
    dispatch = (
        jnp.arange(members_all * capacity, dtype=jnp.int32)[:, None] == target[None, :]
    ).astype(jnp.bfloat16)

    def scatter_rows(values):
        flattened = values.reshape(-1, cell_count * channels)
        placed = jnp.dot(dispatch, flattened, preferred_element_type=jnp.float32).astype(
            jnp.bfloat16
        )
        return placed.reshape(members_all, capacity, cell_count, channels)

    def gather_rows(values):
        flattened = values.reshape(members_all * capacity, cell_count * channels)
        picked = jnp.dot(dispatch.T, flattened, preferred_element_type=jnp.float32).astype(
            jnp.bfloat16
        )
        return picked.reshape(acts.shape)

    def to_local(received):
        grouped = received.reshape(owners, per_owner, capacity, cell_count, channels)
        return jnp.swapaxes(grouped, 0, 1).reshape(
            per_owner, owners * capacity, cell_count, channels
        )

    def from_local(values):
        grouped = values.reshape(per_owner, owners, capacity, cell_count, channels)
        return jnp.swapaxes(grouped, 0, 1).reshape(members_all, capacity, cell_count, channels)

    send_acts = scatter_rows(acts)
    send_grads = scatter_rows(cotangent)
    recv_acts, recv_grads = (
        lax.all_to_all(send_acts, "member", split_axis=0, concat_axis=0, tiled=True),
        lax.all_to_all(send_grads, "member", split_axis=0, concat_axis=0, tiled=True),
    )
    inputs = to_local(recv_acts)
    upstream = to_local(recv_grads)
    owned = 0
    pre_one = board_conv(inputs[owned], w_first[owned]) + b_first[owned][None, None, :]
    hidden_one = jax.nn.silu(pre_one).astype(jnp.bfloat16)
    result_one = (
        inputs[owned].astype(jnp.float32)
        + board_conv(hidden_one, w_second[owned])
        + b_second[owned][None, None, :]
    ).astype(jnp.bfloat16)
    pre_list = [pre_one]
    hidden_list = [hidden_one]
    result_list = [result_one]
    result = jnp.stack(result_list)
    owned = 0
    upstream_one = upstream[owned]
    grad_two_list = [weight_conv(hidden_list[owned], upstream_one)]
    bias_two_list = [jnp.sum(upstream_one.astype(jnp.float32), axis=(0, 1))]
    hidden_grad = board_conv(upstream_one, flipped(w_second[owned]))
    pre_grad = (hidden_grad * silu_slope(pre_list[owned])).astype(jnp.bfloat16)
    grad_one_list = [weight_conv(inputs[owned], pre_grad)]
    bias_one_list = [jnp.sum(pre_grad.astype(jnp.float32), axis=(0, 1))]
    input_list = [
        (upstream_one.astype(jnp.float32) + board_conv(pre_grad, flipped(w_first[owned]))).astype(
            jnp.bfloat16
        )
    ]
    input_grad = jnp.stack(input_list)
    grad_one = jnp.stack(grad_one_list)
    grad_two = jnp.stack(grad_two_list)
    bias_one = jnp.stack(bias_one_list)
    bias_two = jnp.stack(bias_two_list)
    back_out, back_in = (
        lax.all_to_all(from_local(result), "member", split_axis=0, concat_axis=0, tiled=True),
        lax.all_to_all(from_local(input_grad), "member", split_axis=0, concat_axis=0, tiled=True),
    )
    totals = lax.psum((grad_one, grad_two, bias_one, bias_two), "rep")
    return (gather_rows(back_out), gather_rows(back_in), totals[0], totals[1], totals[2], totals[3])


SLOTS = 8
SIDE = BOARD + 2
CELLS = BOARD * BOARD
ROWS = CELLS * SLOTS
LINE = BOARD * SLOTS
PLACES = SIDE * SIDE * SLOTS
TAIL = 64
MESH_ID = pl.DeviceIdType.MESH

ORDER = (
    ["A0", "A1", "B0", "A2", "A4", "A3", "A6", "A7", "A5"]
    + ["B2", "B3", "B6", "B7", "B4", "B5", "B1"]
    + ["C0", "C1", "C2", "C3", "C4", "C5", "C6", "C7"]
)
AT = {name: index for index, name in enumerate(ORDER)}


def inner(line):
    return ((line + 1) * SIDE + 1) * SLOTS


def wide(lhs, rhs):
    return lax.dot_general(lhs, rhs, (((1,), (1,)), ((), ())), preferred_element_type=jnp.float32)


def league_kernel(
    table, acts_in, cot_in, w1_in, w2_in, b1_in, b2_in,
    out_ref, back_ref, whole,
    acts_pair, cot_pair, pair, acts, cot, w1, w2, bs, xb, gb, hb, pb, slope, mix, res_out, res_back,
    even, odd, paired, chips, diag, cross, total, split, outside, inside,
    load_sems, w_send, w_recv, g_send, g_recv, z_send, z_recv,
):
    f32, bf16 = jnp.float32, jnp.bfloat16
    channels = w1.shape[-1]
    taps = 9 * channels
    block = taps // 4
    rows_g = taps + TAIL
    half_g = rows_g // 2
    quarter = rows_g // 4
    me = lax.axis_index("member")
    rep = lax.axis_index("rep")
    odd_plane = rep % 2
    inner_plane = ((rep + 1) // 2) % 2 == 1
    near = {"core": me ^ 1, "x": me ^ 2, "y": me ^ 4}

    loads = [
        pltpu.make_async_copy(src, dst, load_sems.at[at])
        for at, (src, dst) in enumerate(
            (
                (w1_in.at[0], w1.at[0]), (w2_in.at[0], w2.at[0]),
                (b1_in, bs.at[0, pl.ds(0, 1), :]), (b2_in, bs.at[0, pl.ds(1, 1), :]),
                (acts_in, acts_pair), (cot_in, cot_pair),
            )
        )
    ]
    for load in loads:
        load.start()

    barrier = pltpu.get_barrier_semaphore()
    for peer in near.values():
        pl.semaphore_signal(barrier, inc=1, device_id={"member": peer}, device_id_type=MESH_ID)
    for far in (1, 3):
        pl.semaphore_signal(barrier, inc=1, device_id={"rep": rep ^ far}, device_id_type=MESH_ID)
    pl.semaphore_wait(barrier, 5)

    def remote(src, dst, sends, recvs, at, peer):
        return pltpu.make_async_remote_copy(
            src_ref=src, dst_ref=dst, send_sem=sends.at[at], recv_sem=recvs.at[at],
            device_id=peer, device_id_type=MESH_ID,
        )

    def member(name):
        return {"member": near[name]}

    def rows_of(at, blocks=1):
        return pl.ds(pl.multiple_of(at * block, block), blocks * block)

    extra, skipped = 1 + 2 * odd_plane, 3 - 2 * odd_plane
    lead, other = 2 * odd_plane, 2 - 2 * odd_plane
    plane = {"rep": rep ^ 1}

    def give(kind, at, arriving=False):
        buffer = (w1, w2)[kind]
        own = (w1_in, w2_in)[kind].at[0]
        if at in (0, 12, 13, 14):
            src, dst = {0: (own, 1), 12: (buffer.at[2], 3), 13: (buffer.at[4], 5), 14: (buffer.at[6], 7)}[at]
            ends = (src, buffer.at[dst], member("core"))
        elif at < 7:
            rows = rows_of((extra, lead, other)[(at - 1) % 3])
            to = 2 if at < 4 else 4
            ends = (own.at[rows, :], buffer.at[to, rows, :], member("x" if at < 4 else "y"))
        elif at < 9:
            to = 2 * (at - 6)
            target = buffer.at[to, rows_of(skipped if arriving else extra), :]
            ends = (buffer.at[to, rows_of(extra), :], target, plane)
        elif at == 9:
            ends = (buffer.at[2, rows_of(lead), :], buffer.at[6, rows_of(lead), :], member("y"))
        elif at == 10:
            ends = (buffer.at[4, rows_of(extra), :], buffer.at[6, rows_of(extra), :], member("x"))
        else:
            target = buffer.at[6, rows_of(other if arriving else lead, 2), :]
            ends = (buffer.at[6, rows_of(lead, 2), :], target, plane)
        return remote(ends[0], ends[1], w_send, w_recv, kind * 16 + at, ends[2])

    def give_bias(at):
        src, dst, peer = (
            (0, 1, "core"), (0, 2, "x"), (0, 4, "y"), (2, 3, "core"), (4, 5, "core"), (2, 6, "y"), (6, 7, "core")
        )[at]
        return remote(bs.at[src], bs.at[dst], w_send, w_recv, 32 + at, member(peer))

    def send_weights(kind, ats):
        for at in ats:
            give(kind, at).start()

    def have_weights(kind, ats):
        for at in ats:
            give(kind, at, True).wait_recv()

    def send_bias(*ats):
        for at in ats:
            give_bias(at).start()

    def have_bias(*ats):
        for at in ats:
            give_bias(at).wait_recv()

    def grad_copy(j, at):
        if at < 4:
            ends = (odd.at[j, at], paired.at[j, at], "core")
        elif at < 6:
            rows = pl.ds((at - 4) * half_g, half_g)
            ends = (chips.at[j, 3, rows, :], diag.at[j, at - 4], "xy"[at - 4])
        else:
            p, c = (at - 6) // 4, (at - 6) % 4
            rows = pl.ds(c * quarter, quarter)
            ends = (chips.at[j, p + 1, rows, :], cross.at[j, p, rows, :], "xy"[p])
        return remote(ends[0], ends[1], g_send, g_recv, j * 16 + at, member(ends[2]))

    def rep_copy(j, stage, c):
        src, dst, far = (
            (split.at[j, c], outside.at[j, c], 1),
            (split.at[j, c], inside.at[j, c], 3),
            (whole.at[j, c], whole.at[j, c], 1),
        )[stage]
        return remote(src, dst, z_send, z_recv, (j * 3 + stage) * 4 + c, {"rep": rep ^ far})

    def send_pair(j, p):
        grad_copy(j, p).start()

    def send_diag(j):
        grad_copy(j, 3).wait_recv()
        chips[j, 3] = (even[j, 3] + paired[j, 3].astype(f32)).astype(bf16)
        grad_copy(j, 4).start()
        grad_copy(j, 5).start()

    def send_free(j, p):
        grad_copy(j, p).wait_recv()
        rows = slice(0, half_g) if p == 1 else slice(half_g, rows_g)
        chips[j, p, rows] = (even[j, p, rows] + paired[j, p, rows].astype(f32)).astype(bf16)
        for c in ((0, 1) if p == 1 else (2, 3)):
            grad_copy(j, 6 + 4 * (p - 1) + c).start()

    def send_rest(j, p):
        grad_copy(j, 6 - p).wait_recv()
        rows = slice(half_g, rows_g) if p == 1 else slice(0, half_g)
        value = even[j, p, rows] + paired[j, p, rows].astype(f32) + diag[j, 2 - p].astype(f32)
        chips[j, p, rows] = value.astype(bf16)
        for c in ((2, 3) if p == 1 else (0, 1)):
            grad_copy(j, 6 + 4 * (p - 1) + c).start()

    def have_own(j):
        grad_copy(j, 0).wait_recv()

    def add_up(j, *cs):
        for c in cs:
            rows = slice(c * quarter, (c + 1) * quarter)
            grad_copy(j, 6 + c).wait_recv()
            grad_copy(j, 10 + c).wait_recv()
            value = even[j, 0, rows] + paired[j, 0, rows].astype(f32)
            total[j, c] = value + cross[j, 0, rows].astype(f32) + cross[j, 1, rows].astype(f32)

            @pl.when(jnp.logical_not(inner_plane))
            def _():
                split[j, c] = total[j, c].astype(bf16)
                rep_copy(j, 0, c).start()

    def middle(j, *cs):
        @pl.when(inner_plane)
        def _():
            for c in cs:
                rep_copy(j, 0, c).wait_recv()
                split[j, c] = (total[j, c] + outside[j, c].astype(f32)).astype(bf16)
                rep_copy(j, 1, c).start()

    def ending(j, *cs):
        @pl.when(inner_plane)
        def _():
            for c in cs:
                rep_copy(j, 1, c).wait_recv()
                whole[j, c] = (split[j, c].astype(f32) + inside[j, c].astype(f32)).astype(bf16)
                rep_copy(j, 2, c).start()

    def settle():
        @pl.when(jnp.logical_not(inner_plane))
        def _():
            for j in range(2):
                for c in range(4):
                    rep_copy(j, 2, c).wait_recv()
                    rep_copy(j, 0, c).wait_send()

        @pl.when(inner_plane)
        def _():
            for j in range(2):
                for c in range(4):
                    rep_copy(j, 1, c).wait_send()
                    rep_copy(j, 2, c).wait_send()

    send_weights(0, (1, 4, 2, 5, 3, 6, 0))

    for ref in (xb, gb, hb, pb):
        ref[...] = jnp.zeros_like(ref)
    for load in loads:
        load.wait()

    def apart(state, carry):
        for at, (src, dst) in enumerate(((acts_pair, acts), (cot_pair, cot))):
            pair[at] = src[state].astype(f32)
            for side in range(2):
                dst[state * 2 + side] = pair[at, pl.ds(side, CELLS, stride=2), :].astype(bf16)
        return carry

    lax.fori_loop(0, acts_pair.shape[0], apart, 0)

    def patch(board, q):
        columns = []
        for tap in range(9):
            down, right = tap // 3, tap % 3
            lines = []
            for line in range(BOARD):
                start = ((line + down) * SIDE + right) * SLOTS
                lines.append(board[q, start : start + LINE, :])
            columns.append(jnp.concatenate(lines, axis=0))
        return jnp.concatenate(columns, axis=1)

    def put(board, q, value):
        for line in range(BOARD):
            board[q, inner(line) : inner(line) + LINE, :] = value[line * LINE : (line + 1) * LINE].astype(bf16)

    def centre(board, q):
        return jnp.concatenate(
            [board[q, inner(line) : inner(line) + LINE, :] for line in range(BOARD)], axis=0
        ).astype(f32)

    def flipped_wide(weight, q):
        return jnp.concatenate(
            [weight[q, (8 - tap) * channels : (9 - tap) * channels, :] for tap in range(9)], axis=1
        )

    def gather(src, board, q):
        for slot in range(SLOTS):
            row = table[q * SLOTS + slot]
            value = src[jnp.maximum(row, 0)].astype(f32)
            mix[pl.ds(slot, CELLS, stride=SLOTS), :] = jnp.where(row >= 0, value, 0.0)
        put(board, q, mix[...])

    def spread(ref, q, value):
        mix[...] = value
        for slot in range(SLOTS):
            ref[q * SLOTS + slot] = mix[pl.ds(slot, CELLS, stride=SLOTS), :].astype(bf16)

    def keep_grad(j, q, grad, patches):
        turned = jnp.dot(grad.T.astype(bf16), patches, preferred_element_type=f32)
        bias = jnp.broadcast_to(jnp.sum(grad, axis=0, keepdims=True), (TAIL, channels))
        pair = q // 2

        def write(ref, kind):
            for tap in range(9):
                ref[j, pair, tap * channels : (tap + 1) * channels, :] = turned[
                    :, tap * channels : (tap + 1) * channels
                ].astype(kind)
            ref[j, pair, taps:, :] = bias.astype(kind)

        @pl.when(q % 2 == 0)
        def _():
            write(even, f32)

        @pl.when(q % 2 == 1)
        def _():
            write(odd, bf16)

    def phase_a(q):
        gather(acts, xb, q)
        gather(cot, gb, q)
        pre = jnp.dot(patch(xb, q), w1[q], preferred_element_type=f32) + bs[q, 0:1]
        gate = 0.5 * jnp.tanh(0.5 * pre) + 0.5
        slope[q] = gate * (1.0 + pre * (1.0 - gate))
        put(hb, q, pre * gate)
        keep_grad(1, q, centre(gb, q), patch(hb, q))

    def phase_b(q):
        pre_grad = wide(patch(gb, q), flipped_wide(w2, q)) * slope[q]
        put(pb, q, pre_grad)
        keep_grad(0, q, pre_grad.astype(bf16).astype(f32), patch(xb, q))

    def phase_c(q):
        spread(
            res_out, q,
            jnp.dot(patch(hb, q), w2[q], preferred_element_type=f32) + bs[q, 1:2] + centre(xb, q),
        )
        spread(res_back, q, wide(patch(pb, q), flipped_wide(w1, q)) + centre(gb, q))

    before = {name: [] for name in ORDER}

    def on(name, action, *args):
        before[name].append(functools.partial(action, *args))

    send_bias(0, 1, 2)
    on("A1", have_weights, 0, (0,))
    on("A1", have_bias, 0)
    on("B0", have_weights, 0, (1, 2, 4))
    on("B0", send_weights, 0, (9, 10, 7, 8))
    on("B0", send_weights, 1, (1, 4, 2, 5, 3, 6, 0))
    on("A2", have_weights, 0, (3, 7, 5, 6, 8))
    on("A2", send_weights, 0, (12, 13))
    on("A2", have_bias, 1, 2)
    on("A2", send_bias, 3, 4, 5)
    on("A4", have_weights, 0, (9, 10))
    on("A4", send_weights, 0, (11,))
    on("A3", have_weights, 0, (12,))
    on("A3", have_bias, 3)
    on("A6", have_weights, 0, (11,))
    on("A6", send_weights, 0, (14,))
    on("A6", have_bias, 5)
    on("A6", send_bias, 6)
    on("A6", have_weights, 1, (1, 2, 4))
    on("A6", send_weights, 1, (9, 10, 7, 8))
    on("A7", have_weights, 0, (14,))
    on("A7", have_bias, 6)
    on("A5", have_weights, 0, (13,))
    on("A5", have_bias, 4)
    on("A5", have_weights, 1, (9, 10))
    on("A5", send_weights, 1, (11,))
    on("A5", have_weights, 1, (3, 7, 5, 6, 8))
    on("A5", send_weights, 1, (12, 13))
    on("B3", have_weights, 1, (12,))
    on("B6", have_weights, 1, (11,))
    on("B6", send_weights, 1, (14,))
    on("B7", have_weights, 1, (14,))
    on("B5", have_weights, 1, (13,))
    on("B1", have_weights, 1, (0,))

    for j, phase in ((1, "A"), (0, "B")):
        for p in range(4):
            on(ORDER[AT[phase + str(2 * p + 1)] + 1], send_pair, j, p)

    on("B2", send_diag, 1)
    on("B6", send_free, 1, 1)
    on("B6", send_free, 1, 2)
    on("B7", send_rest, 1, 1)
    on("B7", send_rest, 1, 2)
    on("B5", send_diag, 0)
    on("C0", have_own, 1)
    on("C0", add_up, 1, 0, 2)
    on("C1", send_free, 0, 1)
    on("C1", send_free, 0, 2)
    on("C1", add_up, 1, 1, 3)
    on("C2", middle, 1, 0, 2)
    on("C3", send_rest, 0, 1)
    on("C3", send_rest, 0, 2)
    on("C3", middle, 1, 1, 3)
    on("C4", ending, 1, 0, 2)
    on("C5", ending, 1, 1, 3)

    phases = {"A": phase_a, "B": phase_b, "C": phase_c}

    def step(at, carry):
        q = jnp.int32(0)
        kind = jnp.int32(0)
        for index, name in enumerate(ORDER):
            q = jnp.where(at == index, int(name[1]), q)
            kind = jnp.where(at == index, "ABC".index(name[0]), kind)
            if before[name]:

                @pl.when(at == index)
                def _(name=name):
                    for action in before[name]:
                        action()

        for index, name in enumerate("ABC"):

            @pl.when(kind == index)
            def _(name=name):
                phases[name](q)

        return carry

    lax.fori_loop(0, len(ORDER), step, 0)


    def together(state, carry):
        for at, (src, dst) in enumerate(((res_out, out_ref), (res_back, back_ref))):
            for side in range(2):
                row = table[8 * SLOTS + state * 2 + side]
                pair[at, pl.ds(side, CELLS, stride=2), :] = src[row].astype(f32)
            dst[state] = pair[at].astype(bf16)
        return carry

    lax.fori_loop(0, out_ref.shape[0], together, 0)
    have_own(0)
    add_up(0, 0, 2)
    middle(0, 0, 2)
    add_up(0, 1, 3)
    ending(0, 0, 2)
    middle(0, 1, 3)
    ending(0, 1, 3)
    settle()

    for at in range(15):
        give(0, at).wait_send()
        give(1, at).wait_send()
    for at in range(7):
        give_bias(at).wait_send()
    for j in range(2):
        for at in range(14):
            grad_copy(j, at).wait_send()


def last_kernel(out_in, back_in, whole, out_ref, back_ref, grad_one, grad_two, bias_one, bias_two, sems):
    channels = whole.shape[-1]
    moves = [
        pltpu.make_async_copy(src, dst, sems.at[at])
        for at, (src, dst) in enumerate(((out_in, out_ref), (back_in, back_ref)))
    ]
    for move in moves:
        move.start()
    chunks, quarter = whole.shape[1:3]
    for j, (grad, bias) in enumerate(((grad_one, bias_one), (grad_two, bias_two))):
        stacked = jnp.concatenate([whole[j, at] for at in range(chunks)], axis=0).astype(jnp.float32)
        for tap in range(9):
            rows = slice(tap * channels, (tap + 1) * channels)
            grad[0, rows, :] = stacked[rows].T
        bias[...] = whole[j, chunks - 1, quarter - TAIL : quarter - TAIL + 8].astype(jnp.float32)[:1]
    for move in moves:
        move.wait()


def at_home(acts, cotangent, routes, w_first, w_second, b_first, b_second):
    owners = lax.axis_size("member")
    channels = acts.shape[-1]
    taps = 9 * channels
    rows_g = taps + TAIL
    f32, bf16 = jnp.float32, jnp.bfloat16
    me = lax.axis_index("member")
    ids = routes.reshape(-1)
    count = ids.shape[0]
    order = jnp.arange(count, dtype=jnp.int32)
    place = jnp.sum(((order[:, None] > order[None, :]) & (ids[:, None] == ids[None, :])).astype(jnp.int32), axis=1)
    position = (ids ^ me) * SLOTS + place
    hit = position[None, :] == jnp.arange(owners * SLOTS, dtype=jnp.int32)[:, None]
    rows = jnp.sum(jnp.where(hit, order[None, :] + 1, 0), axis=1) - 1
    table = jnp.concatenate([rows, position])
    def paired(values):
        return jnp.swapaxes(values, 1, 2).reshape(values.shape[0], 2 * values.shape[2], channels)

    x, g = paired(acts), paired(cotangent)
    anywhere = pl.BlockSpec(memory_space=pl.ANY)
    vmem = pl.BlockSpec(memory_space=pltpu.VMEM)
    shape = jax.ShapeDtypeStruct
    board = pltpu.VMEM((owners, PLACES, channels), bf16)
    weight = pltpu.VMEM((owners, taps, channels), bf16)
    results = pltpu.VMEM((owners * SLOTS, CELLS, channels), bf16)
    sems = pltpu.SemaphoreType.DMA
    made = pl.pallas_call(
        league_kernel,
        out_shape=(
            shape(x.shape, bf16),
            shape(x.shape, bf16),
            shape((2, 4, rows_g // 4, channels), bf16),
        ),
        in_specs=[pl.BlockSpec(memory_space=pltpu.SMEM)] + [anywhere] * 6,
        out_specs=(vmem,) * 3,
        scratch_shapes=[
            pltpu.VMEM(x.shape, bf16),
            pltpu.VMEM(x.shape, bf16),
            pltpu.VMEM((2, 2 * CELLS, channels), f32),
            pltpu.VMEM((count, CELLS, channels), bf16),
            pltpu.VMEM((count, CELLS, channels), bf16),
            weight,
            weight,
            pltpu.VMEM((owners, 8, channels), f32),
            board,
            board,
            board,
            board,
            pltpu.VMEM((owners, ROWS, channels), f32),
            pltpu.VMEM((ROWS, channels), f32),
            results,
            results,
            pltpu.VMEM((2, 4, rows_g, channels), f32),
            pltpu.VMEM((2, 4, rows_g, channels), bf16),
            pltpu.VMEM((2, 4, rows_g, channels), bf16),
            pltpu.VMEM((2, 4, rows_g, channels), bf16),
            pltpu.VMEM((2, 2, rows_g // 2, channels), bf16),
            pltpu.VMEM((2, 2, rows_g, channels), bf16),
            pltpu.VMEM((2, 4, rows_g // 4, channels), f32),
            pltpu.VMEM((2, 4, rows_g // 4, channels), bf16),
            pltpu.VMEM((2, 4, rows_g // 4, channels), bf16),
            pltpu.VMEM((2, 4, rows_g // 4, channels), bf16),
            sems((6,)),
            sems((40,)),
            sems((40,)),
            sems((32,)),
            sems((32,)),
            sems((24,)),
            sems((24,)),
        ],
        compiler_params=pltpu.CompilerParams(
            collective_id=0, has_side_effects=True, vmem_limit_bytes=60 * 1024 * 1024
        ),
        cost_estimate=pl.CostEstimate(
            flops=12 * owners * ROWS * taps * channels, bytes_accessed=9000000, transcendentals=owners * ROWS * channels
        ),
        name="league",
    )(table, x, g, w_first, w_second, b_first, b_second)
    done = pl.pallas_call(
        last_kernel,
        out_shape=(
            shape(x.shape, bf16),
            shape(x.shape, bf16),
            shape((1, taps, channels), f32),
            shape((1, taps, channels), f32),
            shape((1, channels), f32),
            shape((1, channels), f32),
        ),
        in_specs=[anywhere] * 2 + [vmem],
        out_specs=(anywhere,) * 2 + (vmem,) * 4,
        scratch_shapes=[sems((2,))],
        compiler_params=pltpu.CompilerParams(vmem_limit_bytes=60 * 1024 * 1024),
        cost_estimate=pl.CostEstimate(flops=0, bytes_accessed=5000000, transcendentals=0),
        name="last",
    )(*made)

    def unpaired(values):
        return jnp.swapaxes(values.reshape(acts.shape[0], acts.shape[2], 2, channels), 1, 2)

    return (unpaired(done[0]), unpaired(done[1])) + tuple(done[2:])


def solution(mesh):
    placed = (
        P(("rep", "member"), None, None, None),
        P(("rep", "member"), None, None, None),
        P(("rep", "member"), None),
        P("member", None, None),
        P("member", None, None),
        P("member", None),
        P("member", None),
    )
    return jax.shard_map(
        at_home if mesh.shape["member"] == 8 and mesh.shape["rep"] == 4 else shards,
        mesh=mesh,
        in_specs=placed,
        out_specs=(
            P(("rep", "member"), None, None, None),
            P(("rep", "member"), None, None, None),
            P("member", None, None),
            P("member", None, None),
            P("member", None),
            P("member", None),
        ),
        check_vma=False,
    )
```

```python
import functools

import jax
import jax.numpy as jnp
from jax import lax
from jax.experimental import pallas as pl
from jax.experimental.pallas import tpu as pltpu
from jax.sharding import PartitionSpec as P

BOARD = 10


def flipped(weight):
    channels = weight.shape[-1]
    stacked = weight.reshape(weight.shape[:-2] + (9, channels, channels))
    reversed_taps = jnp.flip(stacked, axis=-3)
    return jnp.swapaxes(reversed_taps, -1, -2).reshape(weight.shape)


def silu_slope(pre_act):
    sigmoid_vals = jax.nn.sigmoid(pre_act)
    return sigmoid_vals * (1.0 + pre_act * (1.0 - sigmoid_vals))


def board_conv(values, weight):
    count = values.shape[0]
    channels = values.shape[-1]
    side = BOARD
    boards = values.reshape(count, side, side, channels)
    kernel = weight.reshape(3, 3, channels, channels)
    result = lax.conv_general_dilated(
        boards,
        kernel,
        (1, 1),
        ((1, 1), (1, 1)),
        dimension_numbers=("NHWC", "HWIO", "NHWC"),
        preferred_element_type=jnp.float32,
    )
    return result.reshape(count, side * side, channels)


def weight_conv(values, grads):
    count = values.shape[0]
    channels = values.shape[-1]
    side = BOARD
    boards = values.reshape(count, side, side, channels)
    grad_boards = grads.reshape(count, side, side, channels)
    result = lax.conv_general_dilated(
        boards,
        grad_boards,
        (1, 1),
        ((1, 1), (1, 1)),
        dimension_numbers=("CHWN", "IHWO", "NHWC"),
        preferred_element_type=jnp.float32,
    )
    return jnp.transpose(result, (1, 2, 0, 3)).reshape(9 * channels, channels)


def shards(acts, cotangent, routes, w_first, w_second, b_first, b_second):
    per_owner = w_first.shape[0]
    owners = lax.axis_size("member")
    members_all = owners * per_owner
    capacity = max(2, 4 * routes.shape[0] // members_all)
    channels = acts.shape[-1]
    cell_count = acts.shape[-2]
    member_ids = routes.reshape(-1)
    onehot = (member_ids[:, None] == jnp.arange(members_all, dtype=jnp.int32)[None, :]).astype(
        jnp.int32
    )
    order = jnp.arange(member_ids.shape[0], dtype=jnp.int32)
    earlier = jnp.sum((order[:, None] > order[None, :])[:, :, None] * onehot[None], axis=1)
    slot_index = jnp.sum(earlier * onehot, axis=1)
    target = member_ids * capacity + slot_index
    dispatch = (
        jnp.arange(members_all * capacity, dtype=jnp.int32)[:, None] == target[None, :]
    ).astype(jnp.bfloat16)

    def scatter_rows(values):
        flattened = values.reshape(-1, cell_count * channels)
        placed = jnp.dot(dispatch, flattened, preferred_element_type=jnp.float32).astype(
            jnp.bfloat16
        )
        return placed.reshape(members_all, capacity, cell_count, channels)

    def gather_rows(values):
        flattened = values.reshape(members_all * capacity, cell_count * channels)
        picked = jnp.dot(dispatch.T, flattened, preferred_element_type=jnp.float32).astype(
            jnp.bfloat16
        )
        return picked.reshape(acts.shape)

    def to_local(received):
        grouped = received.reshape(owners, per_owner, capacity, cell_count, channels)
        return jnp.swapaxes(grouped, 0, 1).reshape(
            per_owner, owners * capacity, cell_count, channels
        )

    def from_local(values):
        grouped = values.reshape(per_owner, owners, capacity, cell_count, channels)
        return jnp.swapaxes(grouped, 0, 1).reshape(members_all, capacity, cell_count, channels)

    send_acts = scatter_rows(acts)
    send_grads = scatter_rows(cotangent)
    recv_acts, recv_grads = (
        lax.all_to_all(send_acts, "member", split_axis=0, concat_axis=0, tiled=True),
        lax.all_to_all(send_grads, "member", split_axis=0, concat_axis=0, tiled=True),
    )
    inputs = to_local(recv_acts)
    upstream = to_local(recv_grads)
    owned = 0
    pre_one = board_conv(inputs[owned], w_first[owned]) + b_first[owned][None, None, :]
    hidden_one = jax.nn.silu(pre_one).astype(jnp.bfloat16)
    result_one = (
        inputs[owned].astype(jnp.float32)
        + board_conv(hidden_one, w_second[owned])
        + b_second[owned][None, None, :]
    ).astype(jnp.bfloat16)
    pre_list = [pre_one]
    hidden_list = [hidden_one]
    result_list = [result_one]
    result = jnp.stack(result_list)
    owned = 0
    upstream_one = upstream[owned]
    grad_two_list = [weight_conv(hidden_list[owned], upstream_one)]
    bias_two_list = [jnp.sum(upstream_one.astype(jnp.float32), axis=(0, 1))]
    hidden_grad = board_conv(upstream_one, flipped(w_second[owned]))
    pre_grad = (hidden_grad * silu_slope(pre_list[owned])).astype(jnp.bfloat16)
    grad_one_list = [weight_conv(inputs[owned], pre_grad)]
    bias_one_list = [jnp.sum(pre_grad.astype(jnp.float32), axis=(0, 1))]
    input_list = [
        (upstream_one.astype(jnp.float32) + board_conv(pre_grad, flipped(w_first[owned]))).astype(
            jnp.bfloat16
        )
    ]
    input_grad = jnp.stack(input_list)
    grad_one = jnp.stack(grad_one_list)
    grad_two = jnp.stack(grad_two_list)
    bias_one = jnp.stack(bias_one_list)
    bias_two = jnp.stack(bias_two_list)
    back_out, back_in = (
        lax.all_to_all(from_local(result), "member", split_axis=0, concat_axis=0, tiled=True),
        lax.all_to_all(from_local(input_grad), "member", split_axis=0, concat_axis=0, tiled=True),
    )
    totals = lax.psum((grad_one, grad_two, bias_one, bias_two), "rep")
    return (gather_rows(back_out), gather_rows(back_in), totals[0], totals[1], totals[2], totals[3])


SLOTS = 8
SIDE = BOARD + 2
CELLS = BOARD * BOARD
ROWS = CELLS * SLOTS
LINE = BOARD * SLOTS
PLACES = SIDE * SIDE * SLOTS
TAIL = 64
MESH_ID = pl.DeviceIdType.MESH

ORDER = (
    ["A0", "A1", "B0", "B1", "C0", "D0", "C1", "D1", "A6", "A7", "A2", "A3", "A4", "A5"]
    + ["B2", "B3", "B6", "B7", "B4", "B5"]
    + ["C2", "D2", "C3", "D3", "C4", "D4", "C5", "D5", "C6", "D6", "C7", "D7"]
)
AT = {name: index for index, name in enumerate(ORDER)}


def inner(line):
    return ((line + 1) * SIDE + 1) * SLOTS


def wide(lhs, rhs):
    return lax.dot_general(lhs, rhs, (((1,), (1,)), ((), ())), preferred_element_type=jnp.float32)


def league_kernel(
    table, acts_in, cot_in, w1_in, w2_in, b1_in, b2_in,
    out_ref, back_ref, whole,
    acts_pair, cot_pair, pair, acts, cot, w1, w2, bs, xb, gb, hb, pb, slope, mix, res_out, res_back,
    even, odd, paired, chips, diag, cross, total, split, outside, inside,
    load_sems, w_send, w_recv, g_send, g_recv, z_send, z_recv,
):
    f32, bf16 = jnp.float32, jnp.bfloat16
    channels = w1.shape[-1]
    taps = 9 * channels
    half_w = taps // 2
    rows_g = taps + TAIL
    half_g = rows_g // 2
    quarter = rows_g // 4
    me = lax.axis_index("member")
    rep = lax.axis_index("rep")
    inner_plane = ((rep + 1) // 2) % 2 == 1
    near = {"core": me ^ 1, "x": me ^ 2, "y": me ^ 4}

    loads = [
        pltpu.make_async_copy(src, dst, load_sems.at[at])
        for at, (src, dst) in enumerate(
            (
                (w1_in.at[0], w1.at[0]), (w2_in.at[0], w2.at[0]),
                (b1_in, bs.at[0, pl.ds(0, 1), :]), (b2_in, bs.at[0, pl.ds(1, 1), :]),
                (acts_in, acts_pair), (cot_in, cot_pair),
            )
        )
    ]
    for load in loads:
        load.start()

    barrier = pltpu.get_barrier_semaphore()
    for peer in near.values():
        pl.semaphore_signal(barrier, inc=1, device_id={"member": peer}, device_id_type=MESH_ID)
    for far in (1, 3):
        pl.semaphore_signal(barrier, inc=1, device_id={"rep": rep ^ far}, device_id_type=MESH_ID)
    pl.semaphore_wait(barrier, 5)

    def remote(src, dst, sends, recvs, at, peer):
        return pltpu.make_async_remote_copy(
            src_ref=src, dst_ref=dst, send_sem=sends.at[at], recv_sem=recvs.at[at],
            device_id=peer, device_id_type=MESH_ID,
        )

    def member(name):
        return {"member": near[name]}

    def give(kind, at):
        buffer = (w1, w2)[kind]
        own = (w1_in, w2_in)[kind].at[0]
        if at in (0, 7, 8, 9):
            src, dst = {0: (own, 1), 7: (buffer.at[2], 3), 8: (buffer.at[4], 5), 9: (buffer.at[6], 7)}[at]
            ends = (src, buffer.at[dst], member("core"))
        elif at < 5:
            rows = pl.ds((0, 1, 1, 0)[at - 1] * half_w, half_w)
            to = 2 if at < 3 else 4
            ends = (own.at[rows, :], buffer.at[to, rows, :], member("x" if at < 3 else "y"))
        else:
            source, peer = ((2, "y"), (4, "x"))[at - 5]
            rows = pl.ds((at - 5) * half_w, half_w)
            ends = (buffer.at[source, rows, :], buffer.at[6, rows, :], member(peer))
        return remote(ends[0], ends[1], w_send, w_recv, kind * 16 + at, ends[2])

    def give_bias(at):
        src, dst, peer = (
            (0, 1, "core"), (0, 2, "x"), (0, 4, "y"), (2, 3, "core"), (4, 5, "core"), (2, 6, "y"), (6, 7, "core")
        )[at]
        return remote(bs.at[src], bs.at[dst], w_send, w_recv, 32 + at, member(peer))

    def send_weights(kind, ats):
        for at in ats:
            give(kind, at).start()

    def have_weights(kind, ats):
        for at in ats:
            give(kind, at).wait_recv()

    def send_bias(*ats):
        for at in ats:
            give_bias(at).start()

    def have_bias(*ats):
        for at in ats:
            give_bias(at).wait_recv()

    def grad_copy(j, at):
        if at < 4:
            ends = (odd.at[j, 2 * at + 1], paired.at[j, at], "core")
        elif at < 6:
            rows = pl.ds((at - 4) * half_g, half_g)
            ends = (chips.at[j, 3, rows, :], diag.at[j, at - 4], "xy"[at - 4])
        else:
            p, c = (at - 6) // 4, (at - 6) % 4
            rows = pl.ds(c * quarter, quarter)
            ends = (chips.at[j, p + 1, rows, :], cross.at[j, p, rows, :], "xy"[p])
        return remote(ends[0], ends[1], g_send, g_recv, j * 16 + at, member(ends[2]))

    def rep_copy(j, stage, c):
        src, dst, far = (
            (split.at[j, c], outside.at[j, c], 1),
            (split.at[j, c], inside.at[j, c], 3),
            (whole.at[j, c], whole.at[j, c], 1),
        )[stage]
        return remote(src, dst, z_send, z_recv, (j * 3 + stage) * 4 + c, {"rep": rep ^ far})

    def send_pair(j, p):
        grad_copy(j, p).start()

    def send_diag(j):
        grad_copy(j, 3).wait_recv()
        chips[j, 3] = (even[j, 6] + paired[j, 3].astype(f32)).astype(bf16)
        grad_copy(j, 4).start()
        grad_copy(j, 5).start()

    def send_free(j, p):
        grad_copy(j, p).wait_recv()
        rows = slice(0, half_g) if p == 1 else slice(half_g, rows_g)
        chips[j, p, rows] = (even[j, 2 * p, rows] + paired[j, p, rows].astype(f32)).astype(bf16)
        for c in ((0, 1) if p == 1 else (2, 3)):
            grad_copy(j, 6 + 4 * (p - 1) + c).start()

    def send_rest(j, p):
        grad_copy(j, 6 - p).wait_recv()
        rows = slice(half_g, rows_g) if p == 1 else slice(0, half_g)
        value = even[j, 2 * p, rows] + paired[j, p, rows].astype(f32) + diag[j, 2 - p].astype(f32)
        chips[j, p, rows] = value.astype(bf16)
        for c in ((2, 3) if p == 1 else (0, 1)):
            grad_copy(j, 6 + 4 * (p - 1) + c).start()

    def have_own(j):
        grad_copy(j, 0).wait_recv()

    def add_up(j, *cs):
        for c in cs:
            rows = slice(c * quarter, (c + 1) * quarter)
            grad_copy(j, 6 + c).wait_recv()
            grad_copy(j, 10 + c).wait_recv()
            value = even[j, 0, rows] + paired[j, 0, rows].astype(f32)
            total[j, c] = value + cross[j, 0, rows].astype(f32) + cross[j, 1, rows].astype(f32)

            @pl.when(jnp.logical_not(inner_plane))
            def _():
                split[j, c] = total[j, c].astype(bf16)
                rep_copy(j, 0, c).start()

    def middle(j, *cs):
        @pl.when(inner_plane)
        def _():
            for c in cs:
                rep_copy(j, 0, c).wait_recv()
                split[j, c] = (total[j, c] + outside[j, c].astype(f32)).astype(bf16)
                rep_copy(j, 1, c).start()

    def ending(j, *cs):
        @pl.when(inner_plane)
        def _():
            for c in cs:
                rep_copy(j, 1, c).wait_recv()
                whole[j, c] = (split[j, c].astype(f32) + inside[j, c].astype(f32)).astype(bf16)
                rep_copy(j, 2, c).start()

    def settle():
        @pl.when(jnp.logical_not(inner_plane))
        def _():
            for j in range(2):
                for c in range(4):
                    rep_copy(j, 2, c).wait_recv()
                    rep_copy(j, 0, c).wait_send()

        @pl.when(inner_plane)
        def _():
            for j in range(2):
                for c in range(4):
                    rep_copy(j, 1, c).wait_send()
                    rep_copy(j, 2, c).wait_send()

    send_weights(0, (1, 3, 2, 4, 0))
    send_weights(1, (0,))

    for load in loads:
        load.wait()

    def apart(state, carry):
        for at, (src, dst) in enumerate(((acts_pair, acts), (cot_pair, cot))):
            pair[at] = src[state].astype(f32)
            for side in range(2):
                dst[state * 2 + side] = pair[at, pl.ds(side, CELLS, stride=2), :].astype(bf16)
        return carry

    lax.fori_loop(0, acts_pair.shape[0], apart, 0)

    def patch(board, q):
        columns = []
        for tap in range(9):
            down, right = tap // 3, tap % 3
            lines = []
            for line in range(BOARD):
                start = ((line + down) * SIDE + right) * SLOTS
                lines.append(board[q, start : start + LINE, :])
            columns.append(jnp.concatenate(lines, axis=0))
        return jnp.concatenate(columns, axis=1)

    def put(board, q, value):
        board[q] = jnp.zeros_like(board[q])
        for line in range(BOARD):
            board[q, inner(line) : inner(line) + LINE, :] = value[line * LINE : (line + 1) * LINE].astype(bf16)

    def centre(board, q):
        return jnp.concatenate(
            [board[q, inner(line) : inner(line) + LINE, :] for line in range(BOARD)], axis=0
        ).astype(f32)

    def flipped_wide(weight, q):
        return jnp.concatenate(
            [weight[q, (8 - tap) * channels : (9 - tap) * channels, :] for tap in range(9)], axis=1
        )

    def gather(src, board, q, at):
        for slot in range(SLOTS):
            row = table[q * SLOTS + slot]
            value = src[jnp.maximum(row, 0)].astype(f32)
            mix[at, pl.ds(slot, CELLS, stride=SLOTS), :] = jnp.where(row >= 0, value, 0.0)
        put(board, q, mix[at])

    def spread(ref, q, value):
        mix[0] = value
        for slot in range(SLOTS):
            ref[q * SLOTS + slot] = mix[0, pl.ds(slot, CELLS, stride=SLOTS), :].astype(bf16)

    def keep_grad(j, q, grad, patches):
        turned = jnp.dot(grad.T.astype(bf16), patches, preferred_element_type=f32)
        bias = jnp.broadcast_to(jnp.sum(grad, axis=0, keepdims=True), (TAIL, channels))
        for ref in (even, odd):
            for tap in range(9):
                ref[j, q, tap * channels : (tap + 1) * channels, :] = turned[
                    :, tap * channels : (tap + 1) * channels
                ].astype(ref.dtype)
            ref[j, q, taps:, :] = bias.astype(ref.dtype)

    def phase_a(q):
        gather(acts, xb, q, 0)
        gather(cot, gb, q, 1)
        pre = jnp.dot(patch(xb, q), w1[q], preferred_element_type=f32) + bs[q, 0:1]
        gate = 0.5 * jnp.tanh(0.5 * pre) + 0.5
        slope[q] = gate * (1.0 + pre * (1.0 - gate))
        put(hb, q, pre * gate)
        keep_grad(1, q, centre(gb, q), patch(hb, q))

    def phase_b(q):
        pre_grad = wide(patch(gb, q), flipped_wide(w2, q)) * slope[q]
        put(pb, q, pre_grad)
        keep_grad(0, q, pre_grad.astype(bf16).astype(f32), patch(xb, q))

    def phase_c(q):
        spread(
            res_out, q,
            jnp.dot(patch(hb, q), w2[q], preferred_element_type=f32) + bs[q, 1:2] + centre(xb, q),
        )

    def phase_d(q):
        spread(res_back, q, wide(patch(pb, q), flipped_wide(w1, q)) + centre(gb, q))

    before = {name: [] for name in ORDER}

    def on(name, action, *args):
        before[name].append(functools.partial(action, *args))

    send_bias(0, 1, 2)
    on("A1", have_weights, 0, (0,))
    on("A1", have_bias, 0)
    on("B1", have_weights, 1, (0,))
    on("B1", have_weights, 0, (1, 3))
    on("B1", send_weights, 0, (5, 6))
    on("B1", have_weights, 0, (2, 4))
    on("B1", send_weights, 0, (7, 8))
    on("B1", have_bias, 1, 2)
    on("B1", send_bias, 3, 4, 5)
    on("B1", send_weights, 1, (1, 3, 2, 4))
    on("A6", have_weights, 0, (5, 6))
    on("A6", send_weights, 0, (9,))
    on("A6", have_bias, 5)
    on("A6", send_bias, 6)
    on("A7", have_weights, 0, (9,))
    on("A7", have_bias, 6)
    on("A3", have_weights, 0, (7,))
    on("A3", have_bias, 3)
    on("A5", have_weights, 0, (8,))
    on("A5", have_bias, 4)
    on("A4", have_weights, 1, (1, 3))
    on("A4", send_weights, 1, (5, 6))
    on("A4", have_weights, 1, (2, 4))
    on("A4", send_weights, 1, (7, 8))
    on("B3", have_weights, 1, (7,))
    on("B6", have_weights, 1, (5, 6))
    on("B6", send_weights, 1, (9,))
    on("B7", have_weights, 1, (9,))
    on("B5", have_weights, 1, (8,))

    for j, phase in ((1, "A"), (0, "B")):
        for p in range(4):
            on(ORDER[AT[phase + str(2 * p + 1)] + 1], send_pair, j, p)

    on("A3", send_diag, 1)
    on("A5", send_free, 1, 1)
    on("B3", send_free, 1, 2)
    on("B3", send_rest, 1, 1)
    on("B3", send_rest, 1, 2)
    on("B4", send_free, 0, 1)
    on("B5", send_diag, 0)
    on("D2", send_free, 0, 2)
    on("C2", have_own, 1)
    on("D2", add_up, 1, 0, 2)
    on("C3", add_up, 1, 1, 3)
    on("C5", middle, 1, 0)
    on("C4", send_rest, 0, 1)
    on("C4", send_rest, 0, 2)
    on("D6", middle, 1, 2)
    on("C7", have_own, 0)
    on("C7", add_up, 0, 0, 2)
    on("D7", add_up, 0, 1, 3)
    on("D7", middle, 1, 1)
    on("D7", ending, 1, 0)

    phases = {"A": phase_a, "B": phase_b, "C": phase_c, "D": phase_d}

    def step(at, carry):
        q = jnp.int32(0)
        kind = jnp.int32(0)
        for index, name in enumerate(ORDER):
            q = jnp.where(at == index, int(name[1]), q)
            kind = jnp.where(at == index, "ABCD".index(name[0]), kind)
            if before[name]:

                @pl.when(at == index)
                def _(name=name):
                    for action in before[name]:
                        action()

        for index, name in enumerate("ABCD"):

            @pl.when(kind == index)
            def _(name=name):
                phases[name](q)

        return carry

    lax.fori_loop(0, len(ORDER), step, 0)


    middle(1, 3)
    ending(1, 2)

    def together(state, carry):
        for at, (src, dst) in enumerate(((res_out, out_ref), (res_back, back_ref))):
            for side in range(2):
                row = table[8 * SLOTS + state * 2 + side]
                pair[at, pl.ds(side, CELLS, stride=2), :] = src[row].astype(f32)
            dst[state] = pair[at].astype(bf16)
        return carry

    lax.fori_loop(0, out_ref.shape[0], together, 0)
    middle(0, 0)
    ending(1, 1)
    middle(0, 2)
    ending(1, 3)
    middle(0, 1)
    ending(0, 0)
    middle(0, 3)
    ending(0, 2, 1, 3)
    settle()

    for at in range(10):
        give(0, at).wait_send()
        give(1, at).wait_send()
    for at in range(7):
        give_bias(at).wait_send()
    for j in range(2):
        for at in range(14):
            grad_copy(j, at).wait_send()


def last_kernel(
    out_in, back_in, whole_in, out_ref, back_ref, grad_one, grad_two, bias_one, bias_two, boards, whole, grads, sems
):
    channels = whole.shape[-1]
    chunks, quarter = whole.shape[1:3]

    def move(src, dst, at):
        return pltpu.make_async_copy(src, dst, sems.at[at])

    loads = [move(whole_in, whole, 0), move(out_in, boards.at[0], 1), move(back_in, boards.at[1], 2)]
    stores = [
        move(boards.at[0], out_ref, 3), move(boards.at[1], back_ref, 4),
        move(grads.at[0], grad_one.at[0], 5), move(grads.at[1], grad_two.at[0], 6),
    ]
    for load in loads:
        load.start()
    loads[0].wait()
    for j, bias in enumerate((bias_one, bias_two)):
        stacked = jnp.concatenate([whole[j, at] for at in range(chunks)], axis=0).astype(jnp.float32)
        for tap in range(9):
            rows = slice(tap * channels, (tap + 1) * channels)
            grads[j, rows, :] = stacked[rows].T
        stores[2 + j].start()
        loads[1 + j].wait()
        stores[j].start()
        bias[...] = whole[j, chunks - 1, quarter - TAIL : quarter - TAIL + 8].astype(jnp.float32)[:1]
    for store in stores:
        store.wait()


def at_home(acts, cotangent, routes, w_first, w_second, b_first, b_second):
    owners = lax.axis_size("member")
    channels = acts.shape[-1]
    taps = 9 * channels
    rows_g = taps + TAIL
    f32, bf16 = jnp.float32, jnp.bfloat16
    me = lax.axis_index("member")
    ids = routes.reshape(-1)
    count = ids.shape[0]
    order = jnp.arange(count, dtype=jnp.int32)
    place = jnp.sum(((order[:, None] > order[None, :]) & (ids[:, None] == ids[None, :])).astype(jnp.int32), axis=1)
    position = (ids ^ me) * SLOTS + place
    hit = position[None, :] == jnp.arange(owners * SLOTS, dtype=jnp.int32)[:, None]
    rows = jnp.sum(jnp.where(hit, order[None, :] + 1, 0), axis=1) - 1
    table = jnp.concatenate([rows, position])
    def paired(values):
        return jnp.swapaxes(values, 1, 2).reshape(values.shape[0], 2 * values.shape[2], channels)

    x, g = paired(acts), paired(cotangent)
    anywhere = pl.BlockSpec(memory_space=pl.ANY)
    vmem = pl.BlockSpec(memory_space=pltpu.VMEM)
    shape = jax.ShapeDtypeStruct
    board = pltpu.VMEM((owners, PLACES, channels), bf16)
    weight = pltpu.VMEM((owners, taps, channels), bf16)
    results = pltpu.VMEM((owners * SLOTS, CELLS, channels), bf16)
    sems = pltpu.SemaphoreType.DMA
    made = pl.pallas_call(
        league_kernel,
        out_shape=(
            shape(x.shape, bf16),
            shape(x.shape, bf16),
            shape((2, 4, rows_g // 4, channels), bf16),
        ),
        in_specs=[pl.BlockSpec(memory_space=pltpu.SMEM)] + [anywhere] * 6,
        out_specs=(vmem,) * 3,
        scratch_shapes=[
            pltpu.VMEM(x.shape, bf16),
            pltpu.VMEM(x.shape, bf16),
            pltpu.VMEM((2, 2 * CELLS, channels), f32),
            pltpu.VMEM((count, CELLS, channels), bf16),
            pltpu.VMEM((count, CELLS, channels), bf16),
            weight,
            weight,
            pltpu.VMEM((owners, 8, channels), f32),
            board,
            board,
            board,
            board,
            pltpu.VMEM((owners, ROWS, channels), f32),
            pltpu.VMEM((2, ROWS, channels), f32),
            results,
            results,
            pltpu.VMEM((2, owners, rows_g, channels), f32),
            pltpu.VMEM((2, owners, rows_g, channels), bf16),
            pltpu.VMEM((2, 4, rows_g, channels), bf16),
            pltpu.VMEM((2, 4, rows_g, channels), bf16),
            pltpu.VMEM((2, 2, rows_g // 2, channels), bf16),
            pltpu.VMEM((2, 2, rows_g, channels), bf16),
            pltpu.VMEM((2, 4, rows_g // 4, channels), f32),
            pltpu.VMEM((2, 4, rows_g // 4, channels), bf16),
            pltpu.VMEM((2, 4, rows_g // 4, channels), bf16),
            pltpu.VMEM((2, 4, rows_g // 4, channels), bf16),
            sems((6,)),
            sems((40,)),
            sems((40,)),
            sems((32,)),
            sems((32,)),
            sems((24,)),
            sems((24,)),
        ],
        compiler_params=pltpu.CompilerParams(
            collective_id=0, has_side_effects=True, vmem_limit_bytes=60 * 1024 * 1024
        ),
        cost_estimate=pl.CostEstimate(
            flops=12 * owners * ROWS * taps * channels, bytes_accessed=9000000, transcendentals=owners * ROWS * channels
        ),
        name="league",
    )(table, x, g, w_first, w_second, b_first, b_second)
    done = pl.pallas_call(
        last_kernel,
        out_shape=(
            shape(x.shape, bf16),
            shape(x.shape, bf16),
            shape((1, taps, channels), f32),
            shape((1, taps, channels), f32),
            shape((1, channels), f32),
            shape((1, channels), f32),
        ),
        in_specs=[anywhere] * 3,
        out_specs=(anywhere,) * 4 + (vmem,) * 2,
        scratch_shapes=[
            pltpu.VMEM((2,) + x.shape, bf16),
            pltpu.VMEM((2, 4, rows_g // 4, channels), bf16),
            pltpu.VMEM((2, taps, channels), f32),
            sems((7,)),
        ],
        compiler_params=pltpu.CompilerParams(vmem_limit_bytes=60 * 1024 * 1024),
        cost_estimate=pl.CostEstimate(flops=0, bytes_accessed=5000000, transcendentals=0),
        name="last",
    )(*made)

    def unpaired(values):
        return jnp.swapaxes(values.reshape(acts.shape[0], acts.shape[2], 2, channels), 1, 2)

    return (unpaired(done[0]), unpaired(done[1])) + tuple(done[2:])


def solution(mesh):
    placed = (
        P(("rep", "member"), None, None, None),
        P(("rep", "member"), None, None, None),
        P(("rep", "member"), None),
        P("member", None, None),
        P("member", None, None),
        P("member", None),
        P("member", None),
    )
    return jax.shard_map(
        at_home if mesh.shape["member"] == 8 and mesh.shape["rep"] == 4 else shards,
        mesh=mesh,
        in_specs=placed,
        out_specs=(
            P(("rep", "member"), None, None, None),
            P(("rep", "member"), None, None, None),
            P("member", None, None),
            P("member", None, None),
            P("member", None),
            P("member", None),
        ),
        check_vma=False,
    )
```

```python
import functools

import jax
import jax.numpy as jnp
from jax import lax
from jax.experimental import pallas as pl
from jax.experimental.pallas import tpu as pltpu
from jax.sharding import PartitionSpec as P

BOARD = 10


def flipped(weight):
    channels = weight.shape[-1]
    stacked = weight.reshape(weight.shape[:-2] + (9, channels, channels))
    reversed_taps = jnp.flip(stacked, axis=-3)
    return jnp.swapaxes(reversed_taps, -1, -2).reshape(weight.shape)


def silu_slope(pre_act):
    sigmoid_vals = jax.nn.sigmoid(pre_act)
    return sigmoid_vals * (1.0 + pre_act * (1.0 - sigmoid_vals))


def board_conv(values, weight):
    count = values.shape[0]
    channels = values.shape[-1]
    side = BOARD
    boards = values.reshape(count, side, side, channels)
    kernel = weight.reshape(3, 3, channels, channels)
    result = lax.conv_general_dilated(
        boards,
        kernel,
        (1, 1),
        ((1, 1), (1, 1)),
        dimension_numbers=("NHWC", "HWIO", "NHWC"),
        preferred_element_type=jnp.float32,
    )
    return result.reshape(count, side * side, channels)


def weight_conv(values, grads):
    count = values.shape[0]
    channels = values.shape[-1]
    side = BOARD
    boards = values.reshape(count, side, side, channels)
    grad_boards = grads.reshape(count, side, side, channels)
    result = lax.conv_general_dilated(
        boards,
        grad_boards,
        (1, 1),
        ((1, 1), (1, 1)),
        dimension_numbers=("CHWN", "IHWO", "NHWC"),
        preferred_element_type=jnp.float32,
    )
    return jnp.transpose(result, (1, 2, 0, 3)).reshape(9 * channels, channels)


def shards(acts, cotangent, routes, w_first, w_second, b_first, b_second):
    per_owner = w_first.shape[0]
    owners = lax.axis_size("member")
    members_all = owners * per_owner
    capacity = max(2, 4 * routes.shape[0] // members_all)
    channels = acts.shape[-1]
    cell_count = acts.shape[-2]
    member_ids = routes.reshape(-1)
    onehot = (member_ids[:, None] == jnp.arange(members_all, dtype=jnp.int32)[None, :]).astype(
        jnp.int32
    )
    order = jnp.arange(member_ids.shape[0], dtype=jnp.int32)
    earlier = jnp.sum((order[:, None] > order[None, :])[:, :, None] * onehot[None], axis=1)
    slot_index = jnp.sum(earlier * onehot, axis=1)
    target = member_ids * capacity + slot_index
    dispatch = (
        jnp.arange(members_all * capacity, dtype=jnp.int32)[:, None] == target[None, :]
    ).astype(jnp.bfloat16)

    def scatter_rows(values):
        flattened = values.reshape(-1, cell_count * channels)
        placed = jnp.dot(dispatch, flattened, preferred_element_type=jnp.float32).astype(
            jnp.bfloat16
        )
        return placed.reshape(members_all, capacity, cell_count, channels)

    def gather_rows(values):
        flattened = values.reshape(members_all * capacity, cell_count * channels)
        picked = jnp.dot(dispatch.T, flattened, preferred_element_type=jnp.float32).astype(
            jnp.bfloat16
        )
        return picked.reshape(acts.shape)

    def to_local(received):
        grouped = received.reshape(owners, per_owner, capacity, cell_count, channels)
        return jnp.swapaxes(grouped, 0, 1).reshape(
            per_owner, owners * capacity, cell_count, channels
        )

    def from_local(values):
        grouped = values.reshape(per_owner, owners, capacity, cell_count, channels)
        return jnp.swapaxes(grouped, 0, 1).reshape(members_all, capacity, cell_count, channels)

    send_acts = scatter_rows(acts)
    send_grads = scatter_rows(cotangent)
    recv_acts, recv_grads = (
        lax.all_to_all(send_acts, "member", split_axis=0, concat_axis=0, tiled=True),
        lax.all_to_all(send_grads, "member", split_axis=0, concat_axis=0, tiled=True),
    )
    inputs = to_local(recv_acts)
    upstream = to_local(recv_grads)
    owned = 0
    pre_one = board_conv(inputs[owned], w_first[owned]) + b_first[owned][None, None, :]
    hidden_one = jax.nn.silu(pre_one).astype(jnp.bfloat16)
    result_one = (
        inputs[owned].astype(jnp.float32)
        + board_conv(hidden_one, w_second[owned])
        + b_second[owned][None, None, :]
    ).astype(jnp.bfloat16)
    pre_list = [pre_one]
    hidden_list = [hidden_one]
    result_list = [result_one]
    result = jnp.stack(result_list)
    owned = 0
    upstream_one = upstream[owned]
    grad_two_list = [weight_conv(hidden_list[owned], upstream_one)]
    bias_two_list = [jnp.sum(upstream_one.astype(jnp.float32), axis=(0, 1))]
    hidden_grad = board_conv(upstream_one, flipped(w_second[owned]))
    pre_grad = (hidden_grad * silu_slope(pre_list[owned])).astype(jnp.bfloat16)
    grad_one_list = [weight_conv(inputs[owned], pre_grad)]
    bias_one_list = [jnp.sum(pre_grad.astype(jnp.float32), axis=(0, 1))]
    input_list = [
        (upstream_one.astype(jnp.float32) + board_conv(pre_grad, flipped(w_first[owned]))).astype(
            jnp.bfloat16
        )
    ]
    input_grad = jnp.stack(input_list)
    grad_one = jnp.stack(grad_one_list)
    grad_two = jnp.stack(grad_two_list)
    bias_one = jnp.stack(bias_one_list)
    bias_two = jnp.stack(bias_two_list)
    back_out, back_in = (
        lax.all_to_all(from_local(result), "member", split_axis=0, concat_axis=0, tiled=True),
        lax.all_to_all(from_local(input_grad), "member", split_axis=0, concat_axis=0, tiled=True),
    )
    totals = lax.psum((grad_one, grad_two, bias_one, bias_two), "rep")
    return (gather_rows(back_out), gather_rows(back_in), totals[0], totals[1], totals[2], totals[3])


SLOTS = 8
SIDE = BOARD + 2
CELLS = BOARD * BOARD
ROWS = CELLS * SLOTS
LINE = BOARD * SLOTS
PLACES = SIDE * SIDE * SLOTS
TAIL = 16
CHUNKS = 8
MESH_ID = pl.DeviceIdType.MESH

ORDER = (
    ["A0", "A1", "B0", "B1", "C0", "D0", "C1", "D1", "A6", "A7", "A2", "A3", "A4", "A5"]
    + ["B2", "B3", "B6", "B7", "B4", "B5"]
    + ["C2", "D2", "C3", "D3", "C4", "D4", "C5", "D5", "C6", "D6", "C7", "D7"]
)
AT = {name: index for index, name in enumerate(ORDER)}


def inner(line):
    return ((line + 1) * SIDE + 1) * SLOTS


def wide(lhs, rhs):
    return lax.dot_general(lhs, rhs, (((1,), (1,)), ((), ())), preferred_element_type=jnp.float32)


def league_kernel(
    routes, acts_in, cot_in, w1_in, w2_in, b1_in, b2_in,
    out_hbm, back_hbm, whole,
    out_ref, back_ref, pair, acts, cot, w1, w2, bs, xb, gb, hb, pb, slope, mix, res_out, res_back,
    even, odd, paired, chips, diag, cross, total, split, outside, inside,
    lookup, table, load_sems, w_send, w_recv, g_send, g_recv, z_send, z_recv,
):
    f32, bf16 = jnp.float32, jnp.bfloat16
    channels = w1.shape[-1]
    taps = 9 * channels
    half_w = taps // 2
    rows_g = taps + TAIL
    piece = taps // CHUNKS
    half_g = taps // 2
    me = lax.axis_index("member")
    rep = lax.axis_index("rep")
    inner_plane = ((rep + 1) // 2) % 2 == 1
    near = {"core": me ^ 1, "x": me ^ 2, "y": me ^ 4}

    loads = [
        pltpu.make_async_copy(src, dst, load_sems.at[at])
        for at, (src, dst) in enumerate(
            (
                (w1_in.at[0], w1.at[0]), (w2_in.at[0], w2.at[0]),
                (b1_in, bs.at[0, pl.ds(0, 1), :]), (b2_in, bs.at[0, pl.ds(1, 1), :]),
                (acts_in, out_ref), (cot_in, back_ref),
            )
        )
    ]
    for load in loads:
        load.start()

    barrier = pltpu.get_barrier_semaphore()
    for peer in near.values():
        pl.semaphore_signal(barrier, inc=1, device_id={"member": peer}, device_id_type=MESH_ID)
    for far in (1, 3):
        pl.semaphore_signal(barrier, inc=1, device_id={"rep": rep ^ far}, device_id_type=MESH_ID)
    pl.semaphore_wait(barrier, 5)

    def remote(src, dst, sends, recvs, at, peer):
        return pltpu.make_async_remote_copy(
            src_ref=src, dst_ref=dst, send_sem=sends.at[at], recv_sem=recvs.at[at],
            device_id=peer, device_id_type=MESH_ID,
        )

    def member(name):
        return {"member": near[name]}

    def give(kind, at):
        buffer = (w1, w2)[kind]
        own = (w1_in, w2_in)[kind].at[0]
        if at in (0, 7, 8, 9):
            src, dst = {0: (own, 1), 7: (buffer.at[2], 3), 8: (buffer.at[4], 5), 9: (buffer.at[6], 7)}[at]
            ends = (src, buffer.at[dst], member("core"))
        elif at < 5:
            rows = pl.ds((0, 1, 1, 0)[at - 1] * half_w, half_w)
            to = 2 if at < 3 else 4
            ends = (own.at[rows, :], buffer.at[to, rows, :], member("x" if at < 3 else "y"))
        else:
            source, peer = ((2, "y"), (4, "x"))[at - 5]
            rows = pl.ds((at - 5) * half_w, half_w)
            ends = (buffer.at[source, rows, :], buffer.at[6, rows, :], member(peer))
        return remote(ends[0], ends[1], w_send, w_recv, kind * 16 + at, ends[2])

    def give_bias(at):
        src, dst, peer = (
            (0, 1, "core"), (0, 2, "x"), (0, 4, "y"), (2, 3, "core"), (4, 5, "core"), (2, 6, "y"), (6, 7, "core")
        )[at]
        return remote(bs.at[src], bs.at[dst], w_send, w_recv, 32 + at, member(peer))

    def send_weights(kind, ats):
        for at in ats:
            give(kind, at).start()

    def have_weights(kind, ats):
        for at in ats:
            give(kind, at).wait_recv()

    def send_bias(*ats):
        for at in ats:
            give_bias(at).start()

    def have_bias(*ats):
        for at in ats:
            give_bias(at).wait_recv()

    def span(c):
        return c * piece, piece + (TAIL if c == CHUNKS - 1 else 0)

    def grad_copy(j, at):
        if at < 4:
            ends = (odd.at[j, 2 * at + 1], paired.at[j, at], "core")
        elif at < 6:
            size = half_g + (at - 4) * TAIL
            source = chips.at[j, 3, pl.ds((at - 4) * half_g, size), :]
            ends = (source, diag.at[j, at - 4, pl.ds(0, size), :], "xy"[at - 4])
        else:
            p, c = (at - 6) // CHUNKS, (at - 6) % CHUNKS
            rows = pl.ds(*span(c))
            ends = (chips.at[j, p + 1, rows, :], cross.at[j, p, rows, :], "xy"[p])
        return remote(ends[0], ends[1], g_send, g_recv, j * 24 + at, member(ends[2]))

    def rep_copy(j, stage, c):
        src, dst, far = ((split, outside, 1), (split, inside, 3), (whole, whole, 1))[stage]
        rows = pl.ds(*span(c))
        at = (j * 3 + stage) * CHUNKS + c
        return remote(src.at[j, rows, :], dst.at[j, rows, :], z_send, z_recv, at, {"rep": rep ^ far})

    def send_pair(j, p):
        grad_copy(j, p).start()

    def send_diag(j):
        grad_copy(j, 3).wait_recv()
        chips[j, 3] = (even[j, 6] + paired[j, 3].astype(f32)).astype(bf16)
        grad_copy(j, 4).start()
        grad_copy(j, 5).start()

    def send_free(j, p):
        grad_copy(j, p).wait_recv()
        rows = slice(0, half_g) if p == 1 else slice(half_g, rows_g)
        chips[j, p, rows] = (even[j, 2 * p, rows] + paired[j, p, rows].astype(f32)).astype(bf16)
        for c in (range(4) if p == 1 else range(4, 8)):
            grad_copy(j, 6 + CHUNKS * (p - 1) + c).start()

    def send_rest(j, p):
        grad_copy(j, 6 - p).wait_recv()
        rows = slice(half_g, rows_g) if p == 1 else slice(0, half_g)
        value = even[j, 2 * p, rows] + paired[j, p, rows].astype(f32) + diag[j, 2 - p, : half_g + (2 - p) * TAIL].astype(f32)
        chips[j, p, rows] = value.astype(bf16)
        for c in (range(4, 8) if p == 1 else range(4)):
            grad_copy(j, 6 + CHUNKS * (p - 1) + c).start()

    def have_own(j):
        grad_copy(j, 0).wait_recv()

    def add_up(j, *cs):
        for c in cs:
            rows = pl.ds(*span(c))
            grad_copy(j, 6 + c).wait_recv()
            grad_copy(j, 6 + CHUNKS + c).wait_recv()
            value = even[j, 0, rows] + paired[j, 0, rows].astype(f32)
            total[j, rows] = value + cross[j, 0, rows].astype(f32) + cross[j, 1, rows].astype(f32)

            @pl.when(jnp.logical_not(inner_plane))
            def _():
                split[j, rows] = total[j, rows].astype(bf16)
                rep_copy(j, 0, c).start()

    def middle(j, *cs):
        @pl.when(inner_plane)
        def _():
            for c in cs:
                rows = pl.ds(*span(c))
                rep_copy(j, 0, c).wait_recv()
                split[j, rows] = (total[j, rows] + outside[j, rows].astype(f32)).astype(bf16)
                rep_copy(j, 1, c).start()

    def ending(j, *cs):
        @pl.when(inner_plane)
        def _():
            for c in cs:
                rows = pl.ds(*span(c))
                rep_copy(j, 1, c).wait_recv()
                whole[j, rows] = (split[j, rows].astype(f32) + inside[j, rows].astype(f32)).astype(bf16)
                rep_copy(j, 2, c).start()

    def settle():
        @pl.when(jnp.logical_not(inner_plane))
        def _():
            for j in range(2):
                for c in range(CHUNKS):
                    rep_copy(j, 2, c).wait_recv()
                    rep_copy(j, 0, c).wait_send()

        @pl.when(inner_plane)
        def _():
            for j in range(2):
                for c in range(CHUNKS):
                    rep_copy(j, 1, c).wait_send()
                    rep_copy(j, 2, c).wait_send()

    send_weights(0, (1, 3, 2, 4, 0))
    send_weights(1, (0,))

    states = acts_in.shape[0]
    count = 2 * states
    lane = lax.broadcasted_iota(jnp.int32, (count, 128), 1)
    line = lax.broadcasted_iota(jnp.int32, (count, 128), 0)
    named = jnp.concatenate([routes[0:1, :], routes[1:2, :], jnp.full((1, 128 - count), -1, jnp.int32)], axis=1)
    across = jnp.broadcast_to(named, (count, 128))
    down = jnp.sum(jnp.where(lane == line, across, 0), axis=1, keepdims=True)
    place = jnp.sum(jnp.where((line > lane) & (across == down), 1, 0), axis=1, keepdims=True)
    position = jnp.bitwise_xor(down, me) * SLOTS + place
    row = (line % states) * 2 + line // states
    rows = jnp.sum(jnp.where(position == lane, row + 1, 0), axis=0, keepdims=True) - 1
    positions = jnp.sum(jnp.where(lane == line + 8 * SLOTS, position, 0), axis=0, keepdims=True)
    lookup[...] = jnp.where(lane[:1] < 8 * SLOTS, rows, positions)
    fill = pltpu.make_async_copy(lookup, table, load_sems.at[6])
    fill.start()
    for load in loads:
        load.wait()

    def apart(state, carry):
        for at, (src, dst) in enumerate(((out_ref, acts), (back_ref, cot))):
            pair[at] = src[state].astype(f32)
            for side in range(2):
                dst[state * 2 + side] = pair[at, pl.ds(side, CELLS, stride=2), :].astype(bf16)
        return carry

    lax.fori_loop(0, out_ref.shape[0], apart, 0)
    fill.wait()

    def patch(board, q):
        columns = []
        for tap in range(9):
            down, right = tap // 3, tap % 3
            lines = []
            for line in range(BOARD):
                start = ((line + down) * SIDE + right) * SLOTS
                lines.append(board[q, start : start + LINE, :])
            columns.append(jnp.concatenate(lines, axis=0))
        return jnp.concatenate(columns, axis=1)

    def put(board, q, value):
        board[q] = jnp.zeros_like(board[q])
        for line in range(BOARD):
            board[q, inner(line) : inner(line) + LINE, :] = value[line * LINE : (line + 1) * LINE].astype(bf16)

    def centre(board, q):
        return jnp.concatenate(
            [board[q, inner(line) : inner(line) + LINE, :] for line in range(BOARD)], axis=0
        ).astype(f32)

    def flipped_wide(weight, q):
        return jnp.concatenate(
            [weight[q, (8 - tap) * channels : (9 - tap) * channels, :] for tap in range(9)], axis=1
        )

    def gather(src, board, q, at):
        for slot in range(SLOTS):
            row = table[0, q * SLOTS + slot]
            value = src[jnp.clip(row, 0, src.shape[0] - 1)].astype(f32)
            mix[at, pl.ds(slot, CELLS, stride=SLOTS), :] = jnp.where(row >= 0, value, 0.0)
        put(board, q, mix[at])

    def spread(ref, q, value):
        mix[0] = value
        for slot in range(SLOTS):
            ref[q * SLOTS + slot] = mix[0, pl.ds(slot, CELLS, stride=SLOTS), :].astype(bf16)

    def keep_grad(j, q, grad, patches):
        turned = jnp.dot(grad.T.astype(bf16), patches, preferred_element_type=f32)
        bias = jnp.broadcast_to(jnp.sum(grad, axis=0, keepdims=True), (TAIL, channels))
        for ref in (even, odd):
            for tap in range(9):
                ref[j, q, tap * channels : (tap + 1) * channels, :] = turned[
                    :, tap * channels : (tap + 1) * channels
                ].astype(ref.dtype)
            ref[j, q, taps:, :] = bias.astype(ref.dtype)

    def phase_a(q):
        gather(acts, xb, q, 0)
        gather(cot, gb, q, 1)
        pre = jnp.dot(patch(xb, q), w1[q], preferred_element_type=f32) + bs[q, 0:1]
        gate = 0.5 * jnp.tanh(0.5 * pre) + 0.5
        slope[q] = gate * (1.0 + pre * (1.0 - gate))
        put(hb, q, pre * gate)
        keep_grad(1, q, centre(gb, q), patch(hb, q))

    def phase_b(q):
        pre_grad = wide(patch(gb, q), flipped_wide(w2, q)) * slope[q]
        put(pb, q, pre_grad)
        keep_grad(0, q, pre_grad.astype(bf16).astype(f32), patch(xb, q))

    def phase_c(q):
        spread(
            res_out, q,
            jnp.dot(patch(hb, q), w2[q], preferred_element_type=f32) + bs[q, 1:2] + centre(xb, q),
        )

    def phase_d(q):
        spread(res_back, q, wide(patch(pb, q), flipped_wide(w1, q)) + centre(gb, q))

    before = {name: [] for name in ORDER}

    def on(name, action, *args):
        before[name].append(functools.partial(action, *args))

    send_bias(0, 1, 2)
    on("A1", have_weights, 0, (0,))
    on("A1", have_bias, 0)
    on("B1", have_weights, 1, (0,))
    on("B1", have_weights, 0, (1, 3))
    on("B1", send_weights, 0, (5, 6))
    on("B1", have_weights, 0, (2, 4))
    on("B1", send_weights, 0, (7, 8))
    on("B1", have_bias, 1, 2)
    on("B1", send_bias, 3, 4, 5)
    on("B1", send_weights, 1, (1, 3, 2, 4))
    on("A6", have_weights, 0, (5, 6))
    on("A6", send_weights, 0, (9,))
    on("A6", have_bias, 5)
    on("A6", send_bias, 6)
    on("A7", have_weights, 0, (9,))
    on("A7", have_bias, 6)
    on("A3", have_weights, 0, (7,))
    on("A3", have_bias, 3)
    on("A5", have_weights, 0, (8,))
    on("A5", have_bias, 4)
    on("A4", have_weights, 1, (1, 3))
    on("A4", send_weights, 1, (5, 6))
    on("A4", have_weights, 1, (2, 4))
    on("A4", send_weights, 1, (7, 8))
    on("B3", have_weights, 1, (7,))
    on("B6", have_weights, 1, (5, 6))
    on("B6", send_weights, 1, (9,))
    on("B7", have_weights, 1, (9,))
    on("B5", have_weights, 1, (8,))

    for j, phase in ((1, "A"), (0, "B")):
        for p in range(4):
            on(ORDER[AT[phase + str(2 * p + 1)] + 1], send_pair, j, p)

    on("A3", send_diag, 1)
    on("A5", send_free, 1, 1)
    on("B3", send_free, 1, 2)
    on("B3", send_rest, 1, 1)
    on("B3", send_rest, 1, 2)
    on("B4", send_free, 0, 1)
    on("B5", send_diag, 0)
    on("D2", send_free, 0, 2)
    on("C2", have_own, 1)
    on("D2", add_up, 1, 0, 4, 1, 5)
    on("C3", add_up, 1, 2, 6, 3, 7)
    on("C5", middle, 1, 0, 4)
    on("C4", send_rest, 0, 1)
    on("C4", send_rest, 0, 2)
    on("D6", middle, 1, 1, 5)
    on("C7", have_own, 0)
    on("C7", add_up, 0, 0, 4, 1, 5)
    on("D7", add_up, 0, 2, 6, 3, 7)
    on("D7", middle, 1, 2, 6)
    on("D7", ending, 1, 0, 4)

    phases = {"A": phase_a, "B": phase_b, "C": phase_c, "D": phase_d}

    def step(at, carry):
        q = jnp.int32(0)
        kind = jnp.int32(0)
        for index, name in enumerate(ORDER):
            q = jnp.where(at == index, int(name[1]), q)
            kind = jnp.where(at == index, "ABCD".index(name[0]), kind)
            if before[name]:

                @pl.when(at == index)
                def _(name=name):
                    for action in before[name]:
                        action()

        for index, name in enumerate("ABCD"):

            @pl.when(kind == index)
            def _(name=name):
                phases[name](q)

        return carry

    lax.fori_loop(0, len(ORDER), step, 0)


    middle(1, 3, 7)
    ending(1, 1, 5)

    def together(state, carry):
        for at, (src, dst) in enumerate(((res_out, out_ref), (res_back, back_ref))):
            for side in range(2):
                row = jnp.clip(table[0, 8 * SLOTS + side * out_ref.shape[0] + state], 0, src.shape[0] - 1)
                pair[at, pl.ds(side, CELLS, stride=2), :] = src[row].astype(f32)
            dst[state] = pair[at].astype(bf16)
        return carry

    lax.fori_loop(0, out_ref.shape[0], together, 0)
    stores = [
        pltpu.make_async_copy(src, dst, load_sems.at[at])
        for at, (src, dst) in enumerate(((out_ref, out_hbm), (back_ref, back_hbm)))
    ]
    for store in stores:
        store.start()
    middle(0, 0, 4)
    ending(1, 2, 6)
    middle(0, 1, 5)
    ending(1, 3, 7)
    ending(0, 0)
    middle(0, 2)
    ending(0, 4)
    middle(0, 6)
    ending(0, 1)
    middle(0, 3)
    ending(0, 5)
    middle(0, 7)
    ending(0, 2, 6, 3, 7)
    settle()
    for store in stores:
        store.wait()

    for at in range(10):
        give(0, at).wait_send()
        give(1, at).wait_send()
    for at in range(7):
        give_bias(at).wait_send()
    for j in range(2):
        for at in range(6 + 2 * CHUNKS):
            grad_copy(j, at).wait_send()


def last_kernel(
    out_in, back_in, whole_in, out_ref, back_ref, grad_one, grad_two, bias_one, bias_two, boards, whole, grads, sems
):
    channels = whole.shape[-1]
    taps = grads.shape[1]

    def move(src, dst, at):
        return pltpu.make_async_copy(src, dst, sems.at[at])

    loads = [move(whole_in, whole, 0), move(out_in, boards.at[0], 1), move(back_in, boards.at[1], 2)]
    stores = [
        move(boards.at[0], out_ref, 3), move(boards.at[1], back_ref, 4),
        move(grads.at[0], grad_one.at[0], 5), move(grads.at[1], grad_two.at[0], 6),
    ]
    for load in loads:
        load.start()
    loads[0].wait()
    for j, bias in enumerate((bias_one, bias_two)):
        stacked = whole[j].astype(jnp.float32)
        for tap in range(9):
            rows = slice(tap * channels, (tap + 1) * channels)
            grads[j, rows, :] = stacked[rows].T
        stores[2 + j].start()
        loads[1 + j].wait()
        stores[j].start()
        bias[...] = whole[j, taps : taps + 8].astype(jnp.float32)[:1]
    for store in stores:
        store.wait()


def at_home(acts, cotangent, routes, w_first, w_second, b_first, b_second):
    owners = lax.axis_size("member")
    channels = acts.shape[-1]
    taps = 9 * channels
    rows_g = taps + TAIL
    f32, bf16 = jnp.float32, jnp.bfloat16
    count = 2 * routes.shape[0]

    def paired(values):
        return jnp.swapaxes(values, 1, 2).reshape(values.shape[0], 2 * values.shape[2], channels)

    x, g = paired(acts), paired(cotangent)
    anywhere = pl.BlockSpec(memory_space=pl.ANY)
    vmem = pl.BlockSpec(memory_space=pltpu.VMEM)
    shape = jax.ShapeDtypeStruct
    board = pltpu.VMEM((owners, PLACES, channels), bf16)
    weight = pltpu.VMEM((owners, taps, channels), bf16)
    results = pltpu.VMEM((owners * SLOTS, CELLS, channels), bf16)
    sems = pltpu.SemaphoreType.DMA
    made = pl.pallas_call(
        league_kernel,
        out_shape=(
            shape(x.shape, bf16),
            shape(x.shape, bf16),
            shape((2, rows_g, channels), bf16),
        ),
        in_specs=[vmem] + [anywhere] * 6,
        out_specs=(anywhere, anywhere, vmem),
        scratch_shapes=[
            pltpu.VMEM(x.shape, bf16),
            pltpu.VMEM(x.shape, bf16),
            pltpu.VMEM((2, 2 * CELLS, channels), f32),
            pltpu.VMEM((count, CELLS, channels), bf16),
            pltpu.VMEM((count, CELLS, channels), bf16),
            weight,
            weight,
            pltpu.VMEM((owners, 8, channels), f32),
            board,
            board,
            board,
            board,
            pltpu.VMEM((owners, ROWS, channels), f32),
            pltpu.VMEM((2, ROWS, channels), f32),
            results,
            results,
            pltpu.VMEM((2, owners, rows_g, channels), f32),
            pltpu.VMEM((2, owners, rows_g, channels), bf16),
            pltpu.VMEM((2, 4, rows_g, channels), bf16),
            pltpu.VMEM((2, 4, rows_g, channels), bf16),
            pltpu.VMEM((2, 2, taps // 2 + TAIL, channels), bf16),
            pltpu.VMEM((2, 2, rows_g, channels), bf16),
            pltpu.VMEM((2, rows_g, channels), f32),
            pltpu.VMEM((2, rows_g, channels), bf16),
            pltpu.VMEM((2, rows_g, channels), bf16),
            pltpu.VMEM((2, rows_g, channels), bf16),
            pltpu.VMEM((1, 128), jnp.int32),
            pltpu.SMEM((1, 128), jnp.int32),
            sems((7,)),
            sems((40,)),
            sems((40,)),
            sems((48,)),
            sems((48,)),
            sems((48,)),
            sems((48,)),
        ],
        compiler_params=pltpu.CompilerParams(
            collective_id=0, has_side_effects=True, vmem_limit_bytes=60 * 1024 * 1024
        ),
        cost_estimate=pl.CostEstimate(
            flops=12 * owners * ROWS * taps * channels, bytes_accessed=9000000, transcendentals=owners * ROWS * channels
        ),
        name="league",
    )(routes.T, x, g, w_first, w_second, b_first, b_second)
    done = pl.pallas_call(
        last_kernel,
        out_shape=(
            shape(x.shape, bf16),
            shape(x.shape, bf16),
            shape((1, taps, channels), f32),
            shape((1, taps, channels), f32),
            shape((1, channels), f32),
            shape((1, channels), f32),
        ),
        in_specs=[anywhere] * 3,
        out_specs=(anywhere,) * 4 + (vmem,) * 2,
        scratch_shapes=[
            pltpu.VMEM((2,) + x.shape, bf16),
            pltpu.VMEM((2, rows_g, channels), bf16),
            pltpu.VMEM((2, taps, channels), f32),
            sems((7,)),
        ],
        compiler_params=pltpu.CompilerParams(vmem_limit_bytes=60 * 1024 * 1024),
        cost_estimate=pl.CostEstimate(flops=0, bytes_accessed=5000000, transcendentals=0),
        name="last",
    )(*made)

    def unpaired(values):
        return jnp.swapaxes(values.reshape(acts.shape[0], acts.shape[2], 2, channels), 1, 2)

    return (unpaired(done[0]), unpaired(done[1])) + tuple(done[2:])


def solution(mesh):
    placed = (
        P(("rep", "member"), None, None, None),
        P(("rep", "member"), None, None, None),
        P(("rep", "member"), None),
        P("member", None, None),
        P("member", None, None),
        P("member", None),
        P("member", None),
    )
    return jax.shard_map(
        at_home if mesh.shape["member"] == 8 and mesh.shape["rep"] == 4 else shards,
        mesh=mesh,
        in_specs=placed,
        out_specs=(
            P(("rep", "member"), None, None, None),
            P(("rep", "member"), None, None, None),
            P("member", None, None),
            P("member", None, None),
            P("member", None),
            P("member", None),
        ),
        check_vma=False,
    )
```

```python
import functools

import jax
import jax.numpy as jnp
from jax import lax
from jax.experimental import pallas as pl
from jax.experimental.pallas import tpu as pltpu
from jax.sharding import PartitionSpec as P

BOARD = 10


def flipped(weight):
    channels = weight.shape[-1]
    stacked = weight.reshape(weight.shape[:-2] + (9, channels, channels))
    reversed_taps = jnp.flip(stacked, axis=-3)
    return jnp.swapaxes(reversed_taps, -1, -2).reshape(weight.shape)


def silu_slope(pre_act):
    sigmoid_vals = jax.nn.sigmoid(pre_act)
    return sigmoid_vals * (1.0 + pre_act * (1.0 - sigmoid_vals))


def board_conv(values, weight):
    count = values.shape[0]
    channels = values.shape[-1]
    side = BOARD
    boards = values.reshape(count, side, side, channels)
    kernel = weight.reshape(3, 3, channels, channels)
    result = lax.conv_general_dilated(
        boards,
        kernel,
        (1, 1),
        ((1, 1), (1, 1)),
        dimension_numbers=("NHWC", "HWIO", "NHWC"),
        preferred_element_type=jnp.float32,
    )
    return result.reshape(count, side * side, channels)


def weight_conv(values, grads):
    count = values.shape[0]
    channels = values.shape[-1]
    side = BOARD
    boards = values.reshape(count, side, side, channels)
    grad_boards = grads.reshape(count, side, side, channels)
    result = lax.conv_general_dilated(
        boards,
        grad_boards,
        (1, 1),
        ((1, 1), (1, 1)),
        dimension_numbers=("CHWN", "IHWO", "NHWC"),
        preferred_element_type=jnp.float32,
    )
    return jnp.transpose(result, (1, 2, 0, 3)).reshape(9 * channels, channels)


def shards(acts, cotangent, routes, w_first, w_second, b_first, b_second):
    per_owner = w_first.shape[0]
    owners = lax.axis_size("member")
    members_all = owners * per_owner
    capacity = max(2, 4 * routes.shape[0] // members_all)
    channels = acts.shape[-1]
    cell_count = acts.shape[-2]
    member_ids = routes.reshape(-1)
    onehot = (member_ids[:, None] == jnp.arange(members_all, dtype=jnp.int32)[None, :]).astype(
        jnp.int32
    )
    order = jnp.arange(member_ids.shape[0], dtype=jnp.int32)
    earlier = jnp.sum((order[:, None] > order[None, :])[:, :, None] * onehot[None], axis=1)
    slot_index = jnp.sum(earlier * onehot, axis=1)
    target = member_ids * capacity + slot_index
    dispatch = (
        jnp.arange(members_all * capacity, dtype=jnp.int32)[:, None] == target[None, :]
    ).astype(jnp.bfloat16)

    def scatter_rows(values):
        flattened = values.reshape(-1, cell_count * channels)
        placed = jnp.dot(dispatch, flattened, preferred_element_type=jnp.float32).astype(
            jnp.bfloat16
        )
        return placed.reshape(members_all, capacity, cell_count, channels)

    def gather_rows(values):
        flattened = values.reshape(members_all * capacity, cell_count * channels)
        picked = jnp.dot(dispatch.T, flattened, preferred_element_type=jnp.float32).astype(
            jnp.bfloat16
        )
        return picked.reshape(acts.shape)

    def to_local(received):
        grouped = received.reshape(owners, per_owner, capacity, cell_count, channels)
        return jnp.swapaxes(grouped, 0, 1).reshape(
            per_owner, owners * capacity, cell_count, channels
        )

    def from_local(values):
        grouped = values.reshape(per_owner, owners, capacity, cell_count, channels)
        return jnp.swapaxes(grouped, 0, 1).reshape(members_all, capacity, cell_count, channels)

    send_acts = scatter_rows(acts)
    send_grads = scatter_rows(cotangent)
    recv_acts, recv_grads = (
        lax.all_to_all(send_acts, "member", split_axis=0, concat_axis=0, tiled=True),
        lax.all_to_all(send_grads, "member", split_axis=0, concat_axis=0, tiled=True),
    )
    inputs = to_local(recv_acts)
    upstream = to_local(recv_grads)
    owned = 0
    pre_one = board_conv(inputs[owned], w_first[owned]) + b_first[owned][None, None, :]
    hidden_one = jax.nn.silu(pre_one).astype(jnp.bfloat16)
    result_one = (
        inputs[owned].astype(jnp.float32)
        + board_conv(hidden_one, w_second[owned])
        + b_second[owned][None, None, :]
    ).astype(jnp.bfloat16)
    pre_list = [pre_one]
    hidden_list = [hidden_one]
    result_list = [result_one]
    result = jnp.stack(result_list)
    owned = 0
    upstream_one = upstream[owned]
    grad_two_list = [weight_conv(hidden_list[owned], upstream_one)]
    bias_two_list = [jnp.sum(upstream_one.astype(jnp.float32), axis=(0, 1))]
    hidden_grad = board_conv(upstream_one, flipped(w_second[owned]))
    pre_grad = (hidden_grad * silu_slope(pre_list[owned])).astype(jnp.bfloat16)
    grad_one_list = [weight_conv(inputs[owned], pre_grad)]
    bias_one_list = [jnp.sum(pre_grad.astype(jnp.float32), axis=(0, 1))]
    input_list = [
        (upstream_one.astype(jnp.float32) + board_conv(pre_grad, flipped(w_first[owned]))).astype(
            jnp.bfloat16
        )
    ]
    input_grad = jnp.stack(input_list)
    grad_one = jnp.stack(grad_one_list)
    grad_two = jnp.stack(grad_two_list)
    bias_one = jnp.stack(bias_one_list)
    bias_two = jnp.stack(bias_two_list)
    back_out, back_in = (
        lax.all_to_all(from_local(result), "member", split_axis=0, concat_axis=0, tiled=True),
        lax.all_to_all(from_local(input_grad), "member", split_axis=0, concat_axis=0, tiled=True),
    )
    totals = lax.psum((grad_one, grad_two, bias_one, bias_two), "rep")
    return (gather_rows(back_out), gather_rows(back_in), totals[0], totals[1], totals[2], totals[3])


SLOTS = 8
SIDE = BOARD + 2
CELLS = BOARD * BOARD
ROWS = CELLS * SLOTS
LINE = BOARD * SLOTS
PLACES = SIDE * SIDE * SLOTS
TAIL = 16
CHUNKS = 8
MESH_ID = pl.DeviceIdType.MESH

ORDER = (
    ["A0", "A1", "B0", "B1", "C0", "D0", "C1", "D1", "A6", "A7", "A2", "A3", "A4", "A5"]
    + ["B2", "B3", "B6", "B7", "B4", "B5"]
    + ["C2", "D2", "C3", "D3", "C4", "D4", "C5", "D5", "C6", "D6", "C7", "D7"]
)
AT = {name: index for index, name in enumerate(ORDER)}


def inner(line):
    return ((line + 1) * SIDE + 1) * SLOTS


def wide(lhs, rhs):
    return lax.dot_general(lhs, rhs, (((1,), (1,)), ((), ())), preferred_element_type=jnp.float32)


def league_kernel(
    routes, acts_in, cot_in, w1_in, w2_in, b1_in, b2_in,
    out_hbm, back_hbm, whole,
    out_ref, back_ref, pair, acts, cot, w1, w2, bs, xb, gb, hb, pb, slope, mix, res_out, res_back,
    even, odd, paired, chips, diag, cross, total, split, outside, inside,
    lookup, table, load_sems, w_send, w_recv, g_send, g_recv, z_send, z_recv,
):
    f32, bf16 = jnp.float32, jnp.bfloat16
    channels = w1.shape[-1]
    taps = 9 * channels
    half_w = taps // 2
    rows_g = taps + TAIL
    piece = taps // CHUNKS
    half_g = taps // 2
    me = lax.axis_index("member")
    rep = lax.axis_index("rep")
    inner_plane = ((rep + 1) // 2) % 2 == 1
    near = {"core": me ^ 1, "x": me ^ 2, "y": me ^ 4}

    loads = [
        pltpu.make_async_copy(src, dst, load_sems.at[at])
        for at, (src, dst) in enumerate(
            (
                (w1_in.at[0], w1.at[0]), (w2_in.at[0], w2.at[0]),
                (b1_in, bs.at[0, pl.ds(0, 1), :]), (b2_in, bs.at[0, pl.ds(1, 1), :]),
                (acts_in, out_ref), (cot_in, back_ref),
            )
        )
    ]
    for load in loads:
        load.start()

    barrier = pltpu.get_barrier_semaphore()
    for peer in near.values():
        pl.semaphore_signal(barrier, inc=1, device_id={"member": peer}, device_id_type=MESH_ID)
    for far in (1, 3):
        pl.semaphore_signal(barrier, inc=1, device_id={"rep": rep ^ far}, device_id_type=MESH_ID)
    pl.semaphore_wait(barrier, 5)

    def remote(src, dst, sends, recvs, at, peer):
        return pltpu.make_async_remote_copy(
            src_ref=src, dst_ref=dst, send_sem=sends.at[at], recv_sem=recvs.at[at],
            device_id=peer, device_id_type=MESH_ID,
        )

    def member(name):
        return {"member": near[name]}

    def give(kind, at):
        buffer = (w1, w2)[kind]
        own = (w1_in, w2_in)[kind].at[0]
        if at in (0, 7, 8, 9):
            src, dst = {0: (own, 1), 7: (buffer.at[2], 3), 8: (buffer.at[4], 5), 9: (buffer.at[6], 7)}[at]
            ends = (src, buffer.at[dst], member("core"))
        elif at < 5:
            rows = pl.ds((0, 1, 1, 0)[at - 1] * half_w, half_w)
            to = 2 if at < 3 else 4
            ends = (own.at[rows, :], buffer.at[to, rows, :], member("x" if at < 3 else "y"))
        else:
            source, peer = ((2, "y"), (4, "x"))[at - 5]
            rows = pl.ds((at - 5) * half_w, half_w)
            ends = (buffer.at[source, rows, :], buffer.at[6, rows, :], member(peer))
        return remote(ends[0], ends[1], w_send, w_recv, kind * 16 + at, ends[2])

    def give_bias(at):
        src, dst, peer = (
            (0, 1, "core"), (0, 2, "x"), (0, 4, "y"), (2, 3, "core"), (4, 5, "core"), (2, 6, "y"), (6, 7, "core")
        )[at]
        return remote(bs.at[src], bs.at[dst], w_send, w_recv, 32 + at, member(peer))

    def send_weights(kind, ats):
        for at in ats:
            give(kind, at).start()

    def have_weights(kind, ats):
        for at in ats:
            give(kind, at).wait_recv()

    def send_bias(*ats):
        for at in ats:
            give_bias(at).start()

    def have_bias(*ats):
        for at in ats:
            give_bias(at).wait_recv()

    def span(c):
        return c * piece, piece + (TAIL if c == CHUNKS - 1 else 0)

    def grad_copy(j, at):
        if at < 4:
            ends = (odd.at[j, 2 * at + 1], paired.at[j, at], "core")
        elif at < 6:
            size = half_g + (at - 4) * TAIL
            source = chips.at[j, 3, pl.ds((at - 4) * half_g, size), :]
            ends = (source, diag.at[j, at - 4, pl.ds(0, size), :], "xy"[at - 4])
        else:
            p, c = (at - 6) // CHUNKS, (at - 6) % CHUNKS
            rows = pl.ds(*span(c))
            ends = (chips.at[j, p + 1, rows, :], cross.at[j, p, rows, :], "xy"[p])
        return remote(ends[0], ends[1], g_send, g_recv, j * 24 + at, member(ends[2]))

    def rep_copy(j, stage, c):
        src, dst, far = ((split, outside, 1), (split, inside, 3), (whole, whole, 1))[stage]
        rows = pl.ds(*span(c))
        at = (j * 3 + stage) * CHUNKS + c
        return remote(src.at[j, rows, :], dst.at[j, rows, :], z_send, z_recv, at, {"rep": rep ^ far})

    def send_pair(j, p):
        grad_copy(j, p).start()

    def send_diag(j):
        grad_copy(j, 3).wait_recv()
        chips[j, 3] = (even[j, 6] + paired[j, 3].astype(f32)).astype(bf16)
        grad_copy(j, 4).start()
        grad_copy(j, 5).start()

    def send_free(j, p):
        grad_copy(j, p).wait_recv()
        rows = slice(0, half_g) if p == 1 else slice(half_g, rows_g)
        chips[j, p, rows] = (even[j, 2 * p, rows] + paired[j, p, rows].astype(f32)).astype(bf16)
        for c in (range(4) if p == 1 else range(4, 8)):
            grad_copy(j, 6 + CHUNKS * (p - 1) + c).start()

    def send_rest(j, p):
        grad_copy(j, 6 - p).wait_recv()
        rows = slice(half_g, rows_g) if p == 1 else slice(0, half_g)
        value = even[j, 2 * p, rows] + paired[j, p, rows].astype(f32) + diag[j, 2 - p, : half_g + (2 - p) * TAIL].astype(f32)
        chips[j, p, rows] = value.astype(bf16)
        for c in (range(4, 8) if p == 1 else range(4)):
            grad_copy(j, 6 + CHUNKS * (p - 1) + c).start()

    def have_own(j):
        grad_copy(j, 0).wait_recv()

    def add_up(j, *cs):
        for c in cs:
            rows = pl.ds(*span(c))
            grad_copy(j, 6 + c).wait_recv()
            grad_copy(j, 6 + CHUNKS + c).wait_recv()
            value = even[j, 0, rows] + paired[j, 0, rows].astype(f32)
            total[j, rows] = value + cross[j, 0, rows].astype(f32) + cross[j, 1, rows].astype(f32)

            @pl.when(jnp.logical_not(inner_plane))
            def _():
                split[j, rows] = total[j, rows].astype(bf16)
                rep_copy(j, 0, c).start()

    def middle(j, *cs):
        @pl.when(inner_plane)
        def _():
            for c in cs:
                rows = pl.ds(*span(c))
                rep_copy(j, 0, c).wait_recv()
                split[j, rows] = (total[j, rows] + outside[j, rows].astype(f32)).astype(bf16)
                rep_copy(j, 1, c).start()

    def ending(j, *cs):
        @pl.when(inner_plane)
        def _():
            for c in cs:
                rows = pl.ds(*span(c))
                rep_copy(j, 1, c).wait_recv()
                whole[j, rows] = (split[j, rows].astype(f32) + inside[j, rows].astype(f32)).astype(bf16)
                rep_copy(j, 2, c).start()

    def settle():
        @pl.when(jnp.logical_not(inner_plane))
        def _():
            for j in range(2):
                for c in range(CHUNKS):
                    rep_copy(j, 2, c).wait_recv()
                    rep_copy(j, 0, c).wait_send()

        @pl.when(inner_plane)
        def _():
            for j in range(2):
                for c in range(CHUNKS):
                    rep_copy(j, 1, c).wait_send()
                    rep_copy(j, 2, c).wait_send()

    send_weights(0, (1, 3, 2, 4, 0))
    send_weights(1, (0,))

    states = acts_in.shape[0]
    count = 2 * states
    lane = lax.broadcasted_iota(jnp.int32, (count, 128), 1)
    line = lax.broadcasted_iota(jnp.int32, (count, 128), 0)
    named = jnp.concatenate([routes[0:1, :], routes[1:2, :], jnp.full((1, 128 - count), -1, jnp.int32)], axis=1)
    across = jnp.broadcast_to(named, (count, 128))
    down = jnp.sum(jnp.where(lane == line, across, 0), axis=1, keepdims=True)
    place = jnp.sum(jnp.where((line > lane) & (across == down), 1, 0), axis=1, keepdims=True)
    position = jnp.bitwise_xor(down, me) * SLOTS + place
    row = (line % states) * 2 + line // states
    rows = jnp.sum(jnp.where(position == lane, row + 1, 0), axis=0, keepdims=True) - 1
    positions = jnp.sum(jnp.where(lane == line + 8 * SLOTS, position, 0), axis=0, keepdims=True)
    lookup[...] = jnp.where(lane[:1] < 8 * SLOTS, rows, positions)
    fill = pltpu.make_async_copy(lookup, table, load_sems.at[6])
    fill.start()
    for load in loads:
        load.wait()

    def apart(state, carry):
        for at, (src, dst) in enumerate(((out_ref, acts), (back_ref, cot))):
            pair[at] = src[state].astype(f32)
            for side in range(2):
                dst[state * 2 + side] = pair[at, pl.ds(side, CELLS, stride=2), :].astype(bf16)
        return carry

    lax.fori_loop(0, out_ref.shape[0], apart, 0)
    fill.wait()

    def patch(board, q):
        columns = []
        for tap in range(9):
            down, right = tap // 3, tap % 3
            lines = []
            for line in range(BOARD):
                start = ((line + down) * SIDE + right) * SLOTS
                lines.append(board[q, start : start + LINE, :])
            columns.append(jnp.concatenate(lines, axis=0))
        return jnp.concatenate(columns, axis=1)

    def put(board, q, value):
        board[q] = jnp.zeros_like(board[q])
        for line in range(BOARD):
            board[q, inner(line) : inner(line) + LINE, :] = value[line * LINE : (line + 1) * LINE].astype(bf16)

    def centre(board, q):
        return jnp.concatenate(
            [board[q, inner(line) : inner(line) + LINE, :] for line in range(BOARD)], axis=0
        ).astype(f32)

    def flipped_wide(weight, q):
        return jnp.concatenate(
            [weight[q, (8 - tap) * channels : (9 - tap) * channels, :] for tap in range(9)], axis=1
        )

    def gather(src, board, q, at):
        for slot in range(SLOTS):
            row = table[0, q * SLOTS + slot]
            value = src[jnp.clip(row, 0, src.shape[0] - 1)].astype(f32)
            mix[at, pl.ds(slot, CELLS, stride=SLOTS), :] = jnp.where(row >= 0, value, 0.0)
        put(board, q, mix[at])

    def spread(ref, q, value):
        mix[0] = value
        for slot in range(SLOTS):
            ref[q * SLOTS + slot] = mix[0, pl.ds(slot, CELLS, stride=SLOTS), :].astype(bf16)

    def keep_grad(j, q, grad, patches):
        turned = jnp.dot(grad.T.astype(bf16), patches, preferred_element_type=f32)
        bias = jnp.broadcast_to(jnp.sum(grad, axis=0, keepdims=True), (TAIL, channels))
        for ref in (even, odd):
            for tap in range(9):
                ref[j, q, tap * channels : (tap + 1) * channels, :] = turned[
                    :, tap * channels : (tap + 1) * channels
                ].astype(ref.dtype)
            ref[j, q, taps:, :] = bias.astype(ref.dtype)

    def phase_a(q):
        gather(acts, xb, q, 0)
        gather(cot, gb, q, 1)
        pre = jnp.dot(patch(xb, q), w1[q], preferred_element_type=f32) + bs[q, 0:1]
        gate = 0.5 * jnp.tanh(0.5 * pre) + 0.5
        slope[q] = gate * (1.0 + pre * (1.0 - gate))
        put(hb, q, pre * gate)
        keep_grad(1, q, centre(gb, q), patch(hb, q))

    def phase_b(q):
        pre_grad = wide(patch(gb, q), flipped_wide(w2, q)) * slope[q]
        put(pb, q, pre_grad)
        keep_grad(0, q, pre_grad.astype(bf16).astype(f32), patch(xb, q))

    def phase_c(q):
        spread(
            res_out, q,
            jnp.dot(patch(hb, q), w2[q], preferred_element_type=f32) + bs[q, 1:2] + centre(xb, q),
        )

    def phase_d(q):
        spread(res_back, q, wide(patch(pb, q), flipped_wide(w1, q)) + centre(gb, q))

    before = {name: [] for name in ORDER}

    def on(name, action, *args):
        before[name].append(functools.partial(action, *args))

    send_bias(0, 1, 2)
    on("A1", have_weights, 0, (0,))
    on("A1", have_bias, 0)
    on("B1", have_weights, 1, (0,))
    on("B1", have_weights, 0, (1, 3))
    on("B1", send_weights, 0, (5, 6))
    on("B1", have_weights, 0, (2, 4))
    on("B1", send_weights, 0, (7, 8))
    on("B1", have_bias, 1, 2)
    on("B1", send_bias, 3, 4, 5)
    on("B1", send_weights, 1, (1, 3, 2, 4))
    on("A6", have_weights, 0, (5, 6))
    on("A6", send_weights, 0, (9,))
    on("A6", have_bias, 5)
    on("A6", send_bias, 6)
    on("A7", have_weights, 0, (9,))
    on("A7", have_bias, 6)
    on("A3", have_weights, 0, (7,))
    on("A3", have_bias, 3)
    on("A5", have_weights, 0, (8,))
    on("A5", have_bias, 4)
    on("A4", have_weights, 1, (1, 3))
    on("A4", send_weights, 1, (5, 6))
    on("A4", have_weights, 1, (2, 4))
    on("A4", send_weights, 1, (7, 8))
    on("B3", have_weights, 1, (7,))
    on("B6", have_weights, 1, (5, 6))
    on("B6", send_weights, 1, (9,))
    on("B7", have_weights, 1, (9,))
    on("B5", have_weights, 1, (8,))

    for j, phase in ((1, "A"), (0, "B")):
        for p in range(4):
            on(ORDER[AT[phase + str(2 * p + 1)] + 1], send_pair, j, p)

    on("A3", send_diag, 1)
    on("B2", send_free, 1, 1)
    on("B3", send_free, 1, 2)
    on("B3", send_rest, 1, 1)
    on("B3", send_rest, 1, 2)
    on("B4", send_free, 0, 1)
    on("B5", send_diag, 0)
    on("D2", send_free, 0, 2)
    on("C2", have_own, 1)
    on("D2", add_up, 1, 0, 4, 1, 5)
    on("C3", add_up, 1, 2, 6, 3, 7)
    on("C5", middle, 1, 0, 4)
    on("C4", send_rest, 0, 1)
    on("C4", send_rest, 0, 2)
    on("D6", middle, 1, 1, 5)
    on("C7", have_own, 0)
    on("C7", add_up, 0, 0, 4, 1, 5)
    on("D7", add_up, 0, 2, 6, 3, 7)
    on("D7", middle, 1, 2, 6)
    on("D7", ending, 1, 0, 4)

    phases = {"A": phase_a, "B": phase_b, "C": phase_c, "D": phase_d}

    def step(at, carry):
        q = jnp.int32(0)
        kind = jnp.int32(0)
        for index, name in enumerate(ORDER):
            q = jnp.where(at == index, int(name[1]), q)
            kind = jnp.where(at == index, "ABCD".index(name[0]), kind)
            if before[name]:

                @pl.when(at == index)
                def _(name=name):
                    for action in before[name]:
                        action()

        for index, name in enumerate("ABCD"):

            @pl.when(kind == index)
            def _(name=name):
                phases[name](q)

        return carry

    lax.fori_loop(0, len(ORDER), step, 0)


    middle(1, 3, 7)
    ending(1, 1, 5)

    def together(state, carry):
        for at, (src, dst) in enumerate(((res_out, out_ref), (res_back, back_ref))):
            for side in range(2):
                row = jnp.clip(table[0, 8 * SLOTS + side * out_ref.shape[0] + state], 0, src.shape[0] - 1)
                pair[at, pl.ds(side, CELLS, stride=2), :] = src[row].astype(f32)
            dst[state] = pair[at].astype(bf16)
        return carry

    lax.fori_loop(0, out_ref.shape[0], together, 0)
    stores = [
        pltpu.make_async_copy(src, dst, load_sems.at[at])
        for at, (src, dst) in enumerate(((out_ref, out_hbm), (back_ref, back_hbm)))
    ]
    for store in stores:
        store.start()
    middle(0, 0, 4)
    ending(1, 2, 6)
    middle(0, 1, 5)
    ending(1, 3, 7)
    ending(0, 0)
    middle(0, 2)
    ending(0, 4)
    middle(0, 6)
    ending(0, 1)
    middle(0, 3)
    ending(0, 5)
    middle(0, 7)
    ending(0, 2, 6, 3, 7)
    settle()
    for store in stores:
        store.wait()

    for at in range(10):
        give(0, at).wait_send()
        give(1, at).wait_send()
    for at in range(7):
        give_bias(at).wait_send()
    for j in range(2):
        for at in range(6 + 2 * CHUNKS):
            grad_copy(j, at).wait_send()


def last_kernel(
    out_in, back_in, whole_in, out_ref, back_ref, grad_one, grad_two, bias_one, bias_two, boards, whole, grads, sems
):
    channels = whole.shape[-1]
    taps = grads.shape[1]

    def move(src, dst, at):
        return pltpu.make_async_copy(src, dst, sems.at[at])

    loads = [move(whole_in, whole, 0), move(out_in, boards.at[0], 1), move(back_in, boards.at[1], 2)]
    stores = [
        move(boards.at[0], out_ref, 3), move(boards.at[1], back_ref, 4),
        move(grads.at[0], grad_one.at[0], 5), move(grads.at[1], grad_two.at[0], 6),
    ]
    for load in loads:
        load.start()
    loads[0].wait()
    for j, bias in enumerate((bias_one, bias_two)):
        stacked = whole[j].astype(jnp.float32)
        for tap in range(9):
            rows = slice(tap * channels, (tap + 1) * channels)
            grads[j, rows, :] = stacked[rows].T
        stores[2 + j].start()
        loads[1 + j].wait()
        stores[j].start()
        bias[...] = whole[j, taps : taps + 8].astype(jnp.float32)[:1]
    for store in stores:
        store.wait()


def at_home(acts, cotangent, routes, w_first, w_second, b_first, b_second):
    owners = lax.axis_size("member")
    channels = acts.shape[-1]
    taps = 9 * channels
    rows_g = taps + TAIL
    f32, bf16 = jnp.float32, jnp.bfloat16
    count = 2 * routes.shape[0]

    def paired(values):
        return jnp.swapaxes(values, 1, 2).reshape(values.shape[0], 2 * values.shape[2], channels)

    x, g = paired(acts), paired(cotangent)
    anywhere = pl.BlockSpec(memory_space=pl.ANY)
    vmem = pl.BlockSpec(memory_space=pltpu.VMEM)
    shape = jax.ShapeDtypeStruct
    board = pltpu.VMEM((owners, PLACES, channels), bf16)
    weight = pltpu.VMEM((owners, taps, channels), bf16)
    results = pltpu.VMEM((owners * SLOTS, CELLS, channels), bf16)
    sems = pltpu.SemaphoreType.DMA
    made = pl.pallas_call(
        league_kernel,
        out_shape=(
            shape(x.shape, bf16),
            shape(x.shape, bf16),
            shape((2, rows_g, channels), bf16),
        ),
        in_specs=[vmem] + [anywhere] * 6,
        out_specs=(anywhere, anywhere, vmem),
        scratch_shapes=[
            pltpu.VMEM(x.shape, bf16),
            pltpu.VMEM(x.shape, bf16),
            pltpu.VMEM((2, 2 * CELLS, channels), f32),
            pltpu.VMEM((count, CELLS, channels), bf16),
            pltpu.VMEM((count, CELLS, channels), bf16),
            weight,
            weight,
            pltpu.VMEM((owners, 8, channels), f32),
            board,
            board,
            board,
            board,
            pltpu.VMEM((owners, ROWS, channels), f32),
            pltpu.VMEM((2, ROWS, channels), f32),
            results,
            results,
            pltpu.VMEM((2, owners, rows_g, channels), f32),
            pltpu.VMEM((2, owners, rows_g, channels), bf16),
            pltpu.VMEM((2, 4, rows_g, channels), bf16),
            pltpu.VMEM((2, 4, rows_g, channels), bf16),
            pltpu.VMEM((2, 2, taps // 2 + TAIL, channels), bf16),
            pltpu.VMEM((2, 2, rows_g, channels), bf16),
            pltpu.VMEM((2, rows_g, channels), f32),
            pltpu.VMEM((2, rows_g, channels), bf16),
            pltpu.VMEM((2, rows_g, channels), bf16),
            pltpu.VMEM((2, rows_g, channels), bf16),
            pltpu.VMEM((1, 128), jnp.int32),
            pltpu.SMEM((1, 128), jnp.int32),
            sems((7,)),
            sems((40,)),
            sems((40,)),
            sems((48,)),
            sems((48,)),
            sems((48,)),
            sems((48,)),
        ],
        compiler_params=pltpu.CompilerParams(
            collective_id=0, has_side_effects=True, vmem_limit_bytes=60 * 1024 * 1024
        ),
        cost_estimate=pl.CostEstimate(
            flops=12 * owners * ROWS * taps * channels, bytes_accessed=9000000, transcendentals=owners * ROWS * channels
        ),
        name="league",
    )(routes.T, x, g, w_first, w_second, b_first, b_second)
    done = pl.pallas_call(
        last_kernel,
        out_shape=(
            shape(x.shape, bf16),
            shape(x.shape, bf16),
            shape((1, taps, channels), f32),
            shape((1, taps, channels), f32),
            shape((1, channels), f32),
            shape((1, channels), f32),
        ),
        in_specs=[anywhere] * 3,
        out_specs=(anywhere,) * 4 + (vmem,) * 2,
        scratch_shapes=[
            pltpu.VMEM((2,) + x.shape, bf16),
            pltpu.VMEM((2, rows_g, channels), bf16),
            pltpu.VMEM((2, taps, channels), f32),
            sems((7,)),
        ],
        compiler_params=pltpu.CompilerParams(vmem_limit_bytes=60 * 1024 * 1024),
        cost_estimate=pl.CostEstimate(flops=0, bytes_accessed=5000000, transcendentals=0),
        name="last",
    )(*made)

    def unpaired(values):
        return jnp.swapaxes(values.reshape(acts.shape[0], acts.shape[2], 2, channels), 1, 2)

    return (unpaired(done[0]), unpaired(done[1])) + tuple(done[2:])


def solution(mesh):
    placed = (
        P(("rep", "member"), None, None, None),
        P(("rep", "member"), None, None, None),
        P(("rep", "member"), None),
        P("member", None, None),
        P("member", None, None),
        P("member", None),
        P("member", None),
    )
    return jax.shard_map(
        at_home if mesh.shape["member"] == 8 and mesh.shape["rep"] == 4 else shards,
        mesh=mesh,
        in_specs=placed,
        out_specs=(
            P(("rep", "member"), None, None, None),
            P(("rep", "member"), None, None, None),
            P("member", None, None),
            P("member", None, None),
            P("member", None),
            P("member", None),
        ),
        check_vma=False,
    )
```

```python
import functools

import jax
import jax.numpy as jnp
from jax import lax
from jax.experimental import pallas as pl
from jax.experimental.pallas import tpu as pltpu
from jax.sharding import PartitionSpec as P

BOARD = 10


def flipped(weight):
    channels = weight.shape[-1]
    stacked = weight.reshape(weight.shape[:-2] + (9, channels, channels))
    reversed_taps = jnp.flip(stacked, axis=-3)
    return jnp.swapaxes(reversed_taps, -1, -2).reshape(weight.shape)


def silu_slope(pre_act):
    sigmoid_vals = jax.nn.sigmoid(pre_act)
    return sigmoid_vals * (1.0 + pre_act * (1.0 - sigmoid_vals))


def board_conv(values, weight):
    count = values.shape[0]
    channels = values.shape[-1]
    side = BOARD
    boards = values.reshape(count, side, side, channels)
    kernel = weight.reshape(3, 3, channels, channels)
    result = lax.conv_general_dilated(
        boards,
        kernel,
        (1, 1),
        ((1, 1), (1, 1)),
        dimension_numbers=("NHWC", "HWIO", "NHWC"),
        preferred_element_type=jnp.float32,
    )
    return result.reshape(count, side * side, channels)


def weight_conv(values, grads):
    count = values.shape[0]
    channels = values.shape[-1]
    side = BOARD
    boards = values.reshape(count, side, side, channels)
    grad_boards = grads.reshape(count, side, side, channels)
    result = lax.conv_general_dilated(
        boards,
        grad_boards,
        (1, 1),
        ((1, 1), (1, 1)),
        dimension_numbers=("CHWN", "IHWO", "NHWC"),
        preferred_element_type=jnp.float32,
    )
    return jnp.transpose(result, (1, 2, 0, 3)).reshape(9 * channels, channels)


def shards(acts, cotangent, routes, w_first, w_second, b_first, b_second):
    per_owner = w_first.shape[0]
    owners = lax.axis_size("member")
    members_all = owners * per_owner
    capacity = max(2, 4 * routes.shape[0] // members_all)
    channels = acts.shape[-1]
    cell_count = acts.shape[-2]
    member_ids = routes.reshape(-1)
    onehot = (member_ids[:, None] == jnp.arange(members_all, dtype=jnp.int32)[None, :]).astype(
        jnp.int32
    )
    order = jnp.arange(member_ids.shape[0], dtype=jnp.int32)
    earlier = jnp.sum((order[:, None] > order[None, :])[:, :, None] * onehot[None], axis=1)
    slot_index = jnp.sum(earlier * onehot, axis=1)
    target = member_ids * capacity + slot_index
    dispatch = (
        jnp.arange(members_all * capacity, dtype=jnp.int32)[:, None] == target[None, :]
    ).astype(jnp.bfloat16)

    def scatter_rows(values):
        flattened = values.reshape(-1, cell_count * channels)
        placed = jnp.dot(dispatch, flattened, preferred_element_type=jnp.float32).astype(
            jnp.bfloat16
        )
        return placed.reshape(members_all, capacity, cell_count, channels)

    def gather_rows(values):
        flattened = values.reshape(members_all * capacity, cell_count * channels)
        picked = jnp.dot(dispatch.T, flattened, preferred_element_type=jnp.float32).astype(
            jnp.bfloat16
        )
        return picked.reshape(acts.shape)

    def to_local(received):
        grouped = received.reshape(owners, per_owner, capacity, cell_count, channels)
        return jnp.swapaxes(grouped, 0, 1).reshape(
            per_owner, owners * capacity, cell_count, channels
        )

    def from_local(values):
        grouped = values.reshape(per_owner, owners, capacity, cell_count, channels)
        return jnp.swapaxes(grouped, 0, 1).reshape(members_all, capacity, cell_count, channels)

    send_acts = scatter_rows(acts)
    send_grads = scatter_rows(cotangent)
    recv_acts, recv_grads = (
        lax.all_to_all(send_acts, "member", split_axis=0, concat_axis=0, tiled=True),
        lax.all_to_all(send_grads, "member", split_axis=0, concat_axis=0, tiled=True),
    )
    inputs = to_local(recv_acts)
    upstream = to_local(recv_grads)
    owned = 0
    pre_one = board_conv(inputs[owned], w_first[owned]) + b_first[owned][None, None, :]
    hidden_one = jax.nn.silu(pre_one).astype(jnp.bfloat16)
    result_one = (
        inputs[owned].astype(jnp.float32)
        + board_conv(hidden_one, w_second[owned])
        + b_second[owned][None, None, :]
    ).astype(jnp.bfloat16)
    pre_list = [pre_one]
    hidden_list = [hidden_one]
    result_list = [result_one]
    result = jnp.stack(result_list)
    owned = 0
    upstream_one = upstream[owned]
    grad_two_list = [weight_conv(hidden_list[owned], upstream_one)]
    bias_two_list = [jnp.sum(upstream_one.astype(jnp.float32), axis=(0, 1))]
    hidden_grad = board_conv(upstream_one, flipped(w_second[owned]))
    pre_grad = (hidden_grad * silu_slope(pre_list[owned])).astype(jnp.bfloat16)
    grad_one_list = [weight_conv(inputs[owned], pre_grad)]
    bias_one_list = [jnp.sum(pre_grad.astype(jnp.float32), axis=(0, 1))]
    input_list = [
        (upstream_one.astype(jnp.float32) + board_conv(pre_grad, flipped(w_first[owned]))).astype(
            jnp.bfloat16
        )
    ]
    input_grad = jnp.stack(input_list)
    grad_one = jnp.stack(grad_one_list)
    grad_two = jnp.stack(grad_two_list)
    bias_one = jnp.stack(bias_one_list)
    bias_two = jnp.stack(bias_two_list)
    back_out, back_in = (
        lax.all_to_all(from_local(result), "member", split_axis=0, concat_axis=0, tiled=True),
        lax.all_to_all(from_local(input_grad), "member", split_axis=0, concat_axis=0, tiled=True),
    )
    totals = lax.psum((grad_one, grad_two, bias_one, bias_two), "rep")
    return (gather_rows(back_out), gather_rows(back_in), totals[0], totals[1], totals[2], totals[3])


SLOTS = 8
SIDE = BOARD + 2
CELLS = BOARD * BOARD
ROWS = CELLS * SLOTS
LINE = BOARD * SLOTS
PLACES = SIDE * SIDE * SLOTS
TAIL = 16
CHUNKS = 8
MESH_ID = pl.DeviceIdType.MESH

ORDER = (
    ["A0", "A1", "B0", "B1", "C0", "D0", "C1", "D1", "A6", "A7", "A2", "A3", "A4", "A5"]
    + ["B2", "B3", "B6", "B7", "B4", "B5"]
    + ["C2", "D2", "C3", "D3", "C4", "D4", "C5", "D5", "C6", "D6", "C7", "D7"]
)
AT = {name: index for index, name in enumerate(ORDER)}


def inner(line):
    return ((line + 1) * SIDE + 1) * SLOTS


def wide(lhs, rhs):
    return lax.dot_general(lhs, rhs, (((1,), (1,)), ((), ())), preferred_element_type=jnp.float32)


def league_kernel(
    routes, acts_in, cot_in, w1_in, w2_in, b1_in, b2_in,
    out_hbm, back_hbm, whole,
    out_ref, back_ref, pair, acts, cot, w1, w2, bs, xb, gb, hb, pb, slope, mix, res_out, res_back,
    even, odd, paired, chips, diag, cross, total, split, outside, inside,
    lookup, table, load_sems, w_send, w_recv, g_send, g_recv, z_send, z_recv,
):
    f32, bf16 = jnp.float32, jnp.bfloat16
    channels = w1.shape[-1]
    taps = 9 * channels
    half_w = taps // 2
    rows_g = taps + TAIL
    piece = taps // CHUNKS
    half_g = taps // 2
    me = lax.axis_index("member")
    rep = lax.axis_index("rep")
    inner_plane = ((rep + 1) // 2) % 2 == 1
    near = {"core": me ^ 1, "x": me ^ 2, "y": me ^ 4}

    loads = [
        pltpu.make_async_copy(src, dst, load_sems.at[at])
        for at, (src, dst) in enumerate(
            (
                (w1_in.at[0], w1.at[0]), (w2_in.at[0], w2.at[0]),
                (b1_in, bs.at[0, pl.ds(0, 1), :]), (b2_in, bs.at[0, pl.ds(1, 1), :]),
                (acts_in, out_ref), (cot_in, back_ref),
            )
        )
    ]
    for load in loads:
        load.start()

    barrier = pltpu.get_barrier_semaphore()
    for peer in near.values():
        pl.semaphore_signal(barrier, inc=1, device_id={"member": peer}, device_id_type=MESH_ID)
    for far in (1, 3):
        pl.semaphore_signal(barrier, inc=1, device_id={"rep": rep ^ far}, device_id_type=MESH_ID)
    pl.semaphore_wait(barrier, 5)

    def remote(src, dst, sends, recvs, at, peer):
        return pltpu.make_async_remote_copy(
            src_ref=src, dst_ref=dst, send_sem=sends.at[at], recv_sem=recvs.at[at],
            device_id=peer, device_id_type=MESH_ID,
        )

    def member(name):
        return {"member": near[name]}

    def give(kind, at):
        buffer = (w1, w2)[kind]
        own = (w1_in, w2_in)[kind].at[0]
        if at in (0, 7, 8, 9):
            src, dst = {0: (own, 1), 7: (buffer.at[2], 3), 8: (buffer.at[4], 5), 9: (buffer.at[6], 7)}[at]
            ends = (src, buffer.at[dst], member("core"))
        elif at < 5:
            rows = pl.ds((0, 1, 1, 0)[at - 1] * half_w, half_w)
            to = 2 if at < 3 else 4
            ends = (own.at[rows, :], buffer.at[to, rows, :], member("x" if at < 3 else "y"))
        else:
            source, peer = ((2, "y"), (4, "x"))[at - 5]
            rows = pl.ds((at - 5) * half_w, half_w)
            ends = (buffer.at[source, rows, :], buffer.at[6, rows, :], member(peer))
        return remote(ends[0], ends[1], w_send, w_recv, kind * 16 + at, ends[2])

    def give_bias(at):
        src, dst, peer = (
            (0, 1, "core"), (0, 2, "x"), (0, 4, "y"), (2, 3, "core"), (4, 5, "core"), (2, 6, "y"), (6, 7, "core")
        )[at]
        return remote(bs.at[src], bs.at[dst], w_send, w_recv, 32 + at, member(peer))

    def send_weights(kind, ats):
        for at in ats:
            give(kind, at).start()

    def have_weights(kind, ats):
        for at in ats:
            give(kind, at).wait_recv()

    def send_bias(*ats):
        for at in ats:
            give_bias(at).start()

    def have_bias(*ats):
        for at in ats:
            give_bias(at).wait_recv()

    def span(c):
        return c * piece, piece + (TAIL if c == CHUNKS - 1 else 0)

    def grad_copy(j, at):
        if at < 4:
            ends = (odd.at[j, 2 * at + 1], paired.at[j, at], "core")
        elif at < 6:
            size = half_g + (at - 4) * TAIL
            source = chips.at[j, 3, pl.ds((at - 4) * half_g, size), :]
            ends = (source, diag.at[j, at - 4, pl.ds(0, size), :], "xy"[at - 4])
        else:
            p, c = (at - 6) // CHUNKS, (at - 6) % CHUNKS
            rows = pl.ds(*span(c))
            ends = (chips.at[j, p + 1, rows, :], cross.at[j, p, rows, :], "xy"[p])
        return remote(ends[0], ends[1], g_send, g_recv, j * 24 + at, member(ends[2]))

    def rep_copy(j, stage, c):
        src, dst, far = ((split, outside, 1), (split, inside, 3), (whole, whole, 1))[stage]
        rows = pl.ds(*span(c))
        at = (j * 3 + stage) * CHUNKS + c
        return remote(src.at[j, rows, :], dst.at[j, rows, :], z_send, z_recv, at, {"rep": rep ^ far})

    def send_pair(j, p):
        grad_copy(j, p).start()

    def send_diag(j):
        grad_copy(j, 3).wait_recv()
        chips[j, 3] = (even[j, 6] + paired[j, 3].astype(f32)).astype(bf16)
        grad_copy(j, 4).start()
        grad_copy(j, 5).start()

    def send_free(j, p):
        grad_copy(j, p).wait_recv()
        rows = slice(0, half_g) if p == 1 else slice(half_g, rows_g)
        chips[j, p, rows] = (even[j, 2 * p, rows] + paired[j, p, rows].astype(f32)).astype(bf16)
        for c in (range(4) if p == 1 else range(4, 8)):
            grad_copy(j, 6 + CHUNKS * (p - 1) + c).start()

    def send_rest(j, p):
        grad_copy(j, 6 - p).wait_recv()
        rows = slice(half_g, rows_g) if p == 1 else slice(0, half_g)
        value = even[j, 2 * p, rows] + paired[j, p, rows].astype(f32) + diag[j, 2 - p, : half_g + (2 - p) * TAIL].astype(f32)
        chips[j, p, rows] = value.astype(bf16)
        for c in (range(4, 8) if p == 1 else range(4)):
            grad_copy(j, 6 + CHUNKS * (p - 1) + c).start()

    def have_own(j):
        grad_copy(j, 0).wait_recv()

    def add_up(j, *cs):
        for c in cs:
            rows = pl.ds(*span(c))
            grad_copy(j, 6 + c).wait_recv()
            grad_copy(j, 6 + CHUNKS + c).wait_recv()
            value = even[j, 0, rows] + paired[j, 0, rows].astype(f32)
            total[j, rows] = value + cross[j, 0, rows].astype(f32) + cross[j, 1, rows].astype(f32)

            @pl.when(jnp.logical_not(inner_plane))
            def _():
                split[j, rows] = total[j, rows].astype(bf16)
                rep_copy(j, 0, c).start()

    def middle(j, *cs):
        @pl.when(inner_plane)
        def _():
            for c in cs:
                rows = pl.ds(*span(c))
                rep_copy(j, 0, c).wait_recv()
                split[j, rows] = (total[j, rows] + outside[j, rows].astype(f32)).astype(bf16)
                rep_copy(j, 1, c).start()

    def ending(j, *cs):
        @pl.when(inner_plane)
        def _():
            for c in cs:
                rows = pl.ds(*span(c))
                rep_copy(j, 1, c).wait_recv()
                whole[j, rows] = (split[j, rows].astype(f32) + inside[j, rows].astype(f32)).astype(bf16)
                rep_copy(j, 2, c).start()

    def settle():
        @pl.when(jnp.logical_not(inner_plane))
        def _():
            for j in range(2):
                for c in range(CHUNKS):
                    rep_copy(j, 2, c).wait_recv()
                    rep_copy(j, 0, c).wait_send()

        @pl.when(inner_plane)
        def _():
            for j in range(2):
                for c in range(CHUNKS):
                    rep_copy(j, 1, c).wait_send()
                    rep_copy(j, 2, c).wait_send()

    send_weights(0, (1, 3, 2, 4, 0))
    send_weights(1, (0,))

    states = acts_in.shape[0]
    count = 2 * states
    lane = lax.broadcasted_iota(jnp.int32, (count, 128), 1)
    line = lax.broadcasted_iota(jnp.int32, (count, 128), 0)
    named = jnp.concatenate([routes[0:1, :], routes[1:2, :], jnp.full((1, 128 - count), -1, jnp.int32)], axis=1)
    across = jnp.broadcast_to(named, (count, 128))
    down = jnp.sum(jnp.where(lane == line, across, 0), axis=1, keepdims=True)
    place = jnp.sum(jnp.where((line > lane) & (across == down), 1, 0), axis=1, keepdims=True)
    position = jnp.bitwise_xor(down, me) * SLOTS + place
    row = (line % states) * 2 + line // states
    rows = jnp.sum(jnp.where(position == lane, row + 1, 0), axis=0, keepdims=True) - 1
    positions = jnp.sum(jnp.where(lane == line + 8 * SLOTS, position, 0), axis=0, keepdims=True)
    lookup[...] = jnp.where(lane[:1] < 8 * SLOTS, rows, positions)
    fill = pltpu.make_async_copy(lookup, table, load_sems.at[6])
    fill.start()
    for load in loads:
        load.wait()

    def apart(state, carry):
        for at, (src, dst) in enumerate(((out_ref, acts), (back_ref, cot))):
            pair[at] = src[state].astype(f32)
            for side in range(2):
                dst[state * 2 + side] = pair[at, pl.ds(side, CELLS, stride=2), :].astype(bf16)
        return carry

    lax.fori_loop(0, out_ref.shape[0], apart, 0)
    fill.wait()

    def patch(board, q):
        columns = []
        for tap in range(9):
            down, right = tap // 3, tap % 3
            lines = []
            for line in range(BOARD):
                start = ((line + down) * SIDE + right) * SLOTS
                lines.append(board[q, start : start + LINE, :])
            columns.append(jnp.concatenate(lines, axis=0))
        return jnp.concatenate(columns, axis=1)

    def put(board, q, value):
        board[q] = jnp.zeros_like(board[q])
        for line in range(BOARD):
            board[q, inner(line) : inner(line) + LINE, :] = value[line * LINE : (line + 1) * LINE].astype(bf16)

    def centre(board, q):
        return jnp.concatenate(
            [board[q, inner(line) : inner(line) + LINE, :] for line in range(BOARD)], axis=0
        ).astype(f32)

    def flipped_wide(weight, q):
        return jnp.concatenate(
            [weight[q, (8 - tap) * channels : (9 - tap) * channels, :] for tap in range(9)], axis=1
        )

    def gather(src, board, q, at):
        for slot in range(SLOTS):
            row = table[0, q * SLOTS + slot]
            value = src[jnp.clip(row, 0, src.shape[0] - 1)].astype(f32)
            mix[at, pl.ds(slot, CELLS, stride=SLOTS), :] = jnp.where(row >= 0, value, 0.0)
        put(board, q, mix[at])

    def spread(ref, q, value):
        mix[0] = value
        for slot in range(SLOTS):
            ref[q * SLOTS + slot] = mix[0, pl.ds(slot, CELLS, stride=SLOTS), :].astype(bf16)

    def keep_grad(j, q, grad, patches):
        turned = jnp.dot(grad.T.astype(bf16), patches, preferred_element_type=f32)
        bias = jnp.broadcast_to(jnp.sum(grad, axis=0, keepdims=True), (TAIL, channels))
        for ref in (even, odd):
            for tap in range(9):
                ref[j, q, tap * channels : (tap + 1) * channels, :] = turned[
                    :, tap * channels : (tap + 1) * channels
                ].astype(ref.dtype)
            ref[j, q, taps:, :] = bias.astype(ref.dtype)

    def phase_a(q):
        gather(acts, xb, q, 0)
        gather(cot, gb, q, 1)
        pre = jnp.dot(patch(xb, q), w1[q], preferred_element_type=f32) + bs[q, 0:1]
        gate = 0.5 * jnp.tanh(0.5 * pre) + 0.5
        slope[q] = gate * (1.0 + pre * (1.0 - gate))
        put(hb, q, pre * gate)
        keep_grad(1, q, centre(gb, q), patch(hb, q))

    def phase_b(q):
        pre_grad = wide(patch(gb, q), flipped_wide(w2, q)) * slope[q]
        put(pb, q, pre_grad)
        keep_grad(0, q, pre_grad.astype(bf16).astype(f32), patch(xb, q))

    def phase_c(q):
        spread(
            res_out, q,
            jnp.dot(patch(hb, q), w2[q], preferred_element_type=f32) + bs[q, 1:2] + centre(xb, q),
        )

    def phase_d(q):
        spread(res_back, q, wide(patch(pb, q), flipped_wide(w1, q)) + centre(gb, q))

    before = {name: [] for name in ORDER}

    def on(name, action, *args):
        before[name].append(functools.partial(action, *args))

    send_bias(0, 1, 2)
    on("A1", have_weights, 0, (0,))
    on("A1", have_bias, 0)
    on("B1", have_weights, 1, (0,))
    on("B1", have_weights, 0, (1, 3))
    on("B1", send_weights, 0, (5, 6))
    on("B1", have_weights, 0, (2, 4))
    on("B1", send_weights, 0, (7, 8))
    on("B1", have_bias, 1, 2)
    on("B1", send_bias, 3, 4, 5)
    on("B1", send_weights, 1, (1, 3, 2, 4))
    on("A6", have_weights, 0, (5, 6))
    on("A6", send_weights, 0, (9,))
    on("A6", have_bias, 5)
    on("A6", send_bias, 6)
    on("A7", have_weights, 0, (9,))
    on("A7", have_bias, 6)
    on("A3", have_weights, 0, (7,))
    on("A3", have_bias, 3)
    on("A5", have_weights, 0, (8,))
    on("A5", have_bias, 4)
    on("A4", have_weights, 1, (1, 3))
    on("A4", send_weights, 1, (5, 6))
    on("A4", have_weights, 1, (2, 4))
    on("A4", send_weights, 1, (7, 8))
    on("B3", have_weights, 1, (7,))
    on("B6", have_weights, 1, (5, 6))
    on("B6", send_weights, 1, (9,))
    on("B7", have_weights, 1, (9,))
    on("B5", have_weights, 1, (8,))

    for j, phase in ((1, "A"), (0, "B")):
        for p in range(4):
            on(ORDER[AT[phase + str(2 * p + 1)] + 1], send_pair, j, p)

    on("A3", send_diag, 1)
    on("B2", send_free, 1, 1)
    on("B3", send_free, 1, 2)
    on("B3", send_rest, 1, 1)
    on("B3", send_rest, 1, 2)
    on("B4", send_free, 0, 1)
    on("B5", send_diag, 0)
    on("D2", send_free, 0, 2)
    on("C2", have_own, 1)
    on("D2", add_up, 1, 0, 4, 1, 5)
    on("C3", add_up, 1, 2, 6, 3, 7)
    on("C5", middle, 1, 0, 4)
    on("C4", send_rest, 0, 1)
    on("C4", send_rest, 0, 2)
    on("D6", middle, 1, 1, 5)
    on("C7", have_own, 0)
    on("C7", add_up, 0, 0, 4, 1, 5)
    on("D7", add_up, 0, 2, 6, 3, 7)
    on("D7", middle, 1, 2, 6)
    on("D7", ending, 1, 0, 4)

    phases = {"A": phase_a, "B": phase_b, "C": phase_c, "D": phase_d}

    def step(at, carry):
        q = jnp.int32(0)
        kind = jnp.int32(0)
        for index, name in enumerate(ORDER):
            q = jnp.where(at == index, int(name[1]), q)
            kind = jnp.where(at == index, "ABCD".index(name[0]), kind)
            if before[name]:

                @pl.when(at == index)
                def _(name=name):
                    for action in before[name]:
                        action()

        for index, name in enumerate("ABCD"):

            @pl.when(kind == index)
            def _(name=name):
                phases[name](q)

        return carry

    lax.fori_loop(0, len(ORDER), step, 0)


    middle(1, 3, 7)
    ending(1, 1, 5)

    def together(state, carry):
        for at, (src, dst) in enumerate(((res_out, out_ref), (res_back, back_ref))):
            for side in range(2):
                row = jnp.clip(table[0, 8 * SLOTS + side * out_ref.shape[0] + state], 0, src.shape[0] - 1)
                pair[at, pl.ds(side, CELLS, stride=2), :] = src[row].astype(f32)
            dst[state] = pair[at].astype(bf16)
        return carry

    lax.fori_loop(0, out_ref.shape[0], together, 0)
    stores = [
        pltpu.make_async_copy(src, dst, load_sems.at[at])
        for at, (src, dst) in enumerate(((out_ref, out_hbm), (back_ref, back_hbm)))
    ]
    for store in stores:
        store.start()
    middle(0, 0, 4)
    ending(1, 2, 6)
    middle(0, 1, 5)
    ending(1, 3, 7)
    ending(0, 0)
    middle(0, 2)
    ending(0, 4)
    middle(0, 6)
    ending(0, 1)
    middle(0, 3)
    ending(0, 5)
    middle(0, 7)
    ending(0, 2, 6, 3, 7)
    settle()
    for store in stores:
        store.wait()

    for at in range(10):
        give(0, at).wait_send()
        give(1, at).wait_send()
    for at in range(7):
        give_bias(at).wait_send()
    for j in range(2):
        for at in range(6 + 2 * CHUNKS):
            grad_copy(j, at).wait_send()


def last_kernel(
    out_in, back_in, whole_in, out_ref, back_ref, grad_one, grad_two, bias_one, bias_two, boards, whole, grads, sems
):
    channels = whole.shape[-1]
    taps = grads.shape[1]

    def move(src, dst, at):
        return pltpu.make_async_copy(src, dst, sems.at[at])

    loads = [
        move(whole_in.at[0], whole.at[0], 0), move(out_in, boards.at[0], 1),
        move(whole_in.at[1], whole.at[1], 7), move(back_in, boards.at[1], 2),
    ]
    stores = [
        move(boards.at[0], out_ref, 3), move(boards.at[1], back_ref, 4),
        move(grads.at[0], grad_one.at[0], 5), move(grads.at[1], grad_two.at[0], 6),
    ]
    for load in loads:
        load.start()
    for j, bias in enumerate((bias_one, bias_two)):
        loads[2 * j].wait()
        stacked = whole[j].astype(jnp.float32)
        for tap in range(9):
            rows = slice(tap * channels, (tap + 1) * channels)
            grads[j, rows, :] = stacked[rows].T
        stores[2 + j].start()
        loads[2 * j + 1].wait()
        stores[j].start()
        bias[...] = whole[j, taps : taps + 8].astype(jnp.float32)[:1]
    for store in stores:
        store.wait()


def at_home(acts, cotangent, routes, w_first, w_second, b_first, b_second):
    owners = lax.axis_size("member")
    channels = acts.shape[-1]
    taps = 9 * channels
    rows_g = taps + TAIL
    f32, bf16 = jnp.float32, jnp.bfloat16
    count = 2 * routes.shape[0]

    def paired(values):
        return jnp.swapaxes(values, 1, 2).reshape(values.shape[0], 2 * values.shape[2], channels)

    x, g = paired(acts), paired(cotangent)
    anywhere = pl.BlockSpec(memory_space=pl.ANY)
    vmem = pl.BlockSpec(memory_space=pltpu.VMEM)
    shape = jax.ShapeDtypeStruct
    board = pltpu.VMEM((owners, PLACES, channels), bf16)
    weight = pltpu.VMEM((owners, taps, channels), bf16)
    results = pltpu.VMEM((owners * SLOTS, CELLS, channels), bf16)
    sems = pltpu.SemaphoreType.DMA
    made = pl.pallas_call(
        league_kernel,
        out_shape=(
            shape(x.shape, bf16),
            shape(x.shape, bf16),
            shape((2, rows_g, channels), bf16),
        ),
        in_specs=[vmem] + [anywhere] * 6,
        out_specs=(anywhere, anywhere, vmem),
        scratch_shapes=[
            pltpu.VMEM(x.shape, bf16),
            pltpu.VMEM(x.shape, bf16),
            pltpu.VMEM((2, 2 * CELLS, channels), f32),
            pltpu.VMEM((count, CELLS, channels), bf16),
            pltpu.VMEM((count, CELLS, channels), bf16),
            weight,
            weight,
            pltpu.VMEM((owners, 8, channels), f32),
            board,
            board,
            board,
            board,
            pltpu.VMEM((owners, ROWS, channels), f32),
            pltpu.VMEM((2, ROWS, channels), f32),
            results,
            results,
            pltpu.VMEM((2, owners, rows_g, channels), f32),
            pltpu.VMEM((2, owners, rows_g, channels), bf16),
            pltpu.VMEM((2, 4, rows_g, channels), bf16),
            pltpu.VMEM((2, 4, rows_g, channels), bf16),
            pltpu.VMEM((2, 2, taps // 2 + TAIL, channels), bf16),
            pltpu.VMEM((2, 2, rows_g, channels), bf16),
            pltpu.VMEM((2, rows_g, channels), f32),
            pltpu.VMEM((2, rows_g, channels), bf16),
            pltpu.VMEM((2, rows_g, channels), bf16),
            pltpu.VMEM((2, rows_g, channels), bf16),
            pltpu.VMEM((1, 128), jnp.int32),
            pltpu.SMEM((1, 128), jnp.int32),
            sems((7,)),
            sems((40,)),
            sems((40,)),
            sems((48,)),
            sems((48,)),
            sems((48,)),
            sems((48,)),
        ],
        compiler_params=pltpu.CompilerParams(
            collective_id=0, has_side_effects=True, vmem_limit_bytes=60 * 1024 * 1024
        ),
        cost_estimate=pl.CostEstimate(
            flops=12 * owners * ROWS * taps * channels, bytes_accessed=9000000, transcendentals=owners * ROWS * channels
        ),
        name="league",
    )(routes.T, x, g, w_first, w_second, b_first, b_second)
    done = pl.pallas_call(
        last_kernel,
        out_shape=(
            shape(x.shape, bf16),
            shape(x.shape, bf16),
            shape((1, taps, channels), f32),
            shape((1, taps, channels), f32),
            shape((1, channels), f32),
            shape((1, channels), f32),
        ),
        in_specs=[anywhere] * 3,
        out_specs=(anywhere,) * 4 + (vmem,) * 2,
        scratch_shapes=[
            pltpu.VMEM((2,) + x.shape, bf16),
            pltpu.VMEM((2, rows_g, channels), bf16),
            pltpu.VMEM((2, taps, channels), f32),
            sems((8,)),
        ],
        compiler_params=pltpu.CompilerParams(vmem_limit_bytes=60 * 1024 * 1024),
        cost_estimate=pl.CostEstimate(flops=0, bytes_accessed=5000000, transcendentals=0),
        name="last",
    )(*made)

    def unpaired(values):
        return jnp.swapaxes(values.reshape(acts.shape[0], acts.shape[2], 2, channels), 1, 2)

    return (unpaired(done[0]), unpaired(done[1])) + tuple(done[2:])


def solution(mesh):
    placed = (
        P(("rep", "member"), None, None, None),
        P(("rep", "member"), None, None, None),
        P(("rep", "member"), None),
        P("member", None, None),
        P("member", None, None),
        P("member", None),
        P("member", None),
    )
    return jax.shard_map(
        at_home if mesh.shape["member"] == 8 and mesh.shape["rep"] == 4 else shards,
        mesh=mesh,
        in_specs=placed,
        out_specs=(
            P(("rep", "member"), None, None, None),
            P(("rep", "member"), None, None, None),
            P("member", None, None),
            P("member", None, None),
            P("member", None),
            P("member", None),
        ),
        check_vma=False,
    )
```

```python
import functools

import jax
import jax.numpy as jnp
from jax import lax
from jax.experimental import pallas as pl
from jax.experimental.pallas import tpu as pltpu
from jax.sharding import PartitionSpec as P

BOARD = 10


def flipped(weight):
    channels = weight.shape[-1]
    stacked = weight.reshape(weight.shape[:-2] + (9, channels, channels))
    reversed_taps = jnp.flip(stacked, axis=-3)
    return jnp.swapaxes(reversed_taps, -1, -2).reshape(weight.shape)


def silu_slope(pre_act):
    sigmoid_vals = jax.nn.sigmoid(pre_act)
    return sigmoid_vals * (1.0 + pre_act * (1.0 - sigmoid_vals))


def board_conv(values, weight):
    count = values.shape[0]
    channels = values.shape[-1]
    side = BOARD
    boards = values.reshape(count, side, side, channels)
    kernel = weight.reshape(3, 3, channels, channels)
    result = lax.conv_general_dilated(
        boards,
        kernel,
        (1, 1),
        ((1, 1), (1, 1)),
        dimension_numbers=("NHWC", "HWIO", "NHWC"),
        preferred_element_type=jnp.float32,
    )
    return result.reshape(count, side * side, channels)


def weight_conv(values, grads):
    count = values.shape[0]
    channels = values.shape[-1]
    side = BOARD
    boards = values.reshape(count, side, side, channels)
    grad_boards = grads.reshape(count, side, side, channels)
    result = lax.conv_general_dilated(
        boards,
        grad_boards,
        (1, 1),
        ((1, 1), (1, 1)),
        dimension_numbers=("CHWN", "IHWO", "NHWC"),
        preferred_element_type=jnp.float32,
    )
    return jnp.transpose(result, (1, 2, 0, 3)).reshape(9 * channels, channels)


def shards(acts, cotangent, routes, w_first, w_second, b_first, b_second):
    per_owner = w_first.shape[0]
    owners = lax.axis_size("member")
    members_all = owners * per_owner
    capacity = max(2, 4 * routes.shape[0] // members_all)
    channels = acts.shape[-1]
    cell_count = acts.shape[-2]
    member_ids = routes.reshape(-1)
    onehot = (member_ids[:, None] == jnp.arange(members_all, dtype=jnp.int32)[None, :]).astype(
        jnp.int32
    )
    order = jnp.arange(member_ids.shape[0], dtype=jnp.int32)
    earlier = jnp.sum((order[:, None] > order[None, :])[:, :, None] * onehot[None], axis=1)
    slot_index = jnp.sum(earlier * onehot, axis=1)
    target = member_ids * capacity + slot_index
    dispatch = (
        jnp.arange(members_all * capacity, dtype=jnp.int32)[:, None] == target[None, :]
    ).astype(jnp.bfloat16)

    def scatter_rows(values):
        flattened = values.reshape(-1, cell_count * channels)
        placed = jnp.dot(dispatch, flattened, preferred_element_type=jnp.float32).astype(
            jnp.bfloat16
        )
        return placed.reshape(members_all, capacity, cell_count, channels)

    def gather_rows(values):
        flattened = values.reshape(members_all * capacity, cell_count * channels)
        picked = jnp.dot(dispatch.T, flattened, preferred_element_type=jnp.float32).astype(
            jnp.bfloat16
        )
        return picked.reshape(acts.shape)

    def to_local(received):
        grouped = received.reshape(owners, per_owner, capacity, cell_count, channels)
        return jnp.swapaxes(grouped, 0, 1).reshape(
            per_owner, owners * capacity, cell_count, channels
        )

    def from_local(values):
        grouped = values.reshape(per_owner, owners, capacity, cell_count, channels)
        return jnp.swapaxes(grouped, 0, 1).reshape(members_all, capacity, cell_count, channels)

    send_acts = scatter_rows(acts)
    send_grads = scatter_rows(cotangent)
    recv_acts, recv_grads = (
        lax.all_to_all(send_acts, "member", split_axis=0, concat_axis=0, tiled=True),
        lax.all_to_all(send_grads, "member", split_axis=0, concat_axis=0, tiled=True),
    )
    inputs = to_local(recv_acts)
    upstream = to_local(recv_grads)
    owned = 0
    pre_one = board_conv(inputs[owned], w_first[owned]) + b_first[owned][None, None, :]
    hidden_one = jax.nn.silu(pre_one).astype(jnp.bfloat16)
    result_one = (
        inputs[owned].astype(jnp.float32)
        + board_conv(hidden_one, w_second[owned])
        + b_second[owned][None, None, :]
    ).astype(jnp.bfloat16)
    pre_list = [pre_one]
    hidden_list = [hidden_one]
    result_list = [result_one]
    result = jnp.stack(result_list)
    owned = 0
    upstream_one = upstream[owned]
    grad_two_list = [weight_conv(hidden_list[owned], upstream_one)]
    bias_two_list = [jnp.sum(upstream_one.astype(jnp.float32), axis=(0, 1))]
    hidden_grad = board_conv(upstream_one, flipped(w_second[owned]))
    pre_grad = (hidden_grad * silu_slope(pre_list[owned])).astype(jnp.bfloat16)
    grad_one_list = [weight_conv(inputs[owned], pre_grad)]
    bias_one_list = [jnp.sum(pre_grad.astype(jnp.float32), axis=(0, 1))]
    input_list = [
        (upstream_one.astype(jnp.float32) + board_conv(pre_grad, flipped(w_first[owned]))).astype(
            jnp.bfloat16
        )
    ]
    input_grad = jnp.stack(input_list)
    grad_one = jnp.stack(grad_one_list)
    grad_two = jnp.stack(grad_two_list)
    bias_one = jnp.stack(bias_one_list)
    bias_two = jnp.stack(bias_two_list)
    back_out, back_in = (
        lax.all_to_all(from_local(result), "member", split_axis=0, concat_axis=0, tiled=True),
        lax.all_to_all(from_local(input_grad), "member", split_axis=0, concat_axis=0, tiled=True),
    )
    totals = lax.psum((grad_one, grad_two, bias_one, bias_two), "rep")
    return (gather_rows(back_out), gather_rows(back_in), totals[0], totals[1], totals[2], totals[3])


SLOTS = 8
SIDE = BOARD + 2
CELLS = BOARD * BOARD
ROWS = CELLS * SLOTS
LINE = BOARD * SLOTS
PLACES = SIDE * SIDE * SLOTS
TAIL = 16
CHUNKS = 8
MESH_ID = pl.DeviceIdType.MESH

ORDER = (
    ["A0", "A1", "B0", "B1", "C0", "D0", "C1", "D1", "A6", "A7", "A2", "A3", "A4", "A5"]
    + ["B2", "B3", "B6", "B7", "B4", "B5"]
    + ["C2", "D2", "C3", "D3", "C4", "D4", "C5", "D5", "C6", "D6", "C7", "D7"]
)
AT = {name: index for index, name in enumerate(ORDER)}


def inner(line):
    return ((line + 1) * SIDE + 1) * SLOTS


def wide(lhs, rhs):
    return lax.dot_general(lhs, rhs, (((1,), (1,)), ((), ())), preferred_element_type=jnp.float32)


def league_kernel(
    routes, acts_in, cot_in, w1_in, w2_in, b1_in, b2_in,
    out_hbm, back_hbm, whole,
    out_ref, back_ref, pair, acts, cot, w1, w2, bs, xb, gb, hb, pb, slope, mix, res_out, res_back,
    even, odd, paired, chips, diag, cross, total, split, outside, inside,
    lookup, table, load_sems, w_send, w_recv, g_send, g_recv, z_send, z_recv,
):
    f32, bf16 = jnp.float32, jnp.bfloat16
    channels = w1.shape[-1]
    taps = 9 * channels
    half_w = taps // 2
    rows_g = taps + TAIL
    piece = taps // CHUNKS
    half_g = taps // 2
    me = lax.axis_index("member")
    rep = lax.axis_index("rep")
    inner_plane = ((rep + 1) // 2) % 2 == 1
    near = {"core": me ^ 1, "x": me ^ 2, "y": me ^ 4}

    loads = [
        pltpu.make_async_copy(src, dst, load_sems.at[at])
        for at, (src, dst) in enumerate(
            (
                (w1_in.at[0], w1.at[0]), (w2_in.at[0], w2.at[0]),
                (b1_in, bs.at[0, pl.ds(0, 1), :]), (b2_in, bs.at[0, pl.ds(1, 1), :]),
                (acts_in, out_ref), (cot_in, back_ref),
            )
        )
    ]
    for load in loads:
        load.start()

    barrier = pltpu.get_barrier_semaphore()
    for peer in near.values():
        pl.semaphore_signal(barrier, inc=1, device_id={"member": peer}, device_id_type=MESH_ID)
    for far in (1, 3):
        pl.semaphore_signal(barrier, inc=1, device_id={"rep": rep ^ far}, device_id_type=MESH_ID)
    pl.semaphore_wait(barrier, 5)

    def remote(src, dst, sends, recvs, at, peer):
        return pltpu.make_async_remote_copy(
            src_ref=src, dst_ref=dst, send_sem=sends.at[at], recv_sem=recvs.at[at],
            device_id=peer, device_id_type=MESH_ID,
        )

    def member(name):
        return {"member": near[name]}

    def give(kind, at):
        buffer = (w1, w2)[kind]
        own = (w1_in, w2_in)[kind].at[0]
        if at in (0, 7, 8, 9):
            src, dst = {0: (own, 1), 7: (buffer.at[2], 3), 8: (buffer.at[4], 5), 9: (buffer.at[6], 7)}[at]
            ends = (src, buffer.at[dst], member("core"))
        elif at < 5:
            rows = pl.ds((0, 1, 1, 0)[at - 1] * half_w, half_w)
            to = 2 if at < 3 else 4
            ends = (own.at[rows, :], buffer.at[to, rows, :], member("x" if at < 3 else "y"))
        else:
            source, peer = ((2, "y"), (4, "x"))[at - 5]
            rows = pl.ds((at - 5) * half_w, half_w)
            ends = (buffer.at[source, rows, :], buffer.at[6, rows, :], member(peer))
        return remote(ends[0], ends[1], w_send, w_recv, kind * 16 + at, ends[2])

    def give_bias(at):
        src, dst, peer = (
            (0, 1, "core"), (0, 2, "x"), (0, 4, "y"), (2, 3, "core"), (4, 5, "core"), (2, 6, "y"), (6, 7, "core")
        )[at]
        return remote(bs.at[src], bs.at[dst], w_send, w_recv, 32 + at, member(peer))

    def send_weights(kind, ats):
        for at in ats:
            give(kind, at).start()

    def have_weights(kind, ats):
        for at in ats:
            give(kind, at).wait_recv()

    def send_bias(*ats):
        for at in ats:
            give_bias(at).start()

    def have_bias(*ats):
        for at in ats:
            give_bias(at).wait_recv()

    def span(c):
        return c * piece, piece + (TAIL if c == CHUNKS - 1 else 0)

    def grad_copy(j, at):
        if at < 4:
            ends = (odd.at[j, 2 * at + 1], paired.at[j, at], "core")
        elif at < 6:
            size = half_g + (at - 4) * TAIL
            source = chips.at[j, 3, pl.ds((at - 4) * half_g, size), :]
            ends = (source, diag.at[j, at - 4, pl.ds(0, size), :], "xy"[at - 4])
        else:
            p, c = (at - 6) // CHUNKS, (at - 6) % CHUNKS
            rows = pl.ds(*span(c))
            ends = (chips.at[j, p + 1, rows, :], cross.at[j, p, rows, :], "xy"[p])
        return remote(ends[0], ends[1], g_send, g_recv, j * 24 + at, member(ends[2]))

    def rep_copy(j, stage, c):
        src, dst, far = ((split, outside, 1), (split, inside, 3), (whole, whole, 1))[stage]
        rows = pl.ds(*span(c))
        at = (j * 3 + stage) * CHUNKS + c
        return remote(src.at[j, rows, :], dst.at[j, rows, :], z_send, z_recv, at, {"rep": rep ^ far})

    def send_pair(j, p):
        grad_copy(j, p).start()

    def send_diag(j):
        grad_copy(j, 3).wait_recv()
        chips[j, 3] = (even[j, 6] + paired[j, 3].astype(f32)).astype(bf16)
        grad_copy(j, 4).start()
        grad_copy(j, 5).start()

    def send_free(j, p):
        grad_copy(j, p).wait_recv()
        rows = slice(0, half_g) if p == 1 else slice(half_g, rows_g)
        chips[j, p, rows] = (even[j, 2 * p, rows] + paired[j, p, rows].astype(f32)).astype(bf16)
        for c in (range(4) if p == 1 else range(4, 8)):
            grad_copy(j, 6 + CHUNKS * (p - 1) + c).start()

    def send_rest(j, p):
        grad_copy(j, 6 - p).wait_recv()
        rows = slice(half_g, rows_g) if p == 1 else slice(0, half_g)
        value = even[j, 2 * p, rows] + paired[j, p, rows].astype(f32) + diag[j, 2 - p, : half_g + (2 - p) * TAIL].astype(f32)
        chips[j, p, rows] = value.astype(bf16)
        for c in (range(4, 8) if p == 1 else range(4)):
            grad_copy(j, 6 + CHUNKS * (p - 1) + c).start()

    def have_own(j):
        grad_copy(j, 0).wait_recv()

    def add_up(j, *cs):
        for c in cs:
            rows = pl.ds(*span(c))
            grad_copy(j, 6 + c).wait_recv()
            grad_copy(j, 6 + CHUNKS + c).wait_recv()
            value = even[j, 0, rows] + paired[j, 0, rows].astype(f32)
            total[j, rows] = value + cross[j, 0, rows].astype(f32) + cross[j, 1, rows].astype(f32)

            @pl.when(jnp.logical_not(inner_plane))
            def _():
                split[j, rows] = total[j, rows].astype(bf16)
                rep_copy(j, 0, c).start()

    def middle(j, *cs):
        @pl.when(inner_plane)
        def _():
            for c in cs:
                rows = pl.ds(*span(c))
                rep_copy(j, 0, c).wait_recv()
                split[j, rows] = (total[j, rows] + outside[j, rows].astype(f32)).astype(bf16)
                rep_copy(j, 1, c).start()

    def ending(j, *cs):
        @pl.when(inner_plane)
        def _():
            for c in cs:
                rows = pl.ds(*span(c))
                rep_copy(j, 1, c).wait_recv()
                whole[j, rows] = (split[j, rows].astype(f32) + inside[j, rows].astype(f32)).astype(bf16)
                rep_copy(j, 2, c).start()

    def settle():
        @pl.when(jnp.logical_not(inner_plane))
        def _():
            for j in range(2):
                for c in range(CHUNKS):
                    rep_copy(j, 2, c).wait_recv()
                    rep_copy(j, 0, c).wait_send()

        @pl.when(inner_plane)
        def _():
            for j in range(2):
                for c in range(CHUNKS):
                    rep_copy(j, 1, c).wait_send()
                    rep_copy(j, 2, c).wait_send()

    send_weights(0, (1, 3, 2, 4, 0))
    send_weights(1, (0,))

    states = acts_in.shape[0]
    count = 2 * states
    lane = lax.broadcasted_iota(jnp.int32, (count, 128), 1)
    line = lax.broadcasted_iota(jnp.int32, (count, 128), 0)
    named = jnp.concatenate([routes[0:1, :], routes[1:2, :], jnp.full((1, 128 - count), -1, jnp.int32)], axis=1)
    across = jnp.broadcast_to(named, (count, 128))
    down = jnp.sum(jnp.where(lane == line, across, 0), axis=1, keepdims=True)
    place = jnp.sum(jnp.where((line > lane) & (across == down), 1, 0), axis=1, keepdims=True)
    position = jnp.bitwise_xor(down, me) * SLOTS + place
    row = (line % states) * 2 + line // states
    rows = jnp.sum(jnp.where(position == lane, row + 1, 0), axis=0, keepdims=True) - 1
    positions = jnp.sum(jnp.where(lane == line + 8 * SLOTS, position, 0), axis=0, keepdims=True)
    lookup[...] = jnp.where(lane[:1] < 8 * SLOTS, rows, positions)
    fill = pltpu.make_async_copy(lookup, table, load_sems.at[6])
    fill.start()
    for load in loads:
        load.wait()

    def apart(state, carry):
        for at, (src, dst) in enumerate(((out_ref, acts), (back_ref, cot))):
            pair[at] = src[state].astype(f32)
            for side in range(2):
                dst[state * 2 + side] = pair[at, pl.ds(side, CELLS, stride=2), :].astype(bf16)
        return carry

    lax.fori_loop(0, out_ref.shape[0], apart, 0)
    fill.wait()

    def patch(board, q):
        columns = []
        for tap in range(9):
            down, right = tap // 3, tap % 3
            lines = []
            for line in range(BOARD):
                start = ((line + down) * SIDE + right) * SLOTS
                lines.append(board[q, start : start + LINE, :])
            columns.append(jnp.concatenate(lines, axis=0))
        return jnp.concatenate(columns, axis=1)

    def put(board, q, value):
        board[q] = jnp.zeros_like(board[q])
        for line in range(BOARD):
            board[q, inner(line) : inner(line) + LINE, :] = value[line * LINE : (line + 1) * LINE].astype(bf16)

    def centre(board, q):
        return jnp.concatenate(
            [board[q, inner(line) : inner(line) + LINE, :] for line in range(BOARD)], axis=0
        ).astype(f32)

    def flipped_wide(weight, q):
        return jnp.concatenate(
            [weight[q, (8 - tap) * channels : (9 - tap) * channels, :] for tap in range(9)], axis=1
        )

    def gather(src, board, q, at):
        for slot in range(SLOTS):
            row = table[0, q * SLOTS + slot]
            value = src[jnp.clip(row, 0, src.shape[0] - 1)].astype(f32)
            mix[at, pl.ds(slot, CELLS, stride=SLOTS), :] = jnp.where(row >= 0, value, 0.0)
        put(board, q, mix[at])

    def spread(ref, q, value):
        mix[0] = value
        for slot in range(SLOTS):
            ref[q * SLOTS + slot] = mix[0, pl.ds(slot, CELLS, stride=SLOTS), :].astype(bf16)

    def keep_grad(j, q, grad, patches):
        turned = jnp.dot(grad.T.astype(bf16), patches, preferred_element_type=f32)
        bias = jnp.broadcast_to(jnp.sum(grad, axis=0, keepdims=True), (TAIL, channels))
        for ref in (even, odd):
            for tap in range(9):
                ref[j, q, tap * channels : (tap + 1) * channels, :] = turned[
                    :, tap * channels : (tap + 1) * channels
                ].astype(ref.dtype)
            ref[j, q, taps:, :] = bias.astype(ref.dtype)

    def phase_a(q):
        gather(acts, xb, q, 0)
        gather(cot, gb, q, 1)
        pre = jnp.dot(patch(xb, q), w1[q], preferred_element_type=f32) + bs[q, 0:1]
        gate = 0.5 * jnp.tanh(0.5 * pre) + 0.5
        slope[q] = gate * (1.0 + pre * (1.0 - gate))
        put(hb, q, pre * gate)
        keep_grad(1, q, centre(gb, q), patch(hb, q))

    def phase_b(q):
        pre_grad = wide(patch(gb, q), flipped_wide(w2, q)) * slope[q]
        put(pb, q, pre_grad)
        keep_grad(0, q, pre_grad.astype(bf16).astype(f32), patch(xb, q))

    def phase_c(q):
        spread(
            res_out, q,
            jnp.dot(patch(hb, q), w2[q], preferred_element_type=f32) + bs[q, 1:2] + centre(xb, q),
        )

    def phase_d(q):
        spread(res_back, q, wide(patch(pb, q), flipped_wide(w1, q)) + centre(gb, q))

    before = {name: [] for name in ORDER}

    def on(name, action, *args):
        before[name].append(functools.partial(action, *args))

    send_bias(0, 1, 2)
    on("A1", have_weights, 0, (0,))
    on("A1", have_bias, 0)
    on("B1", have_weights, 1, (0,))
    on("B1", have_weights, 0, (1, 3))
    on("B1", send_weights, 0, (5, 6))
    on("B1", have_weights, 0, (2, 4))
    on("B1", send_weights, 0, (7, 8))
    on("B1", have_bias, 1, 2)
    on("B1", send_bias, 3, 4, 5)
    on("B1", send_weights, 1, (1, 3, 2, 4))
    on("A6", have_weights, 0, (5, 6))
    on("A6", send_weights, 0, (9,))
    on("A6", have_bias, 5)
    on("A6", send_bias, 6)
    on("A7", have_weights, 0, (9,))
    on("A7", have_bias, 6)
    on("A3", have_weights, 0, (7,))
    on("A3", have_bias, 3)
    on("A5", have_weights, 0, (8,))
    on("A5", have_bias, 4)
    on("A4", have_weights, 1, (1, 3))
    on("A4", send_weights, 1, (5, 6))
    on("A4", have_weights, 1, (2, 4))
    on("A4", send_weights, 1, (7, 8))
    on("B3", have_weights, 1, (7,))
    on("B6", have_weights, 1, (5, 6))
    on("B6", send_weights, 1, (9,))
    on("B7", have_weights, 1, (9,))
    on("B5", have_weights, 1, (8,))

    for j, phase in ((1, "A"), (0, "B")):
        for p in range(4):
            on(ORDER[AT[phase + str(2 * p + 1)] + 1], send_pair, j, p)

    on("A3", send_diag, 1)
    on("B2", send_free, 1, 1)
    on("B3", send_free, 1, 2)
    on("B6", send_rest, 1, 1)
    on("B6", send_rest, 1, 2)
    on("B4", send_free, 0, 1)
    on("B5", send_diag, 0)
    on("D2", send_free, 0, 2)
    on("C2", have_own, 1)
    on("D2", add_up, 1, 0, 4, 1, 5)
    on("C3", add_up, 1, 2, 6, 3, 7)
    on("C5", middle, 1, 0, 4)
    on("C4", send_rest, 0, 1)
    on("C4", send_rest, 0, 2)
    on("D6", middle, 1, 1, 5)
    on("C7", have_own, 0)
    on("C7", add_up, 0, 0, 4, 1, 5)
    on("D7", add_up, 0, 2, 6, 3, 7)
    on("D7", middle, 1, 2, 6)
    on("D7", ending, 1, 0, 4)

    phases = {"A": phase_a, "B": phase_b, "C": phase_c, "D": phase_d}

    def step(at, carry):
        q = jnp.int32(0)
        kind = jnp.int32(0)
        for index, name in enumerate(ORDER):
            q = jnp.where(at == index, int(name[1]), q)
            kind = jnp.where(at == index, "ABCD".index(name[0]), kind)
            if before[name]:

                @pl.when(at == index)
                def _(name=name):
                    for action in before[name]:
                        action()

        for index, name in enumerate("ABCD"):

            @pl.when(kind == index)
            def _(name=name):
                phases[name](q)

        return carry

    lax.fori_loop(0, len(ORDER), step, 0)


    middle(1, 3, 7)
    ending(1, 1, 5)

    def together(state, carry):
        for at, (src, dst) in enumerate(((res_out, out_ref), (res_back, back_ref))):
            for side in range(2):
                row = jnp.clip(table[0, 8 * SLOTS + side * out_ref.shape[0] + state], 0, src.shape[0] - 1)
                pair[at, pl.ds(side, CELLS, stride=2), :] = src[row].astype(f32)
            dst[state] = pair[at].astype(bf16)
        return carry

    lax.fori_loop(0, out_ref.shape[0], together, 0)
    stores = [
        pltpu.make_async_copy(src, dst, load_sems.at[at])
        for at, (src, dst) in enumerate(((out_ref, out_hbm), (back_ref, back_hbm)))
    ]
    for store in stores:
        store.start()
    middle(0, 0, 4)
    ending(1, 2, 6)
    middle(0, 1, 5)
    ending(1, 3, 7)
    ending(0, 0)
    middle(0, 2)
    ending(0, 4)
    middle(0, 6)
    ending(0, 1)
    middle(0, 3)
    ending(0, 5)
    middle(0, 7)
    ending(0, 2, 6, 3, 7)
    settle()
    for store in stores:
        store.wait()

    for at in range(10):
        give(0, at).wait_send()
        give(1, at).wait_send()
    for at in range(7):
        give_bias(at).wait_send()
    for j in range(2):
        for at in range(6 + 2 * CHUNKS):
            grad_copy(j, at).wait_send()


def last_kernel(
    out_in, back_in, whole_in, out_ref, back_ref, grad_one, grad_two, bias_one, bias_two, boards, whole, grads, sems
):
    channels = whole.shape[-1]
    taps = grads.shape[1]

    def move(src, dst, at):
        return pltpu.make_async_copy(src, dst, sems.at[at])

    loads = [move(whole_in, whole, 0), move(out_in, boards.at[0], 1), move(back_in, boards.at[1], 2)]
    stores = [
        move(boards.at[0], out_ref, 3), move(boards.at[1], back_ref, 4),
        move(grads.at[0], grad_one.at[0], 5), move(grads.at[1], grad_two.at[0], 6),
    ]
    for load in loads:
        load.start()
    loads[0].wait()
    for j, bias in enumerate((bias_one, bias_two)):
        stacked = whole[j].astype(jnp.float32)
        for tap in range(9):
            rows = slice(tap * channels, (tap + 1) * channels)
            grads[j, rows, :] = stacked[rows].T
        stores[2 + j].start()
        loads[1 + j].wait()
        stores[j].start()
        bias[...] = whole[j, taps : taps + 8].astype(jnp.float32)[:1]
    for store in stores:
        store.wait()


def at_home(acts, cotangent, routes, w_first, w_second, b_first, b_second):
    owners = lax.axis_size("member")
    channels = acts.shape[-1]
    taps = 9 * channels
    rows_g = taps + TAIL
    f32, bf16 = jnp.float32, jnp.bfloat16
    count = 2 * routes.shape[0]

    def paired(values):
        return jnp.swapaxes(values, 1, 2).reshape(values.shape[0], 2 * values.shape[2], channels)

    x, g = paired(acts), paired(cotangent)
    anywhere = pl.BlockSpec(memory_space=pl.ANY)
    vmem = pl.BlockSpec(memory_space=pltpu.VMEM)
    shape = jax.ShapeDtypeStruct
    board = pltpu.VMEM((owners, PLACES, channels), bf16)
    weight = pltpu.VMEM((owners, taps, channels), bf16)
    results = pltpu.VMEM((owners * SLOTS, CELLS, channels), bf16)
    sems = pltpu.SemaphoreType.DMA
    made = pl.pallas_call(
        league_kernel,
        out_shape=(
            shape(x.shape, bf16),
            shape(x.shape, bf16),
            shape((2, rows_g, channels), bf16),
        ),
        in_specs=[vmem] + [anywhere] * 6,
        out_specs=(anywhere, anywhere, vmem),
        scratch_shapes=[
            pltpu.VMEM(x.shape, bf16),
            pltpu.VMEM(x.shape, bf16),
            pltpu.VMEM((2, 2 * CELLS, channels), f32),
            pltpu.VMEM((count, CELLS, channels), bf16),
            pltpu.VMEM((count, CELLS, channels), bf16),
            weight,
            weight,
            pltpu.VMEM((owners, 8, channels), f32),
            board,
            board,
            board,
            board,
            pltpu.VMEM((owners, ROWS, channels), f32),
            pltpu.VMEM((2, ROWS, channels), f32),
            results,
            results,
            pltpu.VMEM((2, owners, rows_g, channels), f32),
            pltpu.VMEM((2, owners, rows_g, channels), bf16),
            pltpu.VMEM((2, 4, rows_g, channels), bf16),
            pltpu.VMEM((2, 4, rows_g, channels), bf16),
            pltpu.VMEM((2, 2, taps // 2 + TAIL, channels), bf16),
            pltpu.VMEM((2, 2, rows_g, channels), bf16),
            pltpu.VMEM((2, rows_g, channels), f32),
            pltpu.VMEM((2, rows_g, channels), bf16),
            pltpu.VMEM((2, rows_g, channels), bf16),
            pltpu.VMEM((2, rows_g, channels), bf16),
            pltpu.VMEM((1, 128), jnp.int32),
            pltpu.SMEM((1, 128), jnp.int32),
            sems((7,)),
            sems((40,)),
            sems((40,)),
            sems((48,)),
            sems((48,)),
            sems((48,)),
            sems((48,)),
        ],
        compiler_params=pltpu.CompilerParams(
            collective_id=0, has_side_effects=True, vmem_limit_bytes=60 * 1024 * 1024
        ),
        cost_estimate=pl.CostEstimate(
            flops=12 * owners * ROWS * taps * channels, bytes_accessed=9000000, transcendentals=owners * ROWS * channels
        ),
        name="league",
    )(routes.T, x, g, w_first, w_second, b_first, b_second)
    done = pl.pallas_call(
        last_kernel,
        out_shape=(
            shape(x.shape, bf16),
            shape(x.shape, bf16),
            shape((1, taps, channels), f32),
            shape((1, taps, channels), f32),
            shape((1, channels), f32),
            shape((1, channels), f32),
        ),
        in_specs=[anywhere] * 3,
        out_specs=(anywhere,) * 4 + (vmem,) * 2,
        scratch_shapes=[
            pltpu.VMEM((2,) + x.shape, bf16),
            pltpu.VMEM((2, rows_g, channels), bf16),
            pltpu.VMEM((2, taps, channels), f32),
            sems((7,)),
        ],
        compiler_params=pltpu.CompilerParams(vmem_limit_bytes=60 * 1024 * 1024),
        cost_estimate=pl.CostEstimate(flops=0, bytes_accessed=5000000, transcendentals=0),
        name="last",
    )(*made)

    def unpaired(values):
        return jnp.swapaxes(values.reshape(acts.shape[0], acts.shape[2], 2, channels), 1, 2)

    return (unpaired(done[0]), unpaired(done[1])) + tuple(done[2:])


def solution(mesh):
    placed = (
        P(("rep", "member"), None, None, None),
        P(("rep", "member"), None, None, None),
        P(("rep", "member"), None),
        P("member", None, None),
        P("member", None, None),
        P("member", None),
        P("member", None),
    )
    return jax.shard_map(
        at_home if mesh.shape["member"] == 8 and mesh.shape["rep"] == 4 else shards,
        mesh=mesh,
        in_specs=placed,
        out_specs=(
            P(("rep", "member"), None, None, None),
            P(("rep", "member"), None, None, None),
            P("member", None, None),
            P("member", None, None),
            P("member", None),
            P("member", None),
        ),
        check_vma=False,
    )
```
